512 devices in a mesh: dp: 32 (over x, z_hi, core), expert: 16 (over y, z_lo).
Axes of the slice: x: 4, y: 8, z: 8 (z_hi: 4, z_lo: 2; z = z_hi * 2 + z_lo), core: 2. Of those that a mesh axis runs over, the one named last changes fastest.
Arguments:
- tokens: bfloat16 [65536, 3584], P(('dp', 'expert')), may hold values from -6 to 6
- grad_out: bfloat16 [65536, 3584], P(('dp', 'expert')), may hold values from -24 to 24
- routing: int32 [65536, 1], P(('dp', 'expert')), may hold values from 0 to 31; in each aligned block of 128 rows (0 to 127, 128 to 255, ...) at most 6 rows name the same one
- route_weight: float32 [65536, 1], P(('dp', 'expert')), may hold values from 0.1 to 1
- gate_weight: bfloat16 [3584, 8192], P('dp', 'expert'), may hold values from -0.09375 to 0.09375
- up_weight: bfloat16 [3584, 8192], P('dp', 'expert'), may hold values from -0.09375 to 0.09375
- down_weight: bfloat16 [3584, 8192], P('dp', 'expert'), may hold values from -0.1875 to 0.1875
Outputs:
- token_grad: bfloat16 [65536, 3584], P(('dp', 'expert'))
- route_grad: float32 [65536, 1], P(('dp', 'expert'))
- down_grad: bfloat16 [3584, 8192], P('dp', 'expert')
The draws below stay inside these ranges and needn't reach their ends.
Inputs may be any that keep to these rules, and one draw needn't show every extreme that they name: `routing`: ids under 8 name this group's experts, the others experts elsewhere. In the tokens of one device no id appears more than 6 times, and some id appears exactly 6 times.
All inputs are finite; a program needn't handle non-finite values.
Results may differ from the reference program's by a relative error of at most 0.024.
Values may be sent and summed in bfloat16 or wider, within the bound.
No kernel may reach another device: no remote copies, remote signals or barrier semaphores. Data moves between devices by JAX's collectives and lax.ppermute only.
A program may use at most 64 MiB of HBM per device.

```python
import math
import jax
import jax.numpy as jnp
import numpy as np
from jax import lax

D = 3584
HID = 1024
HALF = 512
TOK_DEV = 128
EXPERTS = 8
ROUTES = 32
CAP = 6
TOKENS = 65536
N_DP = 32
N_EXPERT = 16


def spiked(entries, key, source, target, parts, factor):
    def block_of(axis_at):
        return (jnp.arange(entries.shape[axis_at]) // (entries.shape[axis_at] // parts)).reshape((-1,) + (1,) * (entries.ndim - 1 - axis_at))

    first = jax.random.permutation(key, parts)[block_of(target)]
    far = (block_of(target) + parts // 2) % parts
    return jnp.where((block_of(source) == first) | (block_of(source) == far), factor * entries, entries)


def level_of(stream_key, extent, split, least, top_value):
    def one(position, parts):
        steps = jax.random.uniform(jax.random.fold_in(jax.random.fold_in(stream_key, 6), position), (parts,), jnp.float32, least / len(split), top_value / len(split))
        return jnp.repeat(jnp.exp(steps), extent[position] // parts).reshape((-1,) + (1,) * (len(extent) - position - 1))

    level = one(*split[0])
    for cut in split[1:]:
        level = level * one(*cut)
    return level


def assign_block(own_key, own, number, rows, count, top, reach, slope):
    order = jax.random.permutation(own_key, count)
    heavy_load, ordinary = shares(count, rows * top, reach, slope, True), shares(count, rows * top, reach, slope, False)
    places = jnp.arange(count)

    def named(lengths, offset_by):
        used = int((lengths > 0).sum())
        fixed = max(1, used // 4)
        shifted = fixed + (places - fixed + offset_by * (used - fixed)) % max(1, count - fixed)
        return jnp.zeros((count,), jnp.int32).at[order[jnp.where(places < fixed, places, shifted)]].set(jnp.asarray(lengths, jnp.int32))

    lengths = jnp.where(number % 4 == 0, named(heavy_load, number // 4), named(ordinary, number - number // 4 - 1))
    mixed = jax.random.permutation(jax.random.fold_in(own, 3), count)
    source_of, taker = mixed[0:count // 2 * 2:2], mixed[1:count // 2 * 2:2]
    room = jnp.minimum(lengths[source_of] - 1, reach - lengths[taker]) // 2
    room = jnp.where((source_of == order[0]) | (taker == order[0]) | (lengths[taker] == 0), 0, jnp.maximum(room, 0))
    shifted = jax.random.randint(jax.random.fold_in(own, 4), (count // 2,), 0, 1 << 20) % (room + 1)
    lengths = lengths.at[source_of].add(-shifted).at[taker].add(shifted)
    labels = jnp.searchsorted(jnp.cumsum(lengths), jnp.arange(rows * top), side="right").astype(jnp.int32)
    listing = labels.reshape(top, rows).T
    listing = listing[jax.random.permutation(jax.random.fold_in(own, 1), rows)]
    offset_by = jax.random.randint(jax.random.fold_in(own, 2), (rows, 1), 0, top)
    return jnp.take_along_axis(listing, (jnp.arange(top)[None, :] + offset_by) % top, axis=1)


def shares(count, total, bound, lean, full):
    loads = [(1 << 20) // math.isqrt(grade ** lean) + 1 for grade in range(1, count + 1)]
    largest = bound if full else min(bound, max(-(-total // count), total * loads[0] // sum(loads)))
    least = 1 if total - largest >= count - 1 else 0
    counts, surplus = [largest] + [least] * (count - 1), total - largest - least * (count - 1)
    while surplus > 0:
        free = [i for i in range(1, count) if counts[i] < largest] or [i for i in range(1, count) if counts[i] < bound]
        pool, budget = sum([loads[i] for i in free]), surplus
        for i in free:
            addition = min(bound - counts[i], max(1, budget * loads[i] // pool), surplus)
            counts[i] = counts[i] + addition
            surplus = surplus - addition
    return np.array(counts)


def noise(stream_key, shape, width, reach, pieces=(), held_as=jnp.bfloat16):
    loudness = level_of(stream_key, shape, pieces, -0.22, 0.18) if pieces else 1.0
    drawn = jax.random.normal(stream_key, shape, jnp.float32) * width * loudness
    return jnp.minimum(jnp.maximum(drawn, -reach), reach).astype(held_as)


def bell_draw_with(rng, shape, scale, bound, pieces, heavy, kind=jnp.bfloat16):
    result = scale * jax.random.normal(rng, shape, jnp.float32)
    if pieces:
        result = result * level_of(rng, shape, pieces, -0.22, 0.18)
    return jnp.clip(spiked(result, jax.random.fold_in(rng, 3), *heavy), -bound, bound).astype(kind)


def setup_inputs(seed: int = 0) -> dict:
    arg_keys = jax.random.split(jax.random.key(seed), 8)
    tokens = noise(arg_keys[0], (TOKENS, D), 1.0, 6.0, ((0, 512),))
    grad_out = bell_draw_with(arg_keys[1], (TOKENS, D), 1.0, 24.0, ((0, 512),), (0, 1, 512, 6.0))
    routing_keys = jax.random.split(jax.random.fold_in(arg_keys[2], 1), TOKENS // TOK_DEV)
    routing_turns = jax.random.permutation(jax.random.fold_in(arg_keys[2], 3), TOKENS // TOK_DEV)
    routing = jax.vmap(lambda own, number: assign_block(jax.random.fold_in(arg_keys[2], 2), own, number, TOK_DEV, ROUTES, 1, CAP, 2))(routing_keys, routing_turns).reshape((TOKENS, 1))
    route_weight = jnp.clip(jnp.exp(math.log(1.0) - 2.3025851 * jax.random.uniform(arg_keys[3], (TOKENS, 1), jnp.float32) ** level_of(arg_keys[3], (TOKENS, 1), ((0, 512),), -0.2, 0.2)), 0.1, 1.0)
    gate_weight = noise(arg_keys[4], (D, EXPERTS * HID), D ** -0.5, 0.09375, ((0, 32), (1, 16)))
    up_weight = noise(arg_keys[5], (D, EXPERTS * HID), D ** -0.5, 0.09375, ((0, 32), (1, 16)))
    down_weight = noise(arg_keys[6], (D, EXPERTS * HID), HID ** -0.5, 0.1875, ((0, 32), (1, 16)))
    return {"tokens": tokens, "grad_out": grad_out, "routing": routing, "route_weight": route_weight, "gate_weight": gate_weight, "up_weight": up_weight, "down_weight": down_weight}


def silu_parts(pre_gate):
    sigmoid_val = jax.nn.sigmoid(pre_gate)
    return pre_gate * sigmoid_val, sigmoid_val * (1.0 + pre_gate * (1.0 - sigmoid_val))


def build_table(chosen_ids, expert_index):
    blocks = chosen_ids.reshape(N_DP * N_EXPERT, TOK_DEV)
    member = (blocks == expert_index).astype(jnp.int32)
    ranking = (jnp.cumsum(member, axis=1) - 1).astype(jnp.int32)
    block_ids = jnp.arange(N_DP * N_EXPERT, dtype=jnp.int32)[:, None]
    target = jnp.where(member > 0, block_ids * CAP + ranking, N_DP * N_EXPERT * CAP).astype(jnp.int32)
    sources = jnp.arange(TOKENS, dtype=jnp.int32)
    slot_table = jnp.full((N_DP * N_EXPERT * CAP,), TOKENS, jnp.int32)
    return slot_table.at[target.reshape(-1)].set(sources, mode="drop")


def reference(tokens, grad_out, routing, route_weight, gate_weight, up_weight, down_weight):
    chosen_ids = routing[:, 0]
    tables = []
    grads = []
    routes = []
    columns_out = []
    for expert_index in range(EXPERTS):
        slot_table = build_table(chosen_ids, expert_index)
        x_rows = jnp.take(tokens, slot_table, axis=0, mode="fill", fill_value=0)
        g_rows = jnp.take(grad_out, slot_table, axis=0, mode="fill", fill_value=0)
        p_rows = jnp.take(route_weight[:, 0], slot_table, axis=0, mode="fill", fill_value=0.0)[:, None]
        scaled = (p_rows * g_rows.astype(jnp.float32)).astype(jnp.bfloat16)
        grad_sum = jnp.zeros((x_rows.shape[0], D), jnp.float32)
        route_sum = jnp.zeros((x_rows.shape[0],), jnp.float32)
        for half_index in range(2):
            begin = (2 * expert_index + half_index) * HALF
            gate_cols = gate_weight[:, begin:begin + HALF]
            up_cols = up_weight[:, begin:begin + HALF]
            down_cols = down_weight[:, begin:begin + HALF]
            pre_gate = jnp.dot(x_rows, gate_cols, preferred_element_type=jnp.float32)
            pre_up = jnp.dot(x_rows, up_cols, preferred_element_type=jnp.float32)
            activated, derivative = silu_parts(pre_gate)
            hidden = (activated * pre_up).astype(jnp.bfloat16)
            hidden_grad = jnp.dot(g_rows, down_cols, preferred_element_type=jnp.float32)
            route_sum = route_sum + jnp.sum(hidden.astype(jnp.float32) * hidden_grad, axis=1)
            scaled_grad = p_rows * hidden_grad
            d_gate_pre = (scaled_grad * pre_up * derivative).astype(jnp.bfloat16)
            d_up_pre = (scaled_grad * activated).astype(jnp.bfloat16)
            part_tokens = jnp.dot(d_gate_pre, gate_cols.T, preferred_element_type=jnp.float32)
            part_tokens = part_tokens + jnp.dot(d_up_pre, up_cols.T, preferred_element_type=jnp.float32)
            grad_sum = grad_sum + part_tokens.astype(jnp.bfloat16).astype(jnp.float32)
            hidden_groups = hidden.astype(jnp.float32).reshape(N_DP, N_EXPERT * CAP, HALF)
            scaled_groups = scaled.astype(jnp.float32).reshape(N_DP, N_EXPERT * CAP, D)
            group_down = jnp.einsum("grd,grh->gdh", scaled_groups, hidden_groups).astype(jnp.bfloat16)
            group_down = lax.optimization_barrier(group_down)
            columns_out.append(jnp.sum(group_down.astype(jnp.float32), axis=0).astype(jnp.bfloat16))
        tables.append(slot_table)
        grads.append(grad_sum.astype(jnp.bfloat16))
        routes.append(route_sum)
    all_tables = jnp.concatenate(tables)
    token_grad = jnp.zeros((TOKENS, D), jnp.bfloat16).at[all_tables].set(jnp.concatenate(grads), mode="drop")
    route_grad = jnp.zeros((TOKENS,), jnp.float32).at[all_tables].set(jnp.concatenate(routes), mode="drop")
    down_grad = jnp.concatenate(columns_out, axis=1)
    return token_grad, route_grad[:, None], down_grad
```

```python
import jax
import jax.numpy as jnp
from jax import lax
from jax.experimental import pallas as pl
from jax.experimental.pallas import tpu as pltpu
from jax.sharding import Mesh, PartitionSpec as P

BF = jnp.bfloat16
F32 = jnp.float32
AXES = ("x", "zh", "c", "y", "zl")
TOK = 128
D = 3584
EXPERTS = 8
HALF = 512
QUART = 256
SHARD = 112
BLOCK = 2 * SHARD
XROWS = 4 * BLOCK
SLOTS = 16
ROWS = EXPERTS * SLOTS
BACK = EXPERTS * 8


def expert_rank(ids):
    lanes = lax.broadcasted_iota(jnp.int32, (TOK, TOK), 1)
    subs = lax.broadcasted_iota(jnp.int32, (TOK, TOK), 0)
    member = jnp.where((ids == lanes) & (lanes < EXPERTS), 1.0, 0.0)
    earlier = jnp.where(lanes < subs, 1.0, 0.0)
    counts = jnp.dot(earlier.astype(BF), member.astype(BF), preferred_element_type=F32)
    rank = jnp.sum(member * counts, axis=1, keepdims=True).astype(jnp.int32)
    return rank, lanes


def dispatch_kernel(ids_ref, p_ref, x_ref, g_ref, out_ref):
    ids = ids_ref[...]
    rank, lanes = expert_rank(ids)
    slot = jnp.where(ids < EXPERTS, ids * SLOTS + rank, -SLOTS)
    sel_x = jnp.where(slot == lanes, 1.0, 0.0).astype(BF)
    sel_g = jnp.where(slot + 8 == lanes, 1.0, 0.0).astype(BF)
    scaled = (p_ref[...] * g_ref[...].astype(F32)).astype(BF)
    first = (((0,), (0,)), ((), ()))
    rows = lax.dot_general(sel_x, x_ref[...], first, preferred_element_type=F32)
    rows = rows + lax.dot_general(sel_g, scaled, first, preferred_element_type=F32)
    out_ref[...] = rows.astype(BF)


def dispatch(ids, weight, tokens, grads):
    chunk = D // 4
    whole = pl.BlockSpec((TOK, 1), lambda i: (0, 0))
    part = pl.BlockSpec((TOK, chunk), lambda i: (0, i))
    return pl.pallas_call(
        dispatch_kernel,
        grid=(4,),
        in_specs=[whole, whole, part, part],
        out_specs=pl.BlockSpec((ROWS, chunk), lambda i: (0, i)),
        out_shape=jax.ShapeDtypeStruct((ROWS, D), BF),
        cost_estimate=pl.CostEstimate(flops=4 * TOK * ROWS * D, bytes_accessed=6 * TOK * D, transcendentals=0),
        name="dispatch",
    )(ids, weight, tokens, grads)


def finish_kernel(ids_ref, p_ref, rows_ref, head_ref, tok_ref, route_ref):
    ids = ids_ref[...]
    rank, lanes = expert_rank(ids)
    valid = ids < EXPERTS
    slot = jnp.where(valid, ids * 8 + rank, -8)
    cols = lax.broadcasted_iota(jnp.int32, (TOK, BACK), 1)
    sel = jnp.where(slot == cols, 1.0, 0.0).astype(BF)
    tok_ref[...] = jnp.dot(sel, rows_ref[...], preferred_element_type=F32).astype(BF)

    @pl.when(pl.program_id(0) == 0)
    def _():
        pick = jnp.where(jnp.where(valid, ids * 8 + 6, -8) == cols, 1.0, 0.0).astype(BF)
        values = jnp.dot(pick, head_ref[...], preferred_element_type=F32)
        total = jnp.sum(jnp.where(lanes == rank, values, 0.0), axis=1, keepdims=True)
        route_ref[...] = total / p_ref[...]


def finish(ids, weight, rows):
    chunk = D // 4
    whole = pl.BlockSpec((TOK, 1), lambda i: (0, 0))
    return pl.pallas_call(
        finish_kernel,
        grid=(4,),
        in_specs=[
            whole,
            whole,
            pl.BlockSpec((BACK, chunk), lambda i: (0, i)),
            pl.BlockSpec((BACK, TOK), lambda i: (0, 0)),
        ],
        out_specs=[pl.BlockSpec((TOK, chunk), lambda i: (0, i)), whole],
        out_shape=[jax.ShapeDtypeStruct((TOK, D), BF), jax.ShapeDtypeStruct((TOK, 1), F32)],
        cost_estimate=pl.CostEstimate(flops=2 * TOK * BACK * D, bytes_accessed=4 * TOK * D, transcendentals=0),
        name="finish",
    )(ids, weight, rows, rows)


def expert_kernel(pieces, *refs):
    row_refs = refs[:4]
    weight_refs = refs[4:4 + len(pieces)]
    keep_ref, send_ref, far_ref, plus_ref, minus_ref, own_ref = refs[4 + len(pieces):10 + len(pieces)]
    rows, weights, sem_rows, sem_weights = refs[10 + len(pieces):]
    xi, zi, ci = lax.axis_index("x"), lax.axis_index("zh"), lax.axis_index("c")
    copies = []
    for i, ref in enumerate(row_refs):
        copies.append(pltpu.make_async_copy(ref, rows.at[pl.ds(i * ROWS, ROWS)], sem_rows.at[i]))
    count = 0
    for ref, listed in zip(weight_refs, pieces):
        for at, (dx, dz, which) in enumerate(listed):
            block = lax.rem(xi + dx, 4) * 4 + lax.rem(zi + dz, 4)
            core = ci if which == 0 else 1 - ci
            start = pl.multiple_of(block * BLOCK + core * SHARD, 16)
            copies.append(pltpu.make_async_copy(
                ref.at[pl.ds(at * SHARD, SHARD)], weights.at[pl.ds(start, SHARD)], sem_weights.at[count]
            ))
            count += 1
    for copy in copies:
        copy.start()
    for copy in copies:
        copy.wait()
    pre = jnp.dot(rows[...], weights[...], preferred_element_type=F32)
    pre = pre.reshape(4 * EXPERTS, SLOTS, 3 * QUART)
    tall = 4 * BACK
    gate = pre[:, :8, :QUART].reshape(tall, QUART)
    up = pre[:, :8, QUART:2 * QUART].reshape(tall, QUART)
    grad = pre[:, 8:, 2 * QUART:].reshape(tall, QUART)
    sig = jax.nn.sigmoid(gate)
    act = gate * sig
    slope = sig * (1.0 + gate * (1.0 - sig))
    hidden = (act * up).astype(BF).astype(F32)
    route = jnp.sum(hidden * grad, axis=1, keepdims=True).reshape(4 * EXPERTS, 8, 1)
    spread = jnp.concatenate([jnp.zeros((4 * EXPERTS, 8, QUART), F32), hidden.reshape(4 * EXPERTS, 8, QUART)], axis=1)
    spread = spread.reshape(4 * ROWS, QUART).astype(BF)
    for ref, shift in ((far_ref, 2), (plus_ref, 1), (minus_ref, 3), (own_ref, 0)):
        start = pl.multiple_of(lax.rem(xi + shift, 4) * XROWS, 128)
        ref[...] = lax.dot_general(
            rows[:, pl.ds(start, XROWS)], spread, (((0,), (0,)), ((), ())), preferred_element_type=F32
        ).astype(BF)
    d_pre = jnp.concatenate([(grad * up * slope).astype(BF), (grad * act).astype(BF)], axis=1)
    lanes = lax.broadcasted_iota(jnp.int32, (4 * EXPERTS, 8, 128), 2)
    subs = lax.broadcasted_iota(jnp.int32, (4 * EXPERTS, 8, 128), 1)
    line = jnp.sum(jnp.where(lanes == subs, route, 0.0), axis=1, keepdims=True)
    extra = jnp.where(subs == 6, line, 0.0).reshape(tall, 128)
    chunk = D // 4
    for i in range(4):
        part = lax.dot_general(
            d_pre, weights[i * chunk:(i + 1) * chunk, :2 * QUART], (((1,), (1,)), ((), ())),
            preferred_element_type=F32,
        )
        if i == 0:
            part = jnp.concatenate([part[:, :128] + extra, part[:, 128:]], axis=1)
        part = part.astype(BF)
        keep_ref[:, i * chunk:(i + 1) * chunk] = part[:2 * BACK]
        send_ref[:, i * chunk:(i + 1) * chunk] = part[2 * BACK:]


def expert_compute(rows, blocks, pieces):
    anywhere = pl.BlockSpec(memory_space=pl.ANY)
    vmem = pl.BlockSpec(memory_space=pltpu.VMEM)
    count = sum(len(p) for p in pieces)
    big = jax.ShapeDtypeStruct((2 * BACK, D), BF)
    down = jax.ShapeDtypeStruct((XROWS, QUART), BF)
    return pl.pallas_call(
        lambda *refs: expert_kernel(pieces, *refs),
        in_specs=[anywhere] * (4 + len(blocks)),
        out_specs=[vmem] * 6,
        out_shape=[big, big, down, down, down, down],
        scratch_shapes=[
            pltpu.VMEM((4 * ROWS, D), BF),
            pltpu.VMEM((D, 3 * QUART), BF),
            pltpu.SemaphoreType.DMA((4,)),
            pltpu.SemaphoreType.DMA((count,)),
        ],
        compiler_params=pltpu.CompilerParams(vmem_limit_bytes=48 * 1024 * 1024),
        cost_estimate=pl.CostEstimate(flops=6 * 10**9, bytes_accessed=14 * 10**6, transcendentals=65536),
        name="experts",
    )(*rows, *blocks)


def hop(a, axis, shift):
    n = lax.axis_size(axis)
    return lax.ppermute(a, axis, [(i, (i + shift) % n) for i in range(n)])


def both_ways(a, axis):
    return hop(a, axis, 1), hop(a, axis, -1)


def ring_gather(a, axis):
    n = a.shape[0] // 2
    before, after = both_ways(a, axis)
    return before, after, hop(before[:n], axis, 1), hop(after[n:], axis, -1)


def ring_scatter(far, plus, minus, own, axis):
    n = far.shape[0] // 2
    low = hop(far[:n], axis, 1)
    high = hop(far[n:], axis, -1)
    plus = jnp.concatenate([(plus[:n].astype(F32) + low.astype(F32)).astype(BF), plus[n:]], axis=0)
    minus = jnp.concatenate([minus[:n], (minus[n:].astype(F32) + high.astype(F32)).astype(BF)], axis=0)
    total = hop(plus, axis, 1).astype(F32) + hop(minus, axis, -1).astype(F32) + own.astype(F32)
    return total.astype(BF)


def per_device(tokens, grad_out, routing, route_weight, gate_weight, up_weight, down_weight):
    zi, ci = lax.axis_index("zh"), lax.axis_index("c")

    def columns(which):
        return jnp.concatenate([
            lax.dynamic_slice(w, (0, which * QUART), (SHARD, QUART)) for w in (gate_weight, up_weight, down_weight)
        ], axis=1)

    own = jnp.concatenate([columns(ci), hop(columns(1 - ci), "c", 1)], axis=0)

    sent = dispatch(routing, route_weight, tokens, grad_out).reshape(EXPERTS, SLOTS, D)
    rows_own = lax.all_to_all(sent, "y", split_axis=0, concat_axis=0, tiled=True).reshape(ROWS, D)
    rows_zl = hop(rows_own, "zl", 1)
    rows_c = hop(rows_own, "c", 1)
    rows_czl = hop(rows_zl, "c", 1)

    pair = lambda dx, dz: [(dx, dz, 0), (dx, dz, 1)]
    blocks, pieces = [], []

    def add_x(block, listed):
        before, after, low, high = ring_gather(block, "x")
        half = len(listed) // 2
        blocks.extend([block, before, after, low, high])
        pieces.append(listed)
        pieces.append([((dx + 3) % 4, dz, w) for dx, dz, w in listed])
        pieces.append([((dx + 1) % 4, dz, w) for dx, dz, w in listed])
        pieces.append([((dx + 2) % 4, dz, w) for dx, dz, w in listed[:half]])
        pieces.append([((dx + 2) % 4, dz, w) for dx, dz, w in listed[half:]])

    z_before, z_after, z_low, z_high = ring_gather(own, "zh")
    add_x(own, pair(0, 0))
    add_x(jnp.concatenate([z_before, z_after], axis=0), pair(0, 3) + pair(0, 1))
    add_x(jnp.concatenate([z_low, z_high], axis=0), pair(0, 2))

    keep, send, far, plus, minus, mine = expert_compute([rows_own, rows_zl, rows_c, rows_czl], blocks, pieces)

    got = hop(send, "c", 1)
    to_zl = (keep[BACK:].astype(F32) + got[BACK:].astype(F32)).astype(BF)
    from_zl = hop(to_zl, "zl", 1)
    back = (keep[:BACK].astype(F32) + got[:BACK].astype(F32) + from_zl.astype(F32)).astype(BF)
    back = lax.all_to_all(back.reshape(EXPERTS, 8, D), "y", split_axis=0, concat_axis=0, tiled=True)
    token_grad, route_grad = finish(routing, route_weight, back.reshape(BACK, D))

    summed = ring_scatter(far, plus, minus, mine, "x")
    quarter = lambda shift: lax.dynamic_slice(summed, (lax.rem(zi + shift, 4) * BLOCK, 0), (BLOCK, QUART))
    summed = ring_scatter(quarter(2), quarter(1), quarter(3), quarter(0), "zh")
    stay = lax.dynamic_slice(summed, (ci * SHARD, 0), (SHARD, QUART))
    cross = hop(lax.dynamic_slice(summed, ((1 - ci) * SHARD, 0), (SHARD, QUART)), "c", 1)
    down_grad = jnp.where(ci == 0, jnp.concatenate([stay, cross], axis=1), jnp.concatenate([cross, stay], axis=1))
    return token_grad, route_grad, down_grad


def solution(mesh):
    inner = Mesh(mesh.devices.reshape(4, 4, 2, 8, 2), AXES)
    rows = P(AXES, None)
    weights = P(("x", "zh", "c"), ("y", "zl"))
    return jax.shard_map(
        per_device,
        mesh=inner,
        in_specs=(rows, rows, rows, rows, weights, weights, weights),
        out_specs=(rows, rows, weights),
        check_vma=False,
    )
```

```python
import jax
import jax.numpy as jnp
from jax import lax
from jax.experimental import pallas as pl
from jax.experimental.pallas import tpu as pltpu
from jax.sharding import Mesh, PartitionSpec as P

BF = jnp.bfloat16
F32 = jnp.float32
AXES = ("x", "zh", "c", "y", "zl")
TOK = 128
D = 3584
EXPERTS = 8
HALF = 512
QUART = 256
SHARD = 112
BLOCK = 2 * SHARD
XROWS = 4 * BLOCK
SLOTS = 16
ROWS = EXPERTS * SLOTS
BACK = EXPERTS * 8
VMEM_LIMIT = 28 * 1024 * 1024


def expert_rank(ids):
    lanes = lax.broadcasted_iota(jnp.int32, (TOK, TOK), 1)
    subs = lax.broadcasted_iota(jnp.int32, (TOK, TOK), 0)
    member = jnp.where((ids == lanes) & (lanes < EXPERTS), 1.0, 0.0)
    earlier = jnp.where(lanes < subs, 1.0, 0.0)
    counts = jnp.dot(earlier.astype(BF), member.astype(BF), preferred_element_type=F32)
    rank = jnp.sum(member * counts, axis=1, keepdims=True).astype(jnp.int32)
    return rank, lanes


def dispatch_kernel(ids_ref, p_ref, x_ref, g_ref, out_ref):
    ids = ids_ref[...]
    rank, lanes = expert_rank(ids)
    slot = jnp.where(ids < EXPERTS, ids * SLOTS + rank, -SLOTS)
    sel_x = jnp.where(slot == lanes, 1.0, 0.0).astype(BF)
    sel_g = jnp.where(slot + 8 == lanes, 1.0, 0.0).astype(BF)
    scaled = (p_ref[...] * g_ref[...].astype(F32)).astype(BF)
    first = (((0,), (0,)), ((), ()))
    rows = lax.dot_general(sel_x, x_ref[...], first, preferred_element_type=F32)
    rows = rows + lax.dot_general(sel_g, scaled, first, preferred_element_type=F32)
    out_ref[...] = rows.astype(BF)


def dispatch(ids, weight, tokens, grads):
    chunk = D // 4
    whole = pl.BlockSpec((TOK, 1), lambda i: (0, 0))
    part = pl.BlockSpec((TOK, chunk), lambda i: (0, i))
    return pl.pallas_call(
        dispatch_kernel,
        grid=(4,),
        in_specs=[whole, whole, part, part],
        out_specs=pl.BlockSpec((ROWS, chunk), lambda i: (0, i)),
        out_shape=jax.ShapeDtypeStruct((ROWS, D), BF),
        cost_estimate=pl.CostEstimate(flops=4 * TOK * ROWS * D, bytes_accessed=6 * TOK * D, transcendentals=0),
        name="dispatch",
    )(ids, weight, tokens, grads)


def finish_kernel(ids_ref, p_ref, rows_ref, head_ref, tok_ref, route_ref):
    ids = ids_ref[...]
    rank, lanes = expert_rank(ids)
    valid = ids < EXPERTS
    slot = jnp.where(valid, ids * 8 + rank, -8)
    cols = lax.broadcasted_iota(jnp.int32, (TOK, BACK), 1)
    sel = jnp.where(slot == cols, 1.0, 0.0).astype(BF)
    tok_ref[...] = jnp.dot(sel, rows_ref[...], preferred_element_type=F32).astype(BF)

    @pl.when(pl.program_id(0) == 0)
    def _():
        pick = jnp.where(jnp.where(valid, ids * 8 + 6, -8) == cols, 1.0, 0.0).astype(BF)
        values = jnp.dot(pick, head_ref[...], preferred_element_type=F32)
        total = jnp.sum(jnp.where(lanes == rank, values, 0.0), axis=1, keepdims=True)
        route_ref[...] = total / p_ref[...]


def finish(ids, weight, rows):
    chunk = D // 4
    whole = pl.BlockSpec((TOK, 1), lambda i: (0, 0))
    return pl.pallas_call(
        finish_kernel,
        grid=(4,),
        in_specs=[
            whole,
            whole,
            pl.BlockSpec((BACK, chunk), lambda i: (0, i)),
            pl.BlockSpec((BACK, TOK), lambda i: (0, 0)),
        ],
        out_specs=[pl.BlockSpec((TOK, chunk), lambda i: (0, i)), whole],
        out_shape=[jax.ShapeDtypeStruct((TOK, D), BF), jax.ShapeDtypeStruct((TOK, 1), F32)],
        cost_estimate=pl.CostEstimate(flops=10**7, bytes_accessed=10**4, transcendentals=0),
        name="finish",
    )(ids, weight, rows, rows)


def weight_copies(weight_refs, pieces, weights, sems, width):
    xi, zi, ci = lax.axis_index("x"), lax.axis_index("zh"), lax.axis_index("c")
    copies = []
    for ref, listed in zip(weight_refs, pieces):
        for at, (dx, dz, which) in enumerate(listed):
            x = lax.rem(xi + jnp.where(ci == 0, dx, 4 - dx), 4)
            z = lax.rem(zi + jnp.where(ci == 0, dz, 4 - dz), 4)
            core = ci if which == 0 else 1 - ci
            start = pl.multiple_of((x * 4 + z) * BLOCK + core * SHARD, 16)
            copies.append(pltpu.make_async_copy(
                ref.at[pl.ds(at * SHARD, SHARD), pl.ds(0, width)],
                weights.at[pl.ds(start, SHARD), pl.ds(0, width)],
                sems.at[len(copies)],
            ))
    return copies


def expert_kernel(pieces, *refs):
    row_refs = refs[:4]
    weight_refs = refs[4:4 + len(pieces)]
    keep_ref, send_ref, far_ref, plus_ref, minus_ref, own_ref = refs[4 + len(pieces):10 + len(pieces)]
    rows, weights, sem_rows, sem_weights = refs[10 + len(pieces):]
    xi, ci = lax.axis_index("x"), lax.axis_index("c")
    copies = [
        pltpu.make_async_copy(ref, rows.at[pl.ds(i * ROWS, ROWS)], sem_rows.at[i]) for i, ref in enumerate(row_refs)
    ]
    copies += weight_copies(weight_refs, pieces, weights, sem_weights, 3 * QUART)
    for copy in copies:
        copy.start()
    for copy in copies:
        copy.wait()
    pre = jnp.dot(rows[...], weights[...], preferred_element_type=F32)
    pre = pre.reshape(4 * EXPERTS, SLOTS, 3 * QUART)
    tall = 4 * BACK
    gate = pre[:, :8, :QUART].reshape(tall, QUART)
    up = pre[:, :8, QUART:2 * QUART].reshape(tall, QUART)
    grad = pre[:, 8:, 2 * QUART:].reshape(tall, QUART)
    sig = jax.nn.sigmoid(gate)
    act = gate * sig
    slope = sig * (1.0 + gate * (1.0 - sig))
    hidden = (act * up).astype(BF).astype(F32)
    route = jnp.sum(hidden * grad, axis=1, keepdims=True).reshape(4 * EXPERTS, 8, 1)
    spread = jnp.concatenate([jnp.zeros((4 * EXPERTS, 8, QUART), F32), hidden.reshape(4 * EXPERTS, 8, QUART)], axis=1)
    spread = spread.reshape(4 * ROWS, QUART).astype(BF)
    for ref, shift in ((far_ref, 2), (plus_ref, 1), (minus_ref, 3), (own_ref, 0)):
        around = jnp.where(ci == 0, shift, 4 - shift)
        start = pl.multiple_of(lax.rem(xi + around, 4) * XROWS, 128)
        ref[...] = lax.dot_general(
            rows[:, pl.ds(start, XROWS)], spread, (((0,), (0,)), ((), ())), preferred_element_type=F32
        ).astype(BF)
    d_pre = jnp.concatenate([(grad * up * slope).astype(BF), (grad * act).astype(BF)], axis=1)
    lanes = lax.broadcasted_iota(jnp.int32, (4 * EXPERTS, 8, 128), 2)
    subs = lax.broadcasted_iota(jnp.int32, (4 * EXPERTS, 8, 128), 1)
    line = jnp.sum(jnp.where(lanes == subs, route, 0.0), axis=1, keepdims=True)
    extra = jnp.where(subs == 6, line, 0.0).reshape(tall, 128)
    chunk = D // 4
    for i in range(4):
        part = lax.dot_general(
            d_pre, weights[i * chunk:(i + 1) * chunk, :2 * QUART], (((1,), (1,)), ((), ())),
            preferred_element_type=F32,
        )
        if i == 0:
            part = jnp.concatenate([part[:, :128] + extra, part[:, 128:]], axis=1)
        part = part.astype(BF)
        keep_ref[:, i * chunk:(i + 1) * chunk] = part[:2 * BACK]
        send_ref[:, i * chunk:(i + 1) * chunk] = part[2 * BACK:]


def expert_compute(rows, blocks, pieces):
    anywhere = pl.BlockSpec(memory_space=pl.ANY)
    vmem = pl.BlockSpec(memory_space=pltpu.VMEM)
    count = sum(len(p) for p in pieces)
    big = jax.ShapeDtypeStruct((2 * BACK, D), BF)
    down = jax.ShapeDtypeStruct((XROWS, QUART), BF)
    return pl.pallas_call(
        lambda *refs: expert_kernel(pieces, *refs),
        in_specs=[anywhere] * (4 + len(blocks)),
        out_specs=[vmem] * 6,
        out_shape=[big, big, down, down, down, down],
        scratch_shapes=[
            pltpu.VMEM((4 * ROWS, D), BF),
            pltpu.VMEM((D, 3 * QUART), BF),
            pltpu.SemaphoreType.DMA((4,)),
            pltpu.SemaphoreType.DMA((count,)),
        ],
        compiler_params=pltpu.CompilerParams(vmem_limit_bytes=VMEM_LIMIT),
        cost_estimate=pl.CostEstimate(flops=6 * 10**9, bytes_accessed=14 * 10**6, transcendentals=65536),
        name="experts",
    )(*rows, *blocks)


def hop(a, axis, shift):
    n = lax.axis_size(axis)
    return lax.ppermute(a, axis, [(i, (i + shift) % n) for i in range(n)])


def turn(a, axis, shift):
    n = lax.axis_size(axis)
    pairs = []
    for i in range(n):
        pairs.append((2 * i, 2 * ((i + shift) % n)))
        pairs.append((2 * i + 1, 2 * ((i - shift) % n) + 1))
    return lax.ppermute(a, (axis, "c"), pairs)


def ring_gather(a, axis):
    before, after = turn(a, axis, 1), turn(a, axis, -1)
    return before, after, turn(before, axis, 1)


def ring_scatter(far, plus, minus, own, axis):
    last = turn(minus, axis, -1)
    passed = turn(far, axis, 1)
    total = turn((plus.astype(F32) + passed.astype(F32)).astype(BF), axis, 1)
    return (total.astype(F32) + last.astype(F32) + own.astype(F32)).astype(BF)


def after(a, *others):
    return lax.optimization_barrier((a,) + others)[0]


def per_device(tokens, grad_out, routing, route_weight, gate_weight, up_weight, down_weight):
    zi, ci = lax.axis_index("zh"), lax.axis_index("c")

    def columns(which):
        return jnp.concatenate([
            lax.dynamic_slice(w, (0, which * QUART), (SHARD, QUART)) for w in (gate_weight, up_weight, down_weight)
        ], axis=1)

    sent = dispatch(routing, route_weight, tokens, grad_out)
    own = jnp.concatenate([columns(ci), hop(after(columns(1 - ci), sent), "c", 1)], axis=0)

    pair = lambda dx, dz: [(dx, dz, 0), (dx, dz, 1)]
    z_before, z_after = turn(own, "zh", 1), turn(own, "zh", -1)
    x_before, x_after = turn(own, "x", 1), turn(own, "x", -1)
    z_far = turn(after(z_before, x_before), "zh", 1)
    x_far = turn(x_before, "x", 1)
    rest = jnp.concatenate([z_before, z_after, z_far], axis=0)
    r_before, r_after, r_far = ring_gather(after(rest, x_far, x_after), "x")
    across = pair(0, 3) + pair(0, 1) + pair(0, 2)
    moved = lambda dx: [(dx, dz, w) for _, dz, w in across]
    blocks = [own, x_before, x_after, x_far, rest, r_before, r_after, r_far]
    pieces = [pair(0, 0), pair(3, 0), pair(1, 0), pair(2, 0), across, moved(3), moved(1), moved(2)]

    rows_own = lax.all_to_all(
        sent.reshape(EXPERTS, SLOTS, D), "y", split_axis=0, concat_axis=0, tiled=True
    ).reshape(ROWS, D)
    rows_own = after(rows_own, rest)
    rows_zl = hop(rows_own, "zl", 1)
    rows_c = hop(rows_own, "c", 1)
    rows_czl = hop(rows_zl, "c", 1)

    keep, send, far, plus, minus, mine = expert_compute([rows_own, rows_zl, rows_c, rows_czl], blocks, pieces)

    got = hop(send, "c", 1)
    to_zl = (keep[BACK:].astype(F32) + got[BACK:].astype(F32)).astype(BF)
    from_zl = hop(to_zl, "zl", 1)
    back = (keep[:BACK].astype(F32) + got[:BACK].astype(F32) + from_zl.astype(F32)).astype(BF)
    back = lax.all_to_all(back.reshape(EXPERTS, 8, D), "y", split_axis=0, concat_axis=0, tiled=True)
    token_grad, route_grad = finish(routing, route_weight, back.reshape(BACK, D))

    summed = ring_scatter(far, plus, minus, mine, "x")

    def quarter(shift):
        at = lax.rem(zi + jnp.where(ci == 0, shift, 4 - shift), 4)
        return lax.dynamic_slice(summed, (at * BLOCK, 0), (BLOCK, QUART))

    summed = ring_scatter(quarter(2), quarter(1), quarter(3), quarter(0), "zh")
    stay = lax.dynamic_slice(summed, (ci * SHARD, 0), (SHARD, QUART))
    cross = hop(lax.dynamic_slice(summed, ((1 - ci) * SHARD, 0), (SHARD, QUART)), "c", 1)
    down_grad = jnp.where(ci == 0, jnp.concatenate([stay, cross], axis=1), jnp.concatenate([cross, stay], axis=1))
    return token_grad, route_grad, down_grad


def solution(mesh):
    inner = Mesh(mesh.devices.reshape(4, 4, 2, 8, 2), AXES)
    rows = P(AXES, None)
    weights = P(("x", "zh", "c"), ("y", "zl"))
    return jax.shard_map(
        per_device,
        mesh=inner,
        in_specs=(rows, rows, rows, rows, weights, weights, weights),
        out_specs=(rows, rows, weights),
        check_vma=False,
    )
```

```python
import jax
import jax.numpy as jnp
from jax import lax
from jax.experimental import pallas as pl
from jax.experimental.pallas import tpu as pltpu
from jax.sharding import Mesh, PartitionSpec as P

BF = jnp.bfloat16
F32 = jnp.float32
I32 = jnp.int32
AXES = ("x", "zh", "c", "y", "zl")
TOK = 128
D = 3584
EXPERTS = 8
CAP = 6
QUART = 256
SHARD = 112
BLOCK = 2 * SHARD
XROWS = 4 * BLOCK
PEERS = 16
CHUNK = D // 4
SLAB = 48
GROUP = 8 * SLAB
ROWS = PEERS * CAP
PIECE = 512
WIDE = D + 128
VMEM_LIMIT = 28 * 1024 * 1024
VMEM = pl.BlockSpec(memory_space=pltpu.VMEM)


def iota(shape, dim):
    return lax.broadcasted_iota(I32, shape, dim)


def sixth(i):
    return (i * 43) >> 8


def regroup():
    a, i = iota((8, SLAB, GROUP), 0), iota((8, SLAB, GROUP), 1)
    b = sixth(i)
    hit = iota((8, SLAB, GROUP), 2) == b * SLAB + a * CAP + (i - CAP * b)
    return jnp.where(hit, 1.0, 0.0).reshape(GROUP, GROUP).astype(BF)


def token_ranks(ids):
    member = jnp.where(ids == iota((EXPERTS, TOK), 0), 1.0, 0.0)
    earlier = jnp.where(iota((TOK, TOK), 0) < iota((TOK, TOK), 1), 1.0, 0.0)
    counts = jnp.dot(member.astype(BF), earlier.astype(BF), preferred_element_type=F32)
    return jnp.sum(member * counts, axis=0, keepdims=True).astype(I32)


def to_column(row):
    diagonal = iota((TOK, TOK), 0) == iota((TOK, TOK), 1)
    return jnp.sum(jnp.where(diagonal, row, 0.0), axis=1, keepdims=True)


def dispatch_kernel(ids_ref, p_ref, x_ref, g_ref, out_ref):
    ids = ids_ref[...]
    slot = jnp.where(ids < EXPERTS, ids * CAP + token_ranks(ids), -1)
    i = iota((EXPERTS, 24, TOK), 1)
    which = sixth(i)
    mine = slot == iota((EXPERTS, 24, TOK), 0) * CAP + (i - CAP * which)
    sel = jnp.concatenate([
        jnp.where(mine & (which == j), 1.0, 0.0).reshape(EXPERTS * 24, TOK) for j in range(4)
    ], axis=1).astype(BF)
    scaled = (to_column(p_ref[...]) * g_ref[...].astype(F32)).astype(BF)
    halves = []
    for h in range(2):
        stack = []
        for q in (2 * h, 2 * h + 1):
            stack += [x_ref[:, q * CHUNK:(q + 1) * CHUNK], scaled[:, q * CHUNK:(q + 1) * CHUNK]]
        rows = jnp.dot(sel, jnp.concatenate(stack, axis=0), preferred_element_type=F32)
        halves.append(rows.reshape(EXPERTS, 24, CHUNK))
    rows = jnp.concatenate(halves, axis=1).astype(BF)
    for e in range(EXPERTS):
        out_ref[2 * e] = rows[e]
        out_ref[2 * e + 1] = rows[e]


def dispatch(ids, weight, tokens, grads):
    return pl.pallas_call(
        dispatch_kernel,
        in_specs=[VMEM] * 4,
        out_specs=VMEM,
        out_shape=jax.ShapeDtypeStruct((PEERS, SLAB, CHUNK), BF),
        compiler_params=pltpu.CompilerParams(vmem_limit_bytes=VMEM_LIMIT),
        cost_estimate=pl.CostEstimate(flops=4 * 10**8, bytes_accessed=4 * 10**6, transcendentals=0),
        name="dispatch",
    )(ids, weight, tokens, grads)


def combine_kernel(keep_ref, got_ref, out_ref):
    total = keep_ref[...].astype(F32) + got_ref[...].astype(F32)
    total = jnp.concatenate([total, jnp.zeros((ROWS, 8 * PIECE - WIDE), F32)], axis=1).astype(BF)
    order = regroup()
    for half in range(2):
        rows = total[half * SLAB:(half + 1) * SLAB]
        stack = jnp.concatenate([rows[:, q * PIECE:(q + 1) * PIECE] for q in range(8)], axis=0)
        moved = jnp.dot(order, stack, preferred_element_type=F32).astype(BF)
        out_ref[half * 8:(half + 1) * 8] = moved.reshape(8, SLAB, PIECE)


def combine(keep, got):
    return pl.pallas_call(
        combine_kernel,
        in_specs=[VMEM] * 2,
        out_specs=VMEM,
        out_shape=jax.ShapeDtypeStruct((PEERS, SLAB, PIECE), BF),
        compiler_params=pltpu.CompilerParams(vmem_limit_bytes=VMEM_LIMIT),
        cost_estimate=pl.CostEstimate(flops=3 * 10**8, bytes_accessed=2 * 10**6, transcendentals=0),
        name="combine",
    )(keep, got)


def finish_kernel(ids_ref, p_ref, rows_ref, tok_ref, route_ref):
    ids = ids_ref[...]
    base = jnp.where(ids < EXPERTS, ids * (2 * SLAB) + token_ranks(ids), -2 * D)
    base = to_column(base.astype(F32)).astype(I32)
    offset = iota((TOK, PEERS * SLAB), 1) - base
    for q in range(8):
        sel = jnp.where((offset == q * CAP) | (offset == q * CAP + SLAB), 1.0, 0.0).astype(BF)
        if q < 7:
            got = jnp.dot(sel, rows_ref[...], preferred_element_type=F32)
            tok_ref[:, q * PIECE:(q + 1) * PIECE] = got.astype(BF)
        else:
            route = jnp.dot(sel, rows_ref[:, :TOK], preferred_element_type=F32)[:, :1]
            diagonal = iota((TOK, TOK), 0) == iota((TOK, TOK), 1)
            route_ref[...] = jnp.sum(jnp.where(diagonal, route, 0.0), axis=0, keepdims=True) / p_ref[...]


def finish(ids, weight, rows):
    return pl.pallas_call(
        finish_kernel,
        in_specs=[VMEM] * 3,
        out_specs=[VMEM] * 2,
        out_shape=[jax.ShapeDtypeStruct((TOK, D), BF), jax.ShapeDtypeStruct((1, TOK), F32)],
        compiler_params=pltpu.CompilerParams(vmem_limit_bytes=VMEM_LIMIT),
        cost_estimate=pl.CostEstimate(flops=7 * 10**8, bytes_accessed=2 * 10**6, transcendentals=0),
        name="finish",
    )(ids, weight, rows)


def expert_kernel(pieces, *refs):
    row_refs = refs[:2]
    weight_refs = refs[2:2 + len(pieces)]
    keep_ref, send_ref, far_ref, plus_ref, minus_ref, own_ref = refs[2 + len(pieces):8 + len(pieces)]
    raw, x_rows, g_rows, weights, sem_rows, sem_weights = refs[8 + len(pieces):]
    xi, zi, ci = lax.axis_index("x"), lax.axis_index("zh"), lax.axis_index("c")
    row_copies = [pltpu.make_async_copy(ref, raw.at[i], sem_rows.at[i]) for i, ref in enumerate(row_refs)]
    weight_copies = []
    for ref, listed in zip(weight_refs, pieces):
        for at, (dx, dz, which) in enumerate(listed):
            block = lax.rem(xi + dx, 4) * 4 + lax.rem(zi + dz, 4)
            core = ci if which == 0 else 1 - ci
            start = pl.multiple_of(block * BLOCK + core * SHARD, 16)
            weight_copies.append(pltpu.make_async_copy(
                ref.at[pl.ds(at * SHARD, SHARD)],
                weights.at[pl.ds(start, SHARD)],
                sem_weights.at[len(weight_copies)],
            ))
    for copy in row_copies + weight_copies:
        copy.start()
    order = regroup()
    for i, copy in enumerate(row_copies):
        copy.wait()
        for half in range(2):
            part = raw[i, half * 8:(half + 1) * 8].reshape(GROUP, CHUNK)
            moved = jnp.dot(order, part, preferred_element_type=F32).astype(BF)
            at = (2 * i + half) * SLAB
            for q in range(4):
                columns = pl.ds(q * CHUNK, CHUNK)
                x_rows[at:at + SLAB, columns] = moved[2 * q * SLAB:(2 * q + 1) * SLAB]
                g_rows[at:at + SLAB, columns] = moved[(2 * q + 1) * SLAB:(2 * q + 2) * SLAB]
    for copy in weight_copies:
        copy.wait()
    pre = jnp.dot(x_rows[...], weights[:, :2 * QUART], preferred_element_type=F32)
    grad = jnp.dot(g_rows[...], weights[:, 2 * QUART:], preferred_element_type=F32)
    gate, up = pre[:, :QUART], pre[:, QUART:]
    sig = jax.nn.sigmoid(gate)
    act = gate * sig
    slope = sig * (1.0 + gate * (1.0 - sig))
    hidden = (act * up).astype(BF)
    route = jnp.sum(hidden.astype(F32) * grad, axis=1, keepdims=True)
    for ref, shift in ((far_ref, 2), (plus_ref, 1), (minus_ref, 3), (own_ref, 0)):
        start = pl.multiple_of(lax.rem(xi + shift, 4) * XROWS, 128)
        ref[...] = lax.dot_general(
            g_rows[:, pl.ds(start, XROWS)], hidden, (((0,), (0,)), ((), ())), preferred_element_type=F32
        ).astype(BF)
    d_pre = jnp.concatenate([(grad * up * slope).astype(BF), (grad * act).astype(BF)], axis=1)
    for i in range(4):
        part = lax.dot_general(
            d_pre, weights[i * CHUNK:(i + 1) * CHUNK, :2 * QUART], (((1,), (1,)), ((), ())),
            preferred_element_type=F32,
        ).astype(BF)
        keep_ref[:, i * CHUNK:(i + 1) * CHUNK] = part[:ROWS]
        send_ref[:, i * CHUNK:(i + 1) * CHUNK] = part[ROWS:]
    line = jnp.where(iota((2 * ROWS, 128), 1) == 0, route, 0.0).astype(BF)
    keep_ref[:, D:] = line[:ROWS]
    send_ref[:, D:] = line[ROWS:]


def expert_compute(rows, blocks, pieces):
    anywhere = pl.BlockSpec(memory_space=pl.ANY)
    count = sum(len(p) for p in pieces)
    back = jax.ShapeDtypeStruct((ROWS, WIDE), BF)
    down = jax.ShapeDtypeStruct((XROWS, QUART), BF)
    return pl.pallas_call(
        lambda *refs: expert_kernel(pieces, *refs),
        in_specs=[anywhere] * (2 + len(blocks)),
        out_specs=[VMEM] * 6,
        out_shape=[back, back, down, down, down, down],
        scratch_shapes=[
            pltpu.VMEM((2, PEERS, SLAB, CHUNK), BF),
            pltpu.VMEM((2 * ROWS, D), BF),
            pltpu.VMEM((2 * ROWS, D), BF),
            pltpu.VMEM((D, 3 * QUART), BF),
            pltpu.SemaphoreType.DMA((2,)),
            pltpu.SemaphoreType.DMA((count,)),
        ],
        compiler_params=pltpu.CompilerParams(vmem_limit_bytes=VMEM_LIMIT),
        cost_estimate=pl.CostEstimate(flops=4 * 10**9, bytes_accessed=12 * 10**6, transcendentals=49152),
        name="experts",
    )(*rows, *blocks)


def relay_kernel(plus_ref, minus_ref, low_ref, high_ref, _, plus_out, minus_out):
    half = XROWS // 2
    plus_out[:half] = add(plus_ref[:half], low_ref[...])
    plus_out[half:] = plus_ref[half:]
    minus_out[:half] = minus_ref[:half]
    minus_out[half:] = add(minus_ref[half:], high_ref[...])


def relay(plus, minus, low, high, message):
    down = jax.ShapeDtypeStruct((XROWS, QUART), BF)
    return pl.pallas_call(
        relay_kernel,
        in_specs=[VMEM] * 4 + [pl.BlockSpec(memory_space=pl.ANY)],
        out_specs=[VMEM] * 2,
        out_shape=[down, down],
        compiler_params=pltpu.CompilerParams(vmem_limit_bytes=VMEM_LIMIT),
        cost_estimate=pl.CostEstimate(flops=10**6, bytes_accessed=3 * 10**6, transcendentals=0),
        name="relay",
    )(plus, minus, low, high, message)


def hop(a, axis, shift):
    n = lax.axis_size(axis)
    return lax.ppermute(a, axis, [(i, (i + shift) % n) for i in range(n)])


def tie(*arrays):
    return lax.optimization_barrier(arrays)


def add(*terms):
    return sum(a.astype(F32) for a in terms).astype(BF)


def exchange(a, axes):
    return lax.all_to_all(a, axes, split_axis=0, concat_axis=0, tiled=True)


def per_device(tokens, grad_out, routing, route_weight, gate_weight, up_weight, down_weight):
    ci = lax.axis_index("c")
    ids, share = routing.reshape(1, TOK), route_weight.reshape(1, TOK)

    def columns(which):
        return jnp.concatenate([
            lax.dynamic_slice(w, (0, which * QUART), (SHARD, QUART)) for w in (gate_weight, up_weight, down_weight)
        ], axis=1)

    theirs = hop(columns(1 - ci), "c", 1)
    sent = dispatch(ids, share, tokens, grad_out)
    mine, sent = tie(columns(ci), sent)
    own = jnp.concatenate([mine, theirs], axis=0)

    z_before, z_after = hop(own, "zh", 1), hop(own, "zh", -1)
    x_before, x_after = hop(own, "x", 1), hop(own, "x", -1)
    z_before, z_after, x_before, x_after = tie(z_before, z_after, x_before, x_after)
    z_low, z_high = hop(z_before[:SHARD], "zh", 1), hop(z_after[SHARD:], "zh", -1)
    x_low, x_high = hop(x_before[:SHARD], "x", 1), hop(x_after[SHARD:], "x", -1)
    rest = jnp.concatenate([z_before, z_after, z_low, z_high], axis=0)
    r_before, r_after = hop(rest, "x", 1), hop(rest, "x", -1)
    half = 3 * SHARD
    r_low, r_high = hop(r_before[:half], "x", 1), hop(r_after[half:], "x", -1)

    across = [(0, 3, 0), (0, 3, 1), (0, 1, 0), (0, 1, 1), (0, 2, 0), (0, 2, 1)]
    moved = lambda dx, listed: [(dx, dz, w) for _, dz, w in listed]
    pair = [(0, 0, 0), (0, 0, 1)]
    blocks = [own, x_before, x_after, x_low, x_high, rest, r_before, r_after, r_low, r_high]
    pieces = [
        pair, moved(3, pair), moved(1, pair), moved(2, pair[:1]), moved(2, pair[1:]),
        across, moved(3, across), moved(1, across), moved(2, across[:3]), moved(2, across[3:]),
    ]

    rows = exchange(sent, ("y", "zl"))
    keep, send, far, plus, minus, mine = expert_compute([rows, hop(rows, "c", 1)], blocks, pieces)

    far, got = tie(far, hop(send, "c", 1))
    low, high = hop(far[:XROWS // 2], "x", 1), hop(far[XROWS // 2:], "x", -1)
    message = combine(keep, got)
    back = exchange(message, ("y", "zl"))
    token_grad, route_grad = finish(ids, share, back.reshape(PEERS * SLAB, PIECE))

    plus, minus = relay(plus, minus, low, high, message)
    summed = add(hop(plus, "x", 1), hop(minus, "x", -1), mine)
    summed = exchange(summed.reshape(8, SHARD, QUART), ("zh", "c")).reshape(4, 2, SHARD, QUART)
    summed = jnp.sum(summed.astype(F32), axis=0).astype(BF)
    down_grad = jnp.concatenate([summed[0], summed[1]], axis=1)
    return token_grad, route_grad.reshape(TOK, 1), down_grad


def solution(mesh):
    inner = Mesh(mesh.devices.reshape(4, 4, 2, 8, 2), AXES)
    rows = P(AXES, None)
    weights = P(("x", "zh", "c"), ("y", "zl"))
    return jax.shard_map(
        per_device,
        mesh=inner,
        in_specs=(rows, rows, rows, rows, weights, weights, weights),
        out_specs=(rows, rows, weights),
        check_vma=False,
    )
```

```python
import jax
import jax.numpy as jnp
from jax import lax
from jax.experimental import pallas as pl
from jax.experimental.pallas import tpu as pltpu
from jax.sharding import Mesh, PartitionSpec as P

BF = jnp.bfloat16
F32 = jnp.float32
I32 = jnp.int32
AXES = ("x", "zh", "c", "y", "zl")
TOK = 128
D = 3584
EXPERTS = 8
CAP = 6
QUART = 256
SHARD = 112
BLOCK = 2 * SHARD
XROWS = 4 * BLOCK
PEERS = 16
CHUNK = D // 4
SLAB = 48
GROUP = 8 * SLAB
ROWS = PEERS * CAP
PIECE = 512
WIDE = D + 128
VMEM_LIMIT = 16 * 1024 * 1024
MOST_VMEM = 56 * 1024 * 1024
VMEM = pl.BlockSpec(memory_space=pltpu.VMEM)


def iota(shape, dim):
    return lax.broadcasted_iota(I32, shape, dim)


def sixth(i):
    return (i * 43) >> 8


def regroup():
    a, i = iota((8, SLAB, GROUP), 0), iota((8, SLAB, GROUP), 1)
    b = sixth(i)
    hit = iota((8, SLAB, GROUP), 2) == b * SLAB + a * CAP + (i - CAP * b)
    return jnp.where(hit, 1.0, 0.0).reshape(GROUP, GROUP).astype(BF)


def token_ranks(ids):
    member = jnp.where(ids == iota((EXPERTS, TOK), 0), 1.0, 0.0)
    earlier = jnp.where(iota((TOK, TOK), 0) < iota((TOK, TOK), 1), 1.0, 0.0)
    counts = jnp.dot(member.astype(BF), earlier.astype(BF), preferred_element_type=F32)
    return jnp.sum(member * counts, axis=0, keepdims=True).astype(I32)


def to_column(row):
    diagonal = iota((TOK, TOK), 0) == iota((TOK, TOK), 1)
    return jnp.sum(jnp.where(diagonal, row, 0.0), axis=1, keepdims=True)


def dispatch_kernel(ids_ref, p_ref, x_ref, g_ref, out_ref):
    ids = ids_ref[...]
    slot = jnp.where(ids < EXPERTS, ids * CAP + token_ranks(ids), -1)
    i = iota((EXPERTS, 24, TOK), 1)
    which = sixth(i)
    mine = slot == iota((EXPERTS, 24, TOK), 0) * CAP + (i - CAP * which)
    sel = jnp.concatenate([
        jnp.where(mine & (which == j), 1.0, 0.0).reshape(EXPERTS * 24, TOK) for j in range(4)
    ], axis=1).astype(BF)
    scaled = (to_column(p_ref[...]) * g_ref[...].astype(F32)).astype(BF)
    halves = []
    for h in range(2):
        stack = []
        for q in (2 * h, 2 * h + 1):
            stack += [x_ref[:, q * CHUNK:(q + 1) * CHUNK], scaled[:, q * CHUNK:(q + 1) * CHUNK]]
        rows = jnp.dot(sel, jnp.concatenate(stack, axis=0), preferred_element_type=F32)
        halves.append(rows.reshape(EXPERTS, 24, CHUNK))
    rows = jnp.concatenate(halves, axis=1).astype(BF)
    out_ref[...] = rows


def dispatch(ids, weight, tokens, grads):
    return pl.pallas_call(
        dispatch_kernel,
        in_specs=[VMEM] * 4,
        out_specs=VMEM,
        out_shape=jax.ShapeDtypeStruct((EXPERTS, SLAB, CHUNK), BF),
        compiler_params=pltpu.CompilerParams(vmem_limit_bytes=VMEM_LIMIT),
        cost_estimate=pl.CostEstimate(flops=4 * 10**8, bytes_accessed=4 * 10**6, transcendentals=0),
        name="dispatch",
    )(ids, weight, tokens, grads)


def combine_kernel(keep_ref, got_ref, out_ref):
    total = keep_ref[...].astype(F32) + got_ref[...].astype(F32)
    total = jnp.concatenate([total, jnp.zeros((ROWS, 8 * PIECE - WIDE), F32)], axis=1).astype(BF)
    order = regroup()
    for half in range(2):
        rows = total[half * SLAB:(half + 1) * SLAB]
        stack = jnp.concatenate([rows[:, q * PIECE:(q + 1) * PIECE] for q in range(8)], axis=0)
        moved = jnp.dot(order, stack, preferred_element_type=F32).astype(BF)
        out_ref[:, half] = moved.reshape(EXPERTS, SLAB, PIECE)


def combine(keep, got):
    return pl.pallas_call(
        combine_kernel,
        in_specs=[VMEM] * 2,
        out_specs=VMEM,
        out_shape=jax.ShapeDtypeStruct((EXPERTS, 2, SLAB, PIECE), BF),
        compiler_params=pltpu.CompilerParams(vmem_limit_bytes=VMEM_LIMIT),
        cost_estimate=pl.CostEstimate(flops=3 * 10**8, bytes_accessed=2 * 10**6, transcendentals=0),
        name="combine",
    )(keep, got)


def finish_kernel(ids_ref, p_ref, rows_ref, tok_ref, route_ref):
    ids = ids_ref[...]
    base = jnp.where(ids < EXPERTS, ids * (2 * SLAB) + token_ranks(ids), -2 * D)
    base = to_column(base.astype(F32)).astype(I32)
    offset = iota((TOK, PEERS * SLAB), 1) - base
    for q in range(8):
        sel = jnp.where((offset == q * CAP) | (offset == q * CAP + SLAB), 1.0, 0.0).astype(BF)
        if q < 7:
            got = jnp.dot(sel, rows_ref[...], preferred_element_type=F32)
            tok_ref[:, q * PIECE:(q + 1) * PIECE] = got.astype(BF)
        else:
            route = jnp.dot(sel, rows_ref[:, :TOK], preferred_element_type=F32)[:, :1]
            diagonal = iota((TOK, TOK), 0) == iota((TOK, TOK), 1)
            route_ref[...] = jnp.sum(jnp.where(diagonal, route, 0.0), axis=0, keepdims=True) / p_ref[...]


def finish(ids, weight, rows):
    return pl.pallas_call(
        finish_kernel,
        in_specs=[VMEM] * 3,
        out_specs=[VMEM] * 2,
        out_shape=[jax.ShapeDtypeStruct((TOK, D), BF), jax.ShapeDtypeStruct((1, TOK), F32)],
        compiler_params=pltpu.CompilerParams(vmem_limit_bytes=VMEM_LIMIT),
        cost_estimate=pl.CostEstimate(flops=7 * 10**8, bytes_accessed=2 * 10**6, transcendentals=0),
        name="finish",
    )(ids, weight, rows)


def unpack_kernel(*refs):
    row_refs, x_ref, g_ref = refs[:4], refs[4], refs[5]
    zl = lax.axis_index("zl")
    order = regroup()
    for i, ref in enumerate(row_refs):
        moved = jnp.dot(order, ref[...].reshape(GROUP, CHUNK), preferred_element_type=F32).astype(BF)
        group = 2 * (i // 2) + (zl if i % 2 == 0 else 1 - zl)
        rows = pl.ds(pl.multiple_of(group * SLAB, SLAB), SLAB)
        for q in range(4):
            columns = pl.ds(q * CHUNK, CHUNK)
            x_ref[rows, columns] = moved[2 * q * SLAB:(2 * q + 1) * SLAB]
            g_ref[rows, columns] = moved[(2 * q + 1) * SLAB:(2 * q + 2) * SLAB]


def unpack(*rows):
    dense = jax.ShapeDtypeStruct((2 * ROWS, D), BF)
    return pl.pallas_call(
        unpack_kernel,
        in_specs=[VMEM] * 4,
        out_specs=[VMEM] * 2,
        out_shape=[dense, dense],
        compiler_params=pltpu.CompilerParams(vmem_limit_bytes=VMEM_LIMIT),
        cost_estimate=pl.CostEstimate(flops=10**9, bytes_accessed=5 * 10**6, transcendentals=0),
        name="unpack",
    )(*rows)


def stack_kernel(before_ref, after_ref, low_ref, high_ref, wide_ref, down_ref):
    at = 0
    for ref in (before_ref, after_ref, low_ref, high_ref):
        n = ref.shape[0]
        wide_ref[at:at + n] = ref[:, :2 * QUART]
        down_ref[at:at + n] = ref[:, 2 * QUART:]
        at += n


def stack(*parts):
    n = 6 * SHARD
    return pl.pallas_call(
        stack_kernel,
        in_specs=[VMEM] * 4,
        out_specs=[VMEM] * 2,
        out_shape=[jax.ShapeDtypeStruct((n, 2 * QUART), BF), jax.ShapeDtypeStruct((n, QUART), BF)],
        compiler_params=pltpu.CompilerParams(vmem_limit_bytes=VMEM_LIMIT),
        cost_estimate=pl.CostEstimate(flops=10**6, bytes_accessed=2 * 10**6, transcendentals=0),
        name="stack",
    )(*parts)


def hidden_kernel(pieces, *refs):
    x_ref, g_ref = refs[:2]
    weight_refs = refs[2:2 + len(pieces)]
    wide_ref, d_ref, line_ref, far_ref, plus_ref, minus_ref, own_ref, down, sems = refs[2 + len(pieces):]
    xi, zi, ci = lax.axis_index("x"), lax.axis_index("zh"), lax.axis_index("c")
    copies = []

    def copy(source, target):
        copies.append(pltpu.make_async_copy(source, target, sems.at[len(copies)]))

    for ref, listed in zip(weight_refs, pieces):
        for at, (kind, dx, dz, which) in enumerate(listed):
            x = dx if kind == "fixed" else lax.rem(xi + dx, 4)
            core = ci if which == 0 else 1 - ci
            rows = pl.ds(pl.multiple_of((x * 4 + lax.rem(zi + dz, 4)) * BLOCK + core * SHARD, 16), SHARD)
            source = ref.at[pl.ds(at * SHARD, SHARD)]
            if ref.shape[1] == QUART:
                copy(source, down.at[rows])
            elif ref.shape[1] == 2 * QUART:
                copy(source, wide_ref.at[rows])
            else:
                copy(source.at[:, pl.ds(0, 2 * QUART)], wide_ref.at[rows])
                copy(source.at[:, pl.ds(2 * QUART, QUART)], down.at[rows])
    for one in copies:
        one.start()
    for one in copies:
        one.wait()
    pre = jnp.dot(x_ref[...], wide_ref[...], preferred_element_type=F32)
    grad = jnp.dot(g_ref[...], down[...], preferred_element_type=F32)
    gate, up = pre[:, :QUART], pre[:, QUART:]
    sig = jax.nn.sigmoid(gate)
    act = gate * sig
    slope = sig * (1.0 + gate * (1.0 - sig))
    hidden = (act * up).astype(BF)
    route = jnp.sum(hidden.astype(F32) * grad, axis=1, keepdims=True)
    for ref, shift in ((far_ref, 2), (plus_ref, 1), (minus_ref, 3), (own_ref, 0)):
        start = pl.multiple_of(lax.rem(xi + shift, 4) * XROWS, 128)
        ref[...] = lax.dot_general(
            g_ref[:, pl.ds(start, XROWS)], hidden, (((0,), (0,)), ((), ())), preferred_element_type=F32
        ).astype(BF)
    d_ref[...] = jnp.concatenate([(grad * up * slope).astype(BF), (grad * act).astype(BF)], axis=1)
    line_ref[...] = jnp.where(iota((2 * ROWS, 128), 1) == 0, route, 0.0).astype(BF)


def hidden_compute(x_rows, g_rows, blocks, pieces):
    anywhere = pl.BlockSpec(memory_space=pl.ANY)
    count = sum(len(p) * (2 if b.shape[1] == 3 * QUART else 1) for p, b in zip(pieces, blocks))
    down = jax.ShapeDtypeStruct((XROWS, QUART), BF)
    return pl.pallas_call(
        lambda *refs: hidden_kernel(pieces, *refs),
        in_specs=[VMEM] * 2 + [anywhere] * len(blocks),
        out_specs=[VMEM] * 7,
        out_shape=[
            jax.ShapeDtypeStruct((D, 2 * QUART), BF),
            jax.ShapeDtypeStruct((2 * ROWS, 2 * QUART), BF),
            jax.ShapeDtypeStruct((2 * ROWS, 128), BF),
            down, down, down, down,
        ],
        scratch_shapes=[pltpu.VMEM((D, QUART), BF), pltpu.SemaphoreType.DMA((count,))],
        compiler_params=pltpu.CompilerParams(vmem_limit_bytes=MOST_VMEM),
        cost_estimate=pl.CostEstimate(flops=2 * 10**9, bytes_accessed=12 * 10**6, transcendentals=49152),
        name="hidden",
    )(x_rows, g_rows, *blocks)


def inputs_kernel(d_ref, line_ref, wide_ref, keep_ref, send_ref):
    for i in range(4):
        part = lax.dot_general(
            d_ref[...], wide_ref[i * CHUNK:(i + 1) * CHUNK], (((1,), (1,)), ((), ())), preferred_element_type=F32
        ).astype(BF)
        keep_ref[:, i * CHUNK:(i + 1) * CHUNK] = part[:ROWS]
        send_ref[:, i * CHUNK:(i + 1) * CHUNK] = part[ROWS:]
    keep_ref[:, D:] = line_ref[:ROWS]
    send_ref[:, D:] = line_ref[ROWS:]


def inputs_compute(d_pre, line, wide):
    back = jax.ShapeDtypeStruct((ROWS, WIDE), BF)
    return pl.pallas_call(
        inputs_kernel,
        in_specs=[VMEM] * 3,
        out_specs=[VMEM] * 2,
        out_shape=[back, back],
        compiler_params=pltpu.CompilerParams(vmem_limit_bytes=VMEM_LIMIT),
        cost_estimate=pl.CostEstimate(flops=7 * 10**8, bytes_accessed=6 * 10**6, transcendentals=0),
        name="inputs",
    )(d_pre, line, wide)


def relay_kernel(plus_ref, minus_ref, low_ref, high_ref, _, plus_out, minus_out):
    half = XROWS // 2
    plus_out[:half] = add(plus_ref[:half], low_ref[...])
    plus_out[half:] = plus_ref[half:]
    minus_out[:half] = minus_ref[:half]
    minus_out[half:] = add(minus_ref[half:], high_ref[...])


def relay(plus, minus, low, high, message):
    down = jax.ShapeDtypeStruct((XROWS, QUART), BF)
    return pl.pallas_call(
        relay_kernel,
        in_specs=[VMEM] * 4 + [pl.BlockSpec(memory_space=pl.ANY)],
        out_specs=[VMEM] * 2,
        out_shape=[down, down],
        compiler_params=pltpu.CompilerParams(vmem_limit_bytes=VMEM_LIMIT),
        cost_estimate=pl.CostEstimate(flops=10**6, bytes_accessed=3 * 10**6, transcendentals=0),
        name="relay",
    )(plus, minus, low, high, message)


def hop(a, axis, shift):
    n = lax.axis_size(axis)
    return lax.ppermute(a, axis, [(i, (i + shift) % n) for i in range(n)])


def tie(*arrays):
    return lax.optimization_barrier(arrays)


def add(*terms):
    return sum(a.astype(F32) for a in terms).astype(BF)


def exchange(a, axes):
    return lax.all_to_all(a, axes, split_axis=0, concat_axis=0, tiled=True)


def per_device(tokens, grad_out, routing, route_weight, gate_weight, up_weight, down_weight):
    ci = lax.axis_index("c")
    ids, share = routing.reshape(1, TOK), route_weight.reshape(1, TOK)

    def columns(which):
        return jnp.concatenate([
            lax.dynamic_slice(w, (0, which * QUART), (SHARD, QUART)) for w in (gate_weight, up_weight, down_weight)
        ], axis=1)

    theirs = hop(columns(1 - ci), "c", 1)
    sent = dispatch(ids, share, tokens, grad_out)
    own = jnp.concatenate([columns(ci), theirs], axis=0)

    own_all = lax.all_gather(own, "x", axis=0, tiled=True)
    z_before, z_after = hop(own, "zh", 1), hop(own, "zh", -1)
    z_low, z_high = hop(z_before[:SHARD], "zh", 1), hop(z_after[SHARD:], "zh", -1)
    rest, rest_down = stack(z_before, z_after, z_low, z_high)
    down_all = lax.all_gather(rest_down, "x", axis=0, tiled=True)
    r_before, r_after = hop(rest, "x", 1), hop(rest, "x", -1)
    half = 3 * SHARD
    r_low, r_high = hop(r_before[:half], "x", 1), hop(r_after[half:], "x", -1)

    across = [(3, 0), (3, 1), (1, 0), (1, 1), (2, 0), (2, 1)]
    listed = lambda kind, dx, shards: [(kind, dx, dz, w) for dz, w in shards]
    blocks = [own_all, down_all, rest, r_before, r_after, r_low, r_high]
    pieces = [
        sum([listed("fixed", x, [(0, 0), (0, 1)]) for x in range(4)], []),
        sum([listed("fixed", x, across) for x in range(4)], []),
        listed("moved", 0, across), listed("moved", 3, across), listed("moved", 1, across),
        listed("moved", 2, across[:3]), listed("moved", 2, across[3:]),
    ]

    rows = exchange(sent, "y")
    rows = tie(rows, rest)[0]
    rows_zl = hop(rows, "zl", 1)
    x_rows, g_rows = unpack(rows, rows_zl, hop(rows, "c", 1), hop(rows_zl, "c", 1))
    wide, d_pre, line, far, plus, minus, mine = hidden_compute(x_rows, g_rows, blocks, pieces)
    keep, send = inputs_compute(d_pre, line, wide)

    low, high = hop(far[:XROWS // 2], "x", 1), hop(far[XROWS // 2:], "x", -1)
    message = combine(keep, hop(send, "c", 1)).reshape(PEERS, SLAB, PIECE)
    back = exchange(message, ("y", "zl"))
    token_grad, route_grad = finish(ids, share, back.reshape(PEERS * SLAB, PIECE))

    plus, minus = relay(plus, minus, low, high, message)
    summed = add(hop(plus, "x", 1), hop(minus, "x", -1), mine)
    summed = exchange(summed.reshape(8, SHARD, QUART), ("zh", "c")).reshape(4, 2, SHARD, QUART)
    summed = jnp.sum(summed.astype(F32), axis=0).astype(BF)
    down_grad = jnp.concatenate([summed[0], summed[1]], axis=1)
    return token_grad, route_grad.reshape(TOK, 1), down_grad


def solution(mesh):
    inner = Mesh(mesh.devices.reshape(4, 4, 2, 8, 2), AXES)
    rows = P(AXES, None)
    weights = P(("x", "zh", "c"), ("y", "zl"))
    return jax.shard_map(
        per_device,
        mesh=inner,
        in_specs=(rows, rows, rows, rows, weights, weights, weights),
        out_specs=(rows, rows, weights),
        check_vma=False,
    )
```

```python
import jax
import jax.numpy as jnp
from jax import lax
from jax.experimental import pallas as pl
from jax.experimental.pallas import tpu as pltpu
from jax.sharding import Mesh, PartitionSpec as P

BF = jnp.bfloat16
F32 = jnp.float32
I32 = jnp.int32
AXES = ("x", "zh", "c", "y", "zl")
TOK = 128
D = 3584
EXPERTS = 8
CAP = 6
QUART = 256
SHARD = 112
BLOCK = 2 * SHARD
XROWS = 4 * BLOCK
PEERS = 16
CHUNK = D // 4
SLAB = 48
GROUP = 8 * SLAB
ROWS = PEERS * CAP
PIECE = 512
WIDE = D + 128
VMEM_LIMIT = 16 * 1024 * 1024
MOST_VMEM = 44 * 1024 * 1024
INPUTS_VMEM = 24 * 1024 * 1024
VMEM = pl.BlockSpec(memory_space=pltpu.VMEM)


def iota(shape, dim):
    return lax.broadcasted_iota(I32, shape, dim)


def sixth(i):
    return (i * 43) >> 8


def regroup():
    a, i = iota((8, SLAB, GROUP), 0), iota((8, SLAB, GROUP), 1)
    b = sixth(i)
    hit = iota((8, SLAB, GROUP), 2) == b * SLAB + a * CAP + (i - CAP * b)
    return jnp.where(hit, 1.0, 0.0).reshape(GROUP, GROUP).astype(BF)


def token_ranks(ids):
    member = jnp.where(ids == iota((EXPERTS, TOK), 0), 1.0, 0.0)
    earlier = jnp.where(iota((TOK, TOK), 0) < iota((TOK, TOK), 1), 1.0, 0.0)
    counts = jnp.dot(member.astype(BF), earlier.astype(BF), preferred_element_type=F32)
    return jnp.sum(member * counts, axis=0, keepdims=True).astype(I32)


def to_column(row):
    diagonal = iota((TOK, TOK), 0) == iota((TOK, TOK), 1)
    return jnp.sum(jnp.where(diagonal, row, 0.0), axis=1, keepdims=True)


def dispatch_kernel(ids_ref, p_ref, x_ref, g_ref, out_ref):
    ids = ids_ref[...]
    slot = jnp.where(ids < EXPERTS, ids * CAP + token_ranks(ids), -1)
    i = iota((EXPERTS, 24, TOK), 1)
    which = sixth(i)
    mine = slot == iota((EXPERTS, 24, TOK), 0) * CAP + (i - CAP * which)
    sel = jnp.concatenate([
        jnp.where(mine & (which == j), 1.0, 0.0).reshape(EXPERTS * 24, TOK) for j in range(4)
    ], axis=1).astype(BF)
    scaled = (to_column(p_ref[...]) * g_ref[...].astype(F32)).astype(BF)
    halves = []
    for h in range(2):
        stack = []
        for q in (2 * h, 2 * h + 1):
            stack += [x_ref[:, q * CHUNK:(q + 1) * CHUNK], scaled[:, q * CHUNK:(q + 1) * CHUNK]]
        rows = jnp.dot(sel, jnp.concatenate(stack, axis=0), preferred_element_type=F32)
        halves.append(rows.reshape(EXPERTS, 24, CHUNK))
    rows = jnp.concatenate(halves, axis=1).astype(BF)
    out_ref[...] = rows


def dispatch(ids, weight, tokens, grads):
    return pl.pallas_call(
        dispatch_kernel,
        in_specs=[VMEM] * 4,
        out_specs=VMEM,
        out_shape=jax.ShapeDtypeStruct((EXPERTS, SLAB, CHUNK), BF),
        compiler_params=pltpu.CompilerParams(vmem_limit_bytes=VMEM_LIMIT),
        cost_estimate=pl.CostEstimate(flops=4 * 10**8, bytes_accessed=4 * 10**6, transcendentals=0),
        name="dispatch",
    )(ids, weight, tokens, grads)


def combine_kernel(keep_ref, got_ref, out_ref):
    total = keep_ref[...].astype(F32) + got_ref[...].astype(F32)
    total = jnp.concatenate([total, jnp.zeros((ROWS, 8 * PIECE - WIDE), F32)], axis=1).astype(BF)
    order = regroup()
    for half in range(2):
        rows = total[half * SLAB:(half + 1) * SLAB]
        stack = jnp.concatenate([rows[:, q * PIECE:(q + 1) * PIECE] for q in range(8)], axis=0)
        moved = jnp.dot(order, stack, preferred_element_type=F32).astype(BF)
        out_ref[:, half] = moved.reshape(EXPERTS, SLAB, PIECE)


def combine(keep, got):
    return pl.pallas_call(
        combine_kernel,
        in_specs=[VMEM] * 2,
        out_specs=VMEM,
        out_shape=jax.ShapeDtypeStruct((EXPERTS, 2, SLAB, PIECE), BF),
        compiler_params=pltpu.CompilerParams(vmem_limit_bytes=VMEM_LIMIT),
        cost_estimate=pl.CostEstimate(flops=3 * 10**8, bytes_accessed=2 * 10**6, transcendentals=0),
        name="combine",
    )(keep, got)


def finish_kernel(ids_ref, p_ref, rows_ref, tok_ref, route_ref):
    ids = ids_ref[...]
    base = jnp.where(ids < EXPERTS, ids * (2 * SLAB) + token_ranks(ids), -2 * D)
    base = to_column(base.astype(F32)).astype(I32)
    offset = iota((TOK, PEERS * SLAB), 1) - base
    for q in range(8):
        sel = jnp.where((offset == q * CAP) | (offset == q * CAP + SLAB), 1.0, 0.0).astype(BF)
        if q < 7:
            got = jnp.dot(sel, rows_ref[...], preferred_element_type=F32)
            tok_ref[:, q * PIECE:(q + 1) * PIECE] = got.astype(BF)
        else:
            route = jnp.dot(sel, rows_ref[:, :TOK], preferred_element_type=F32)[:, :1]
            diagonal = iota((TOK, TOK), 0) == iota((TOK, TOK), 1)
            route_ref[...] = jnp.sum(jnp.where(diagonal, route, 0.0), axis=0, keepdims=True) / p_ref[...]


def finish(ids, weight, rows):
    return pl.pallas_call(
        finish_kernel,
        in_specs=[VMEM] * 3,
        out_specs=[VMEM] * 2,
        out_shape=[jax.ShapeDtypeStruct((TOK, D), BF), jax.ShapeDtypeStruct((1, TOK), F32)],
        compiler_params=pltpu.CompilerParams(vmem_limit_bytes=VMEM_LIMIT),
        cost_estimate=pl.CostEstimate(flops=7 * 10**8, bytes_accessed=2 * 10**6, transcendentals=0),
        name="finish",
    )(ids, weight, rows)


def unpack_kernel(*refs):
    row_refs, x_ref, g_ref = refs[:4], refs[4], refs[5]
    zl = lax.axis_index("zl")
    order = regroup()
    for i, ref in enumerate(row_refs):
        moved = jnp.dot(order, ref[...].reshape(GROUP, CHUNK), preferred_element_type=F32).astype(BF)
        group = 2 * (i // 2) + (zl if i % 2 == 0 else 1 - zl)
        rows = pl.ds(pl.multiple_of(group * SLAB, SLAB), SLAB)
        for q in range(4):
            columns = pl.ds(q * CHUNK, CHUNK)
            x_ref[rows, columns] = moved[2 * q * SLAB:(2 * q + 1) * SLAB]
            g_ref[rows, columns] = moved[(2 * q + 1) * SLAB:(2 * q + 2) * SLAB]


def unpack(*rows):
    dense = jax.ShapeDtypeStruct((2 * ROWS, D), BF)
    return pl.pallas_call(
        unpack_kernel,
        in_specs=[VMEM] * 4,
        out_specs=[VMEM] * 2,
        out_shape=[dense, dense],
        compiler_params=pltpu.CompilerParams(vmem_limit_bytes=VMEM_LIMIT),
        cost_estimate=pl.CostEstimate(flops=10**9, bytes_accessed=5 * 10**6, transcendentals=0),
        name="unpack",
    )(*rows)


def hidden_kernel(pieces, *refs):
    x_ref, g_ref = refs[:2]
    weight_refs = refs[2:2 + len(pieces)]
    wide_ref, pre_ref, hidden_ref, far_ref, plus_ref, minus_ref, own_ref, sems = refs[2 + len(pieces):]
    xi, zi, ci = lax.axis_index("x"), lax.axis_index("zh"), lax.axis_index("c")
    copies = []
    for ref, listed in zip(weight_refs, pieces):
        for at, (dx, dz, which) in enumerate(listed):
            block = lax.rem(xi + dx, 4) * 4 + lax.rem(zi + dz, 4)
            core = ci if which == 0 else 1 - ci
            start = pl.multiple_of(block * BLOCK + core * SHARD, 16)
            copies.append(pltpu.make_async_copy(
                ref.at[pl.ds(at * SHARD, SHARD)], wide_ref.at[pl.ds(start, SHARD)], sems.at[len(copies)]
            ))
    for copy in copies:
        copy.start()
    for copy in copies:
        copy.wait()
    pre = jnp.dot(x_ref[...], wide_ref[...], preferred_element_type=F32)
    pre_ref[...] = pre
    gate, up = pre[:, :QUART], pre[:, QUART:]
    hidden = (gate * jax.nn.sigmoid(gate) * up).astype(BF)
    hidden_ref[...] = hidden
    for ref, shift in ((far_ref, 2), (plus_ref, 1), (minus_ref, 3), (own_ref, 0)):
        start = pl.multiple_of(lax.rem(xi + shift, 4) * XROWS, 128)
        ref[...] = lax.dot_general(
            g_ref[:, pl.ds(start, XROWS)], hidden, (((0,), (0,)), ((), ())), preferred_element_type=F32
        ).astype(BF)


def hidden_compute(x_rows, g_rows, blocks, pieces):
    anywhere = pl.BlockSpec(memory_space=pl.ANY)
    down = jax.ShapeDtypeStruct((XROWS, QUART), BF)
    return pl.pallas_call(
        lambda *refs: hidden_kernel(pieces, *refs),
        in_specs=[VMEM] * 2 + [anywhere] * len(blocks),
        out_specs=[VMEM] * 7,
        out_shape=[
            jax.ShapeDtypeStruct((D, 2 * QUART), BF),
            jax.ShapeDtypeStruct((2 * ROWS, 2 * QUART), F32),
            jax.ShapeDtypeStruct((2 * ROWS, QUART), BF),
            down, down, down, down,
        ],
        scratch_shapes=[pltpu.SemaphoreType.DMA((sum(len(p) for p in pieces),))],
        compiler_params=pltpu.CompilerParams(vmem_limit_bytes=MOST_VMEM),
        cost_estimate=pl.CostEstimate(flops=10**9, bytes_accessed=8 * 10**6, transcendentals=49152),
        name="hidden",
    )(x_rows, g_rows, *blocks)


def inputs_kernel(g_ref, wide_ref, pre_ref, hidden_ref, down_ref, keep_ref, send_ref, down, sem):
    columns = pl.ds(pl.multiple_of(lax.axis_index("c") * QUART, QUART), QUART)
    copy = pltpu.make_async_copy(down_ref.at[:, columns], down, sem)
    copy.start()
    gate, up = pre_ref[:, :QUART], pre_ref[:, QUART:]
    sig = jax.nn.sigmoid(gate)
    act = gate * sig
    slope = sig * (1.0 + gate * (1.0 - sig))
    copy.wait()
    grad = jnp.dot(g_ref[...], down[...], preferred_element_type=F32)
    route = jnp.sum(hidden_ref[...].astype(F32) * grad, axis=1, keepdims=True)
    d_pre = jnp.concatenate([(grad * up * slope).astype(BF), (grad * act).astype(BF)], axis=1)
    for i in range(4):
        part = lax.dot_general(
            d_pre, wide_ref[i * CHUNK:(i + 1) * CHUNK], (((1,), (1,)), ((), ())), preferred_element_type=F32
        ).astype(BF)
        keep_ref[:, i * CHUNK:(i + 1) * CHUNK] = part[:ROWS]
        send_ref[:, i * CHUNK:(i + 1) * CHUNK] = part[ROWS:]
    line = jnp.where(iota((2 * ROWS, 128), 1) == 0, route, 0.0).astype(BF)
    keep_ref[:, D:] = line[:ROWS]
    send_ref[:, D:] = line[ROWS:]


def inputs_compute(g_rows, wide, pre, hidden, down_all):
    back = jax.ShapeDtypeStruct((ROWS, WIDE), BF)
    return pl.pallas_call(
        inputs_kernel,
        in_specs=[VMEM] * 4 + [pl.BlockSpec(memory_space=pl.ANY)],
        out_specs=[VMEM] * 2,
        out_shape=[back, back],
        scratch_shapes=[pltpu.VMEM((D, QUART), BF), pltpu.SemaphoreType.DMA(())],
        compiler_params=pltpu.CompilerParams(vmem_limit_bytes=INPUTS_VMEM),
        cost_estimate=pl.CostEstimate(flops=10**9, bytes_accessed=8 * 10**6, transcendentals=49152),
        name="inputs",
    )(g_rows, wide, pre, hidden, down_all)


def relay_kernel(plus_ref, minus_ref, low_ref, high_ref, plus_out, minus_out):
    half = XROWS // 2
    plus_out[:half] = add(plus_ref[:half], low_ref[...])
    plus_out[half:] = plus_ref[half:]
    minus_out[:half] = minus_ref[:half]
    minus_out[half:] = add(minus_ref[half:], high_ref[...])


def relay(plus, minus, low, high):
    down = jax.ShapeDtypeStruct((XROWS, QUART), BF)
    return pl.pallas_call(
        relay_kernel,
        in_specs=[VMEM] * 4,
        out_specs=[VMEM] * 2,
        out_shape=[down, down],
        compiler_params=pltpu.CompilerParams(vmem_limit_bytes=VMEM_LIMIT),
        cost_estimate=pl.CostEstimate(flops=10**6, bytes_accessed=3 * 10**6, transcendentals=0),
        name="relay",
    )(plus, minus, low, high)


def hop(a, axis, shift):
    n = lax.axis_size(axis)
    return lax.ppermute(a, axis, [(i, (i + shift) % n) for i in range(n)])


def tie(*arrays):
    return lax.optimization_barrier(arrays)


def add(*terms):
    return sum(a.astype(F32) for a in terms).astype(BF)


def exchange(a, axes):
    return lax.all_to_all(a, axes, split_axis=0, concat_axis=0, tiled=True)


def per_device(tokens, grad_out, routing, route_weight, gate_weight, up_weight, down_weight):
    zi, ci = lax.axis_index("zh"), lax.axis_index("c")
    ids, share = routing.reshape(1, TOK), route_weight.reshape(1, TOK)

    def columns(which):
        return jnp.concatenate([
            lax.dynamic_slice(w, (0, which * QUART), (SHARD, QUART)) for w in (gate_weight, up_weight)
        ], axis=1)

    down_all = lax.all_gather(down_weight, ("x", "zh", "c"), axis=0, tiled=True)
    theirs = hop(columns(1 - ci), "c", 1)
    sent = dispatch(ids, share, tokens, grad_out)
    own = jnp.concatenate([columns(ci), theirs], axis=0)

    z_before, z_after = hop(own, "zh", 1), hop(own, "zh", -1)
    z_low, z_high = hop(z_before[:SHARD], "zh", 1), hop(z_after[SHARD:], "zh", -1)
    line = jnp.concatenate([own, z_before, z_after, z_low, z_high], axis=0)
    before, after = hop(line, "x", 1), hop(line, "x", -1)
    half = 4 * SHARD
    low, high = hop(before[:half], "x", 1), hop(after[half:], "x", -1)

    across = [(0, 0), (0, 1), (3, 0), (3, 1), (1, 0), (1, 1), (2, 0), (2, 1)]
    listed = lambda dx, shards: [(dx, dz, w) for dz, w in shards]
    blocks = [line, before, after, low, high]
    pieces = [listed(0, across), listed(3, across), listed(1, across), listed(2, across[:4]), listed(2, across[4:])]

    rows = tie(exchange(sent, "y"), line)[0]
    rows_zl = hop(rows, "zl", 1)
    x_rows, g_rows = unpack(rows, rows_zl, hop(rows, "c", 1), hop(rows_zl, "c", 1))
    wide, pre, hidden, far, plus, minus, mine = hidden_compute(x_rows, g_rows, blocks, pieces)

    low, high = hop(far[:XROWS // 2], "x", 1), hop(far[XROWS // 2:], "x", -1)
    down_all, low, high = tie(down_all, low, high)
    keep, send = inputs_compute(g_rows, wide, pre, hidden, down_all)
    message = combine(keep, hop(send, "c", 1)).reshape(PEERS, SLAB, PIECE)
    back = exchange(message, ("y", "zl"))
    token_grad, route_grad = finish(ids, share, back.reshape(PEERS * SLAB, PIECE))

    plus, minus = relay(plus, minus, low, high)
    summed = add(hop(plus, "x", 1), hop(minus, "x", -1), mine)

    def quarter(shift):
        return lax.dynamic_slice(summed, (lax.rem(zi + shift, 4) * BLOCK, 0), (BLOCK, QUART))

    far, plus, minus, mine = quarter(2), quarter(1), quarter(3), quarter(0)
    low, high = hop(far[:SHARD], "zh", 1), hop(far[SHARD:], "zh", -1)
    plus = jnp.concatenate([add(plus[:SHARD], low), plus[SHARD:]], axis=0)
    minus = jnp.concatenate([minus[:SHARD], add(minus[SHARD:], high)], axis=0)
    summed = add(hop(plus, "zh", 1), hop(minus, "zh", -1), mine)
    stay = lax.dynamic_slice(summed, (ci * SHARD, 0), (SHARD, QUART))
    cross = hop(lax.dynamic_slice(summed, ((1 - ci) * SHARD, 0), (SHARD, QUART)), "c", 1)
    down_grad = jnp.where(ci == 0, jnp.concatenate([stay, cross], axis=1), jnp.concatenate([cross, stay], axis=1))
    return token_grad, route_grad.reshape(TOK, 1), down_grad


def solution(mesh):
    inner = Mesh(mesh.devices.reshape(4, 4, 2, 8, 2), AXES)
    rows = P(AXES, None)
    weights = P(("x", "zh", "c"), ("y", "zl"))
    return jax.shard_map(
        per_device,
        mesh=inner,
        in_specs=(rows, rows, rows, rows, weights, weights, weights),
        out_specs=(rows, rows, weights),
        check_vma=False,
    )
```

```python
import jax
import jax.numpy as jnp
from jax import lax
from jax.experimental import pallas as pl
from jax.experimental.pallas import tpu as pltpu
from jax.sharding import Mesh, PartitionSpec as P

BF = jnp.bfloat16
F32 = jnp.float32
I32 = jnp.int32
AXES = ("x", "zh", "c", "y", "zl")
PEERS = ("x", "y", "zl")
TOK = 128
D = 3584
EXPERTS = 8
CAP = 6
HALF = 512
SHARD = 112
PART = D // 4
SOURCES = 2 * EXPERTS
ROWS = SOURCES * CAP
VMEM_LIMIT = 24 * 1024 * 1024
VMEM = pl.BlockSpec(memory_space=pltpu.VMEM)


def iota(shape, dim):
    return lax.broadcasted_iota(I32, shape, dim)


def onehot(hit):
    return jnp.where(hit, 1.0, 0.0).astype(BF)


def sixth(i):
    return (i * 171) >> 10


def token_ranks(ids):
    member = jnp.where(ids == iota((EXPERTS, TOK), 0), 1.0, 0.0)
    earlier = onehot(iota((TOK, TOK), 0) < iota((TOK, TOK), 1))
    counts = jnp.dot(member.astype(BF), earlier, preferred_element_type=F32)
    return jnp.sum(member * counts, axis=0, keepdims=True).astype(I32)


def to_column(row):
    diagonal = iota((TOK, TOK), 0) == iota((TOK, TOK), 1)
    return jnp.sum(jnp.where(diagonal, row, 0.0), axis=1, keepdims=True)


def call(body, name, out_shape, operands, flops, scratch=(), specs=None):
    return pl.pallas_call(
        body,
        in_specs=specs or [VMEM] * len(operands),
        out_specs=[VMEM] * len(out_shape),
        out_shape=[jax.ShapeDtypeStruct(shape, kind) for shape, kind in out_shape],
        scratch_shapes=list(scratch),
        compiler_params=pltpu.CompilerParams(vmem_limit_bytes=VMEM_LIMIT),
        cost_estimate=pl.CostEstimate(flops=flops, bytes_accessed=4 * 10**6, transcendentals=0),
        name=name,
    )(*operands)


def dispatch_kernel(ids_ref, p_ref, x_ref, g_ref, out_ref):
    ids = ids_ref[...]
    slot = jnp.where(ids < EXPERTS, ids * 16 + token_ranks(ids), -16)
    at = iota((TOK, TOK), 0)
    sel = jnp.concatenate([onehot(slot == at), onehot(slot + 8 == at)], axis=1)
    scaled = (to_column(p_ref[...]) * g_ref[...].astype(F32)).astype(BF)
    for i in range(4):
        columns = slice(i * PART, (i + 1) * PART)
        both = jnp.concatenate([x_ref[:, columns], scaled[:, columns]], axis=0)
        rows = jnp.dot(sel, both, preferred_element_type=F32).astype(BF).reshape(EXPERTS, 16, PART)
        out_ref[i, :, 0] = rows
        out_ref[i, :, 1] = rows


def before_kernel(rows_ref, weight_ref, part_ref, g_ref, x_scr):
    row, at = iota((2 * ROWS, SOURCES * 16), 0), iota((2 * ROWS, SOURCES * 16), 1)
    grad = jnp.where(row >= ROWS, 1, 0)
    slot = row - ROWS * grad
    source = sixth(slot)
    pick = onehot(at == source * 16 + (slot - CAP * source) + 8 * grad)
    for i in range(4):
        moved = jnp.dot(pick, rows_ref[i], preferred_element_type=F32).astype(BF)
        x_scr[i * ROWS:(i + 1) * ROWS] = moved[:ROWS]
        g_ref[i * ROWS:(i + 1) * ROWS] = moved[ROWS:]
    pre = jnp.dot(x_scr[...], weight_ref[:, :2 * HALF], preferred_element_type=F32).astype(BF)
    part_ref[:, :, :2 * HALF] = pre.reshape(4, ROWS, 2 * HALF)
    hid = jnp.dot(g_ref[...], weight_ref[:, 2 * HALF:], preferred_element_type=F32).astype(BF)
    part_ref[:, :, 2 * HALF:] = hid.reshape(4, ROWS, HALF)


def middle_kernel(part_ref, out_ref, line_ref):
    total = part_ref[0].astype(F32) + part_ref[1].astype(F32) + part_ref[2].astype(F32) + part_ref[3].astype(F32)
    gate, up, grad = total[:, :HALF], total[:, HALF:2 * HALF], total[:, 2 * HALF:]
    sig = jax.nn.sigmoid(gate)
    act = gate * sig
    slope = sig * (1.0 + gate * (1.0 - sig))
    hidden = (act * up).astype(BF)
    route = jnp.sum(hidden.astype(F32) * grad, axis=1, keepdims=True)
    d_gate, d_up = (grad * up * slope).astype(BF), (grad * act).astype(BF)
    for i in range(4):
        out_ref[i, :, :HALF] = d_gate
        out_ref[i, :, HALF:2 * HALF] = d_up
        out_ref[i, :, 2 * HALF:] = hidden
    row = iota((ROWS, 128), 0)
    line_ref[...] = jnp.where(iota((ROWS, 128), 1) == row - CAP * sixth(row), route, 0.0).astype(BF)


def after_kernel(mid_ref, line_ref, g_ref, weight_ref, back_ref, far_ref, plus_ref, minus_ref, own_ref, send_ref, down):
    xi, zi, ci = lax.axis_index("x"), lax.axis_index("zh"), lax.axis_index("c")
    mid = mid_ref[...].reshape(4 * ROWS, 3 * HALF)
    down[...] = lax.dot_general(
        g_ref[...], mid[:, 2 * HALF:], (((0,), (0,)), ((), ())), preferred_element_type=F32
    ).astype(BF)

    def shard(shift, core):
        block = 2 * lax.rem(zi + shift, 4) + core
        return down[pl.ds(pl.multiple_of(block * SHARD, 16), SHARD)]

    for i, (ref, shift) in enumerate(((far_ref, 2), (plus_ref, 1), (minus_ref, 3), (own_ref, 0))):
        ref[...] = shard(shift, ci)
        send_ref[i] = shard(shift, 1 - ci)
    grads = lax.dot_general(
        mid[:, :2 * HALF], weight_ref[:, :2 * HALF], (((1,), (1,)), ((), ())), preferred_element_type=F32
    ).astype(BF)
    row, at = iota((SOURCES * 8, ROWS), 0), iota((SOURCES * 8, ROWS), 1)
    source = sixth(at)
    spread = onehot(row == source * 8 + (at - CAP * source))
    gather = onehot(row == source * 8 + CAP)
    extra = jnp.dot(gather, line_ref[...], preferred_element_type=F32)
    for i in range(4):
        rows = jnp.dot(spread, grads[i * ROWS:(i + 1) * ROWS], preferred_element_type=F32)
        first = rows[:, :128] + jnp.where(xi == i, extra, 0.0)
        back_ref[i] = jnp.concatenate([first, rows[:, 128:]], axis=1).astype(BF)


def finish_kernel(ids_ref, p_ref, rows_ref, tok_ref, route_ref):
    ids = ids_ref[...]
    rank = token_ranks(ids)
    valid = ids < EXPERTS
    base = to_column(jnp.where(valid, ids * 16, -64).astype(F32)).astype(I32)
    rank = to_column(rank.astype(F32)).astype(I32)
    at = iota((TOK, TOK), 1)
    sel = onehot((at == base + rank) | (at == base + rank + 8))
    pick = onehot((at == base + CAP) | (at == base + CAP + 8))
    values = jnp.zeros((TOK, TOK), F32)
    for i in range(4):
        got = jnp.dot(sel, rows_ref[i], preferred_element_type=F32)
        tok_ref[:, i * PART:(i + 1) * PART] = got.astype(BF)
        values = values + jnp.dot(pick, rows_ref[i, :, :TOK], preferred_element_type=F32)
    route = jnp.sum(jnp.where(at == rank, values, 0.0), axis=1, keepdims=True)
    diagonal = iota((TOK, TOK), 0) == at
    route_ref[...] = jnp.sum(jnp.where(diagonal, route, 0.0), axis=0, keepdims=True) / p_ref[...]


def hop(a, axis, shift):
    n = lax.axis_size(axis)
    return lax.ppermute(a, axis, [(i, (i + shift) % n) for i in range(n)])


def add(*terms):
    return sum(a.astype(F32) for a in terms).astype(BF)


def exchange(a, axes):
    return lax.all_to_all(a, axes, split_axis=0, concat_axis=0, tiled=True)


def per_device(tokens, grad_out, routing, route_weight, gate_weight, up_weight, down_weight):
    ids, share = routing.reshape(1, TOK), route_weight.reshape(1, TOK)
    weights = jnp.concatenate([gate_weight, up_weight, down_weight], axis=1)
    weights = lax.all_gather(weights, ("zh", "c"), axis=0, tiled=True)

    sent, = call(dispatch_kernel, "dispatch", [((4, EXPERTS, 2, 16, PART), BF)],
                 (ids, share, tokens, grad_out), 3 * 10**8)
    rows = exchange(sent.reshape(64, 16, PART), PEERS).reshape(4, SOURCES * 16, PART)
    part, g_rows = call(before_kernel, "before", [((4, ROWS, 3 * HALF), BF), ((4 * ROWS, PART), BF)],
                        (rows, weights), 14 * 10**8, [pltpu.VMEM((4 * ROWS, PART), BF)])
    mid, line = call(middle_kernel, "middle", [((4, ROWS, 3 * HALF), BF), ((ROWS, 128), BF)],
                     (exchange(part, "x"),), 10**7)
    shard = ((SHARD, HALF), BF)
    back, far, plus, minus, mine, send = call(
        after_kernel, "after",
        [((4, SOURCES * 8, PART), BF), shard, shard, shard, shard, ((4, SHARD, HALF), BF)],
        (exchange(mid, "x"), line, g_rows, weights), 14 * 10**8, [pltpu.VMEM((PART, HALF), BF)],
    )
    back = exchange(back.reshape(64, 8, PART), PEERS).reshape(4, SOURCES * 8, PART)
    token_grad, route_grad = call(finish_kernel, "finish", [((TOK, D), BF), ((1, TOK), F32)],
                                  (ids, share, back), 2 * 10**8)

    got = hop(send, "c", 1)
    far, plus, minus, mine = [add(a, got[i]) for i, a in enumerate((far, plus, minus, mine))]
    cut = SHARD // 2
    low, high = hop(far[:cut], "zh", 1), hop(far[cut:], "zh", -1)
    plus = jnp.concatenate([add(plus[:cut], low), plus[cut:]], axis=0)
    minus = jnp.concatenate([minus[:cut], add(minus[cut:], high)], axis=0)
    down_grad = add(hop(plus, "zh", 1), hop(minus, "zh", -1), mine)
    return token_grad, route_grad.reshape(TOK, 1), down_grad


def solution(mesh):
    inner = Mesh(mesh.devices.reshape(4, 4, 2, 8, 2), AXES)
    rows = P(AXES, None)
    weights = P(("x", "zh", "c"), ("y", "zl"))
    return jax.shard_map(
        per_device,
        mesh=inner,
        in_specs=(rows, rows, rows, rows, weights, weights, weights),
        out_specs=(rows, rows, weights),
        check_vma=False,
    )
```

```python
import jax
import jax.numpy as jnp
from jax import lax
from jax.experimental import pallas as pl
from jax.experimental.pallas import tpu as pltpu
from jax.sharding import Mesh, PartitionSpec as P

BF = jnp.bfloat16
F32 = jnp.float32
I32 = jnp.int32
AXES = ("x", "zh", "c", "y", "zl")
PEERS = ("x", "y", "zl")
TOK = 128
D = 3584
EXPERTS = 8
CAP = 6
HALF = 512
SHARD = 112
PART = D // 4
SOURCES = 2 * EXPERTS
ROWS = SOURCES * CAP
SLAB = 88
VMEM_LIMIT = 24 * 1024 * 1024
MOST_VMEM = 56 * 1024 * 1024
ANYWHERE = pl.BlockSpec(memory_space=pl.ANY)
VMEM = pl.BlockSpec(memory_space=pltpu.VMEM)


def iota(shape, dim):
    return lax.broadcasted_iota(I32, shape, dim)


def onehot(hit):
    return jnp.where(hit, 1.0, 0.0).astype(BF)


def sixth(i):
    return (i * 171) >> 10


def token_ranks(ids):
    member = jnp.where(ids == iota((EXPERTS, TOK), 0), 1.0, 0.0)
    earlier = onehot(iota((TOK, TOK), 0) < iota((TOK, TOK), 1))
    counts = jnp.dot(member.astype(BF), earlier, preferred_element_type=F32)
    return jnp.sum(member * counts, axis=0, keepdims=True).astype(I32)


def to_column(row):
    diagonal = iota((TOK, TOK), 0) == iota((TOK, TOK), 1)
    return jnp.sum(jnp.where(diagonal, row, 0.0), axis=1, keepdims=True)


def call(body, name, out_shape, operands, flops, scratch=(), specs=None, limit=VMEM_LIMIT):
    return pl.pallas_call(
        body,
        in_specs=specs or [VMEM] * len(operands),
        out_specs=[VMEM] * len(out_shape),
        out_shape=[jax.ShapeDtypeStruct(shape, kind) for shape, kind in out_shape],
        scratch_shapes=list(scratch),
        compiler_params=pltpu.CompilerParams(vmem_limit_bytes=limit),
        cost_estimate=pl.CostEstimate(flops=flops, bytes_accessed=4 * 10**6, transcendentals=0),
        name=name,
    )(*operands)


def dispatch_kernel(ids_hbm, p_hbm, x_hbm, g_hbm, out_ref, ids_ref, p_ref, x_ref, g_ref, sems):
    copies = [
        pltpu.make_async_copy(source, target, sems.at[i])
        for i, (source, target) in enumerate(((ids_hbm, ids_ref), (p_hbm, p_ref), (x_hbm, x_ref), (g_hbm, g_ref)))
    ]
    for copy in copies:
        copy.start()
    k, at = iota((EXPERTS, SLAB, 7 * TOK), 1), iota((EXPERTS, SLAB, 7 * TOK), 2)
    q = (k * 43) >> 9
    k = k - 12 * q
    order = q * TOK + iota((EXPERTS, SLAB, 7 * TOK), 0) * 16 + k + jnp.where(k >= CAP, 2, 0)
    order = onehot(at == order).reshape(EXPERTS * SLAB, 7 * TOK)
    for copy in copies:
        copy.wait()
    ids = ids_ref[...]
    slot = jnp.where(ids < EXPERTS, ids * 16 + token_ranks(ids), -16)
    at = iota((TOK, TOK), 0)
    sel = jnp.concatenate([onehot(slot == at), onehot(slot + 8 == at)], axis=1)
    scaled = (to_column(p_ref[...]) * g_ref[...].astype(F32)).astype(BF)
    both = jnp.concatenate([x_ref[...], scaled], axis=0)
    rows = jnp.dot(sel, both, preferred_element_type=F32).astype(BF)
    for i in range(2):
        stack = []
        for q in range(7):
            left = 2 * i * PART + q * TOK
            stack.append(jnp.concatenate([rows[:, left:left + TOK], rows[:, left + PART:left + PART + TOK]], axis=1))
        moved = jnp.dot(order, jnp.concatenate(stack, axis=0), preferred_element_type=F32).astype(BF)
        for j in range(2):
            one = moved[:, j * TOK:(j + 1) * TOK].reshape(EXPERTS, SLAB, TOK)
            out_ref[2 * i + j, :, 0] = one
            out_ref[2 * i + j, :, 1] = one


def before_kernel(rows_ref, wide_hbm, line_ref, other_ref, part_ref, g_ref, x_scr, wide, down, sem):
    zi, ci = lax.axis_index("zh"), lax.axis_index("c")
    copy = pltpu.make_async_copy(wide_hbm, wide, sem)
    copy.start()
    shape = (7, 2, 48, EXPERTS * SLAB)
    j = iota(shape, 2)
    source = sixth(j)
    place = source * SLAB + iota(shape, 0) * 12 + iota(shape, 1) * CAP + (j - CAP * source)
    pick = onehot(iota(shape, 3) == place).reshape(7 * ROWS, EXPERTS * SLAB)
    for i in range(2):
        for h in range(2):
            half = slice(h * EXPERTS * SLAB, (h + 1) * EXPERTS * SLAB)
            both = jnp.concatenate([rows_ref[2 * i, half], rows_ref[2 * i + 1, half]], axis=1)
            moved = jnp.dot(pick, both, preferred_element_type=F32).astype(BF)
            for k in range(2):
                at = slice((2 * i + k) * ROWS + h * 48, (2 * i + k) * ROWS + h * 48 + 48)
                for q in range(7):
                    columns = slice(q * TOK, (q + 1) * TOK)
                    x_scr[at, columns] = moved[q * ROWS:q * ROWS + 48, k * TOK:(k + 1) * TOK]
                    g_ref[at, columns] = moved[q * ROWS + 48:(q + 1) * ROWS, k * TOK:(k + 1) * TOK]
    for i, shift in enumerate((0, 3, 1, 2)):
        block = 2 * lax.rem(zi + shift, 4)
        rows = slice(i * SHARD, (i + 1) * SHARD)
        down[pl.ds(pl.multiple_of((block + ci) * SHARD, 16), SHARD)] = line_ref[rows]
        down[pl.ds(pl.multiple_of((block + 1 - ci) * SHARD, 16), SHARD)] = other_ref[rows]
    hid = jnp.dot(g_ref[...], down[...], preferred_element_type=F32).astype(BF)
    part_ref[:, :, 2 * HALF:] = hid.reshape(4, ROWS, HALF)
    copy.wait()
    pre = jnp.dot(x_scr[...], wide[...], preferred_element_type=F32).astype(BF)
    part_ref[:, :, :2 * HALF] = pre.reshape(4, ROWS, 2 * HALF)


def middle_kernel(part_ref, out_ref, line_ref):
    total = part_ref[0].astype(F32) + part_ref[1].astype(F32) + part_ref[2].astype(F32) + part_ref[3].astype(F32)
    gate, up, grad = total[:, :HALF], total[:, HALF:2 * HALF], total[:, 2 * HALF:]
    sig = jax.nn.sigmoid(gate)
    act = gate * sig
    slope = sig * (1.0 + gate * (1.0 - sig))
    hidden = (act * up).astype(BF)
    route = jnp.sum(hidden.astype(F32) * grad, axis=1, keepdims=True)
    d_gate, d_up = (grad * up * slope).astype(BF), (grad * act).astype(BF)
    for i in range(4):
        out_ref[i, :, :HALF] = d_gate
        out_ref[i, :, HALF:2 * HALF] = d_up
        out_ref[i, :, 2 * HALF:] = hidden
    row = iota((ROWS, 128), 0)
    line_ref[...] = jnp.where(iota((ROWS, 128), 1) == row - CAP * sixth(row), route, 0.0).astype(BF)


def after_kernel(mid_ref, line_ref, g_ref, weight_ref, back_ref, far_ref, plus_ref, minus_ref, own_ref, send_ref, down):
    xi, zi, ci = lax.axis_index("x"), lax.axis_index("zh"), lax.axis_index("c")
    mid = mid_ref[...].reshape(4 * ROWS, 3 * HALF)
    down[...] = lax.dot_general(
        g_ref[...], mid[:, 2 * HALF:], (((0,), (0,)), ((), ())), preferred_element_type=F32
    ).astype(BF)

    def shard(shift, core):
        block = 2 * lax.rem(zi + shift, 4) + core
        return down[pl.ds(pl.multiple_of(block * SHARD, 16), SHARD)]

    for i, (ref, shift) in enumerate(((far_ref, 2), (plus_ref, 1), (minus_ref, 3), (own_ref, 0))):
        ref[...] = shard(shift, ci)
        send_ref[i] = shard(shift, 1 - ci)
    grads = lax.dot_general(
        mid[:, :2 * HALF], weight_ref[...], (((1,), (1,)), ((), ())), preferred_element_type=F32
    ).astype(BF)
    row, at = iota((SOURCES * 8, ROWS), 0), iota((SOURCES * 8, ROWS), 1)
    source = sixth(at)
    spread = onehot(row == source * 8 + (at - CAP * source))
    gather = onehot(row == source * 8 + CAP)
    extra = jnp.dot(gather, line_ref[...], preferred_element_type=F32)
    for i in range(4):
        rows = jnp.dot(spread, grads[i * ROWS:(i + 1) * ROWS], preferred_element_type=F32)
        first = rows[:, :128] + jnp.where(xi == i, extra, 0.0)
        back_ref[i] = jnp.concatenate([first, rows[:, 128:]], axis=1).astype(BF)


def finish_kernel(ids_ref, p_ref, rows_ref, tok_ref, route_ref):
    ids = ids_ref[...]
    rank = token_ranks(ids)
    valid = ids < EXPERTS
    base = to_column(jnp.where(valid, ids * 16, -64).astype(F32)).astype(I32)
    rank = to_column(rank.astype(F32)).astype(I32)
    at = iota((TOK, TOK), 1)
    sel = onehot((at == base + rank) | (at == base + rank + 8))
    pick = onehot((at == base + CAP) | (at == base + CAP + 8))
    values = jnp.zeros((TOK, TOK), F32)
    for i in range(4):
        got = jnp.dot(sel, rows_ref[i], preferred_element_type=F32)
        tok_ref[:, i * PART:(i + 1) * PART] = got.astype(BF)
        values = values + jnp.dot(pick, rows_ref[i, :, :TOK], preferred_element_type=F32)
    route = jnp.sum(jnp.where(at == rank, values, 0.0), axis=1, keepdims=True)
    diagonal = iota((TOK, TOK), 0) == at
    route_ref[...] = jnp.sum(jnp.where(diagonal, route, 0.0), axis=0, keepdims=True) / p_ref[...]


def hop(a, axis, shift):
    n = lax.axis_size(axis)
    return lax.ppermute(a, axis, [(i, (i + shift) % n) for i in range(n)])


def add(*terms):
    return sum(a.astype(F32) for a in terms).astype(BF)


def exchange(a, axes):
    return lax.all_to_all(a, axes, split_axis=0, concat_axis=0, tiled=True)


def per_device(tokens, grad_out, routing, route_weight, gate_weight, up_weight, down_weight):
    ids, share = routing.reshape(1, TOK), route_weight.reshape(1, TOK)
    wide = lax.all_gather(jnp.concatenate([gate_weight, up_weight], axis=1), ("zh", "c"), axis=0, tiled=True)

    sent, = call(
        dispatch_kernel, "dispatch", [((4, EXPERTS, 2, SLAB, TOK), BF)], (ids, share, tokens, grad_out), 10**9,
        [pltpu.VMEM((1, TOK), I32), pltpu.VMEM((1, TOK), F32), pltpu.VMEM((TOK, D), BF), pltpu.VMEM((TOK, D), BF),
         pltpu.SemaphoreType.DMA((4,))], [ANYWHERE] * 4, MOST_VMEM,
    )
    rows = exchange(sent.reshape(64, SLAB, TOK), PEERS).reshape(4, SOURCES * SLAB, TOK)

    cut = SHARD // 2
    z_before, z_after = hop(down_weight, "zh", 1), hop(down_weight, "zh", -1)
    z_low, z_high = hop(z_before[:cut], "zh", 1), hop(z_after[cut:], "zh", -1)
    shards = jnp.concatenate([down_weight, z_before, z_after, z_low, z_high], axis=0)
    part, g_rows = call(
        before_kernel, "before", [((4, ROWS, 3 * HALF), BF), ((4 * ROWS, PART), BF)],
        (rows, wide, shards, hop(shards, "c", 1)), 2 * 10**9,
        [pltpu.VMEM((4 * ROWS, PART), BF), pltpu.VMEM((PART, 2 * HALF), BF), pltpu.VMEM((PART, HALF), BF),
         pltpu.SemaphoreType.DMA(())], [VMEM, ANYWHERE, VMEM, VMEM],
    )
    mid, line = call(middle_kernel, "middle", [((4, ROWS, 3 * HALF), BF), ((ROWS, 128), BF)],
                     (exchange(part, "x"),), 10**7)
    shard = ((SHARD, HALF), BF)
    back, far, plus, minus, mine, send = call(
        after_kernel, "after",
        [((4, SOURCES * 8, PART), BF), shard, shard, shard, shard, ((4, SHARD, HALF), BF)],
        (exchange(mid, "x"), line, g_rows, wide), 14 * 10**8, [pltpu.VMEM((PART, HALF), BF)],
    )
    back = exchange(back.reshape(64, 8, PART), PEERS).reshape(4, SOURCES * 8, PART)
    token_grad, route_grad = call(finish_kernel, "finish", [((TOK, D), BF), ((1, TOK), F32)],
                                  (ids, share, back), 2 * 10**8)

    got = hop(send, "c", 1)
    far, plus, minus, mine = [add(a, got[i]) for i, a in enumerate((far, plus, minus, mine))]
    down_grad = add(hop(plus, "zh", 1), hop(minus, "zh", -1), hop(far, "zh", 2), mine)
    return token_grad, route_grad.reshape(TOK, 1), down_grad


def solution(mesh):
    inner = Mesh(mesh.devices.reshape(4, 4, 2, 8, 2), AXES)
    rows = P(AXES, None)
    weights = P(("x", "zh", "c"), ("y", "zl"))
    return jax.shard_map(
        per_device,
        mesh=inner,
        in_specs=(rows, rows, rows, rows, weights, weights, weights),
        out_specs=(rows, rows, weights),
        check_vma=False,
    )
```

```python
import jax
import jax.numpy as jnp
from jax import lax
from jax.experimental import pallas as pl
from jax.experimental.pallas import tpu as pltpu
from jax.sharding import Mesh, PartitionSpec as P

BF = jnp.bfloat16
F32 = jnp.float32
I32 = jnp.int32
AXES = ("x", "zh", "c", "y", "zl")
PEERS = ("x", "y")
TOK = 128
D = 3584
EXPERTS = 8
CAP = 6
HALF = 512
SHARD = 112
PART = D // 4
ROWS = 2 * EXPERTS * CAP
SLAB = 48
GROUP = 8 * SLAB
VMEM_LIMIT = 56 * 1024 * 1024
MOST_VMEM = 56 * 1024 * 1024
ANYWHERE = pl.BlockSpec(memory_space=pl.ANY)
VMEM = pl.BlockSpec(memory_space=pltpu.VMEM)


def iota(shape, dim):
    return lax.broadcasted_iota(I32, shape, dim)


def onehot(hit):
    return jnp.where(hit, 1.0, 0.0).astype(BF)


def sixth(i):
    return (i * 43) >> 8


def regroup():
    a, i = iota((8, SLAB, GROUP), 0), iota((8, SLAB, GROUP), 1)
    b = sixth(i)
    return onehot(iota((8, SLAB, GROUP), 2) == b * SLAB + a * CAP + (i - CAP * b)).reshape(GROUP, GROUP)


def token_ranks(ids):
    member = jnp.where(ids == iota((EXPERTS, TOK), 0), 1.0, 0.0)
    earlier = onehot(iota((TOK, TOK), 0) < iota((TOK, TOK), 1))
    counts = jnp.dot(member.astype(BF), earlier, preferred_element_type=F32)
    return jnp.sum(member * counts, axis=0, keepdims=True).astype(I32)


def to_column(row):
    diagonal = iota((TOK, TOK), 0) == iota((TOK, TOK), 1)
    return jnp.sum(jnp.where(diagonal, row, 0.0), axis=1, keepdims=True)


def call(body, name, out_shape, operands, flops, scratch=(), specs=None, limit=VMEM_LIMIT):
    return pl.pallas_call(
        body,
        in_specs=specs or [VMEM] * len(operands),
        out_specs=[VMEM] * len(out_shape),
        out_shape=[jax.ShapeDtypeStruct(shape, kind) for shape, kind in out_shape],
        scratch_shapes=list(scratch),
        compiler_params=pltpu.CompilerParams(vmem_limit_bytes=limit),
        cost_estimate=pl.CostEstimate(flops=flops, bytes_accessed=4 * 10**6, transcendentals=0),
        name=name,
    )(*operands)


def dispatch_kernel(ids_hbm, p_hbm, rows_hbm, out_ref, ids_ref, p_ref, rows_ref, sems, scale):
    copies = [
        pltpu.make_async_copy(source, target, sems.at[i])
        for i, (source, target) in enumerate(((ids_hbm, ids_ref), (p_hbm, p_ref), (rows_hbm, rows_ref)))
    ]
    for copy in copies:
        copy.start()
    k, at = iota((EXPERTS, SLAB, 7 * 64), 1), iota((EXPERTS, SLAB, 7 * 64), 2)
    q = sixth(k)
    order = onehot((at == q * 64 + iota((EXPERTS, SLAB, 7 * 64), 0) * 8 + (k - CAP * q)) & (q < 7))
    order = order.reshape(GROUP, 7 * 64)
    for copy in copies:
        copy.wait()
    ids = ids_ref[...]
    slot = jnp.where(ids < EXPERTS, ids * 8 + token_ranks(ids), -16)
    sel = onehot(slot == iota((64, TOK), 0))
    rows = rows_ref[...]
    if scale:
        rows = (to_column(p_ref[...]) * rows.astype(F32)).astype(BF)
    rows = jnp.dot(sel, rows, preferred_element_type=F32).astype(BF)
    for i in range(2):
        stack = []
        for q in range(7):
            left = 2 * i * PART + q * TOK
            stack.append(jnp.concatenate([rows[:, left:left + TOK], rows[:, left + PART:left + PART + TOK]], axis=1))
        moved = jnp.dot(order, jnp.concatenate(stack, axis=0), preferred_element_type=F32).astype(BF)
        for j in range(2):
            out_ref[2 * i + j] = moved[:, j * TOK:(j + 1) * TOK].reshape(EXPERTS, SLAB, TOK)


def dispatch(ids, share, rows, scale, name):
    return call(
        lambda *refs: dispatch_kernel(*refs, scale), name, [((4, EXPERTS, SLAB, TOK), BF)], (ids, share, rows),
        3 * 10**8,
        [pltpu.VMEM((1, TOK), I32), pltpu.VMEM((1, TOK), F32), pltpu.VMEM((TOK, D), BF), pltpu.SemaphoreType.DMA((3,))],
        [ANYWHERE] * 3, MOST_VMEM,
    )[0]


def unpack(mine_ref, other_ref, out_ref):
    zl = lax.axis_index("zl")
    order = regroup()
    for ref, z in ((mine_ref, zl), (other_ref, 1 - zl)):
        for i in range(2):
            both = jnp.concatenate([ref[2 * i], ref[2 * i + 1]], axis=1)
            moved = jnp.dot(order, both, preferred_element_type=F32).astype(BF)
            for j in range(2):
                rows = pl.ds(pl.multiple_of((2 * (2 * i + j) + z) * SLAB, 16), SLAB)
                for q in range(7):
                    part = moved[q * SLAB:(q + 1) * SLAB, j * TOK:(j + 1) * TOK]
                    out_ref[rows, q * TOK:(q + 1) * TOK] = part


def gate_up_kernel(mine_ref, other_ref, weights_hbm, part_ref, x_scr, wide, sem):
    copy = pltpu.make_async_copy(weights_hbm.at[:, pl.ds(0, 2 * HALF)], wide, sem)
    copy.start()
    unpack(mine_ref, other_ref, x_scr)
    copy.wait()
    pre = jnp.dot(x_scr[...], wide[...], preferred_element_type=F32).astype(BF)
    part_ref[...] = pre.reshape(4, ROWS, 2 * HALF)


def hidden_grad_kernel(mine_ref, other_ref, weights_hbm, g_ref, own_ref, plus_ref, minus_ref, far_ref, part, down, sem):
    xi = lax.axis_index("x")
    copy = pltpu.make_async_copy(weights_hbm.at[:, pl.ds(2 * HALF, HALF)], down, sem)
    copy.start()
    unpack(mine_ref, other_ref, g_ref)
    copy.wait()
    part[...] = jnp.dot(g_ref[...], down[...], preferred_element_type=F32).astype(BF)
    for ref, shift in ((own_ref, 0), (plus_ref, 1), (minus_ref, 3), (far_ref, 2)):
        ref[...] = part[pl.ds(pl.multiple_of(lax.rem(xi + shift, 4) * ROWS, 16), ROWS)]


def middle_kernel(part_ref, a_ref, b_ref, c_ref, d_ref, out_ref, line_ref):
    total = part_ref[0].astype(F32) + part_ref[1].astype(F32) + part_ref[2].astype(F32) + part_ref[3].astype(F32)
    grad = a_ref[...].astype(F32) + b_ref[...].astype(F32) + c_ref[...].astype(F32) + d_ref[...].astype(F32)
    gate, up = total[:, :HALF], total[:, HALF:]
    sig = jax.nn.sigmoid(gate)
    act = gate * sig
    slope = sig * (1.0 + gate * (1.0 - sig))
    hidden = (act * up).astype(BF)
    route = jnp.sum(hidden.astype(F32) * grad, axis=1, keepdims=True)
    d_gate, d_up = (grad * up * slope).astype(BF), (grad * act).astype(BF)
    for i in range(4):
        out_ref[i, :, :HALF] = d_gate
        out_ref[i, :, HALF:2 * HALF] = d_up
        out_ref[i, :, 2 * HALF:] = hidden
    line_ref[...] = jnp.where(iota((ROWS, TOK), 1) == 0, route, 0.0).astype(BF)


def after_kernel(mid_ref, line_ref, g_ref, weights_hbm, keep_ref, give_ref,
                 far_ref, plus_ref, minus_ref, own_ref, send_ref, down, wide, grads, line, sem):
    xi, zi, ci, zl = [lax.axis_index(a) for a in ("x", "zh", "c", "zl")]
    copy = pltpu.make_async_copy(weights_hbm.at[:, pl.ds(0, 2 * HALF)], wide, sem)
    copy.start()
    mid = mid_ref[...].reshape(4 * ROWS, 3 * HALF)
    copy.wait()
    grads[...] = lax.dot_general(
        mid[:, :2 * HALF], wide[...], (((1,), (1,)), ((), ())), preferred_element_type=F32
    ).astype(BF)
    line[...] = line_ref[...]
    for ref, z in ((keep_ref, zl), (give_ref, 1 - zl)):
        own = line[pl.ds(pl.multiple_of(z * SLAB, 16), SLAB)]
        for i in range(4):
            ref[i, :, :PART] = grads[pl.ds(pl.multiple_of((2 * i + z) * SLAB, 16), SLAB)]
            ref[i, :, PART:] = jnp.where(xi == i, own, jnp.zeros_like(own))
    down[...] = lax.dot_general(
        g_ref[...], mid[:, 2 * HALF:], (((0,), (0,)), ((), ())), preferred_element_type=F32
    ).astype(BF)

    def shard(shift, core):
        block = 2 * lax.rem(zi + shift, 4) + core
        return down[pl.ds(pl.multiple_of(block * SHARD, 16), SHARD)]

    for i, (ref, shift) in enumerate(((far_ref, 2), (plus_ref, 1), (minus_ref, 3), (own_ref, 0))):
        ref[...] = shard(shift, ci)
        send_ref[i] = shard(shift, 1 - ci)


def combine_kernel(keep_ref, got_ref, out_ref):
    order = regroup()
    for i in range(2):
        left, right = add(keep_ref[2 * i], got_ref[2 * i]), add(keep_ref[2 * i + 1], got_ref[2 * i + 1])
        stack = []
        for q in range(8):
            columns = slice(q * TOK, (q + 1) * TOK)
            stack.append(jnp.concatenate([left[:, columns], right[:, columns]], axis=1))
        moved = jnp.dot(order, jnp.concatenate(stack, axis=0), preferred_element_type=F32).astype(BF)
        for j in range(2):
            out_ref[2 * i + j] = moved[:, j * TOK:(j + 1) * TOK].reshape(EXPERTS, SLAB, TOK)


def finish_kernel(ids_ref, p_ref, rows_ref, tok_ref, route_ref):
    ids = ids_ref[...]
    base = jnp.where(ids < EXPERTS, ids * SLAB + token_ranks(ids), -GROUP)
    offset = iota((TOK, GROUP), 1) - to_column(base.astype(F32)).astype(I32)
    pairs = [jnp.concatenate([rows_ref[2 * i], rows_ref[2 * i + 1]], axis=1) for i in range(2)]
    route = jnp.zeros((TOK, 1), F32)
    for q in range(8):
        sel = onehot(offset == q * CAP)
        for i in range(2):
            got = jnp.dot(sel, pairs[i], preferred_element_type=F32)
            if q == 7:
                route = route + got[:, :1] + got[:, TOK:TOK + 1]
                continue
            for j in range(2):
                left = (2 * i + j) * PART + q * TOK
                tok_ref[:, left:left + TOK] = got[:, j * TOK:(j + 1) * TOK].astype(BF)
    diagonal = iota((TOK, TOK), 0) == iota((TOK, TOK), 1)
    route_ref[...] = jnp.sum(jnp.where(diagonal, route, 0.0), axis=0, keepdims=True) / p_ref[...]


def hop(a, axis, shift):
    n = lax.axis_size(axis)
    return lax.ppermute(a, axis, [(i, (i + shift) % n) for i in range(n)])


def add(*terms):
    return sum(a.astype(F32) for a in terms).astype(BF)


def exchange(a, axes):
    return lax.all_to_all(a, axes, split_axis=0, concat_axis=0, tiled=True)


def per_device(tokens, grad_out, routing, route_weight, gate_weight, up_weight, down_weight):
    ids, share = routing.reshape(1, TOK), route_weight.reshape(1, TOK)
    weights = jnp.concatenate([gate_weight, up_weight, down_weight], axis=1)
    weights = lax.all_gather(weights, ("zh", "c"), axis=0, tiled=True)

    def send_rows(a):
        return exchange(a.reshape(32, SLAB, TOK), PEERS).reshape(4, GROUP, TOK)

    x_own = send_rows(dispatch(ids, share, tokens, False, "pack_tokens"))
    g_own = send_rows(dispatch(ids, share, grad_out, True, "pack_grads"))
    x_own, x_other, g_other = lax.optimization_barrier((x_own, hop(x_own, "zl", 1), hop(g_own, "zl", 1)))
    x_rows, g_rows = (x_own, x_other), (g_own, g_other)

    semaphore = pltpu.SemaphoreType.DMA(())
    dense = pltpu.VMEM((4 * ROWS, PART), BF)
    part, = call(
        gate_up_kernel, "gate_up", [((4, ROWS, 2 * HALF), BF)], (*x_rows, weights), 10**9,
        [dense, pltpu.VMEM((PART, 2 * HALF), BF), semaphore], [VMEM, VMEM, ANYWHERE],
    )
    block = ((ROWS, HALF), BF)
    g_dense, own, plus, minus, far = call(
        hidden_grad_kernel, "hidden_grad", [((4 * ROWS, PART), BF), block, block, block, block], (*g_rows, weights),
        6 * 10**8, [pltpu.VMEM((4 * ROWS, HALF), BF), pltpu.VMEM((PART, HALF), BF), semaphore], [VMEM, VMEM, ANYWHERE],
    )
    mid, line = call(
        middle_kernel, "middle", [((4, ROWS, 3 * HALF), BF), ((ROWS, TOK), BF)],
        (exchange(part, "x"), own, hop(plus, "x", 1), hop(minus, "x", -1), hop(far, "x", 2)), 10**7,
    )
    shard, wide = ((SHARD, HALF), BF), ((4, SLAB, PART + TOK), BF)
    keep, give, far, plus, minus, mine, send = call(
        after_kernel, "after", [wide, wide, shard, shard, shard, shard, ((4, SHARD, HALF), BF)],
        (exchange(mid, "x"), line, g_dense, weights), 14 * 10**8,
        [pltpu.VMEM((PART, HALF), BF), pltpu.VMEM((PART, 2 * HALF), BF), dense, pltpu.VMEM((ROWS, TOK), BF), semaphore],
        [VMEM, VMEM, VMEM, ANYWHERE],
    )
    back, = call(combine_kernel, "combine", [((4, EXPERTS, SLAB, TOK), BF)], (keep, hop(give, "zl", 1)), 2 * 10**8)
    back = exchange(back.reshape(32, SLAB, TOK), PEERS).reshape(4, GROUP, TOK)
    token_grad, route_grad = call(finish_kernel, "finish", [((TOK, D), BF), ((1, TOK), F32)],
                                  (ids, share, back), 4 * 10**8)

    got = hop(send, "c", 1)
    far, plus, minus, mine = [add(a, got[i]) for i, a in enumerate((far, plus, minus, mine))]
    down_grad = add(hop(plus, "zh", 1), hop(minus, "zh", -1), hop(far, "zh", 2), mine)
    return token_grad, route_grad.reshape(TOK, 1), down_grad


def solution(mesh):
    inner = Mesh(mesh.devices.reshape(4, 4, 2, 8, 2), AXES)
    rows = P(AXES, None)
    weights = P(("x", "zh", "c"), ("y", "zl"))
    return jax.shard_map(
        per_device,
        mesh=inner,
        in_specs=(rows, rows, rows, rows, weights, weights, weights),
        out_specs=(rows, rows, weights),
        check_vma=False,
    )
```

```python
import jax
import jax.numpy as jnp
from jax import lax
from jax.experimental import pallas as pl
from jax.experimental.pallas import tpu as pltpu
from jax.sharding import Mesh, PartitionSpec as P

BF = jnp.bfloat16
F32 = jnp.float32
I32 = jnp.int32
AXES = ("x", "zh", "c", "y", "zl")
PEERS = ("x", "y")
TOK = 128
D = 3584
EXPERTS = 8
CAP = 6
HALF = 512
SHARD = 112
PART = D // 4
ROWS = 2 * EXPERTS * CAP
SLAB = 48
GROUP = 8 * SLAB
WIDE = 88
WIDER = 8 * WIDE
VMEM_LIMIT = 24 * 1024 * 1024
MOST_VMEM = 56 * 1024 * 1024
ANYWHERE = pl.BlockSpec(memory_space=pl.ANY)
VMEM = pl.BlockSpec(memory_space=pltpu.VMEM)


def iota(shape, dim):
    return lax.broadcasted_iota(I32, shape, dim)


def onehot(hit):
    return jnp.where(hit, 1.0, 0.0).astype(BF)


def sixth(i):
    return (i * 43) >> 8


def regroup():
    a, i = iota((8, SLAB, GROUP), 0), iota((8, SLAB, GROUP), 1)
    b = sixth(i)
    return onehot(iota((8, SLAB, GROUP), 2) == b * SLAB + a * CAP + (i - CAP * b)).reshape(GROUP, GROUP)


def token_ranks(ids):
    member = jnp.where(ids == iota((EXPERTS, TOK), 0), 1.0, 0.0)
    earlier = onehot(iota((TOK, TOK), 0) < iota((TOK, TOK), 1))
    counts = jnp.dot(member.astype(BF), earlier, preferred_element_type=F32)
    return jnp.sum(member * counts, axis=0, keepdims=True).astype(I32)


def to_column(row):
    diagonal = iota((TOK, TOK), 0) == iota((TOK, TOK), 1)
    return jnp.sum(jnp.where(diagonal, row, 0.0), axis=1, keepdims=True)


def call(body, name, out_shape, operands, flops, scratch=(), specs=None, limit=VMEM_LIMIT):
    return pl.pallas_call(
        body,
        in_specs=specs or [VMEM] * len(operands),
        out_specs=[VMEM] * len(out_shape),
        out_shape=[jax.ShapeDtypeStruct(shape, kind) for shape, kind in out_shape],
        scratch_shapes=list(scratch),
        compiler_params=pltpu.CompilerParams(vmem_limit_bytes=limit),
        cost_estimate=pl.CostEstimate(flops=flops, bytes_accessed=4 * 10**6, transcendentals=0),
        name=name,
    )(*operands)


def dispatch_kernel(ids_hbm, p_hbm, x_hbm, g_hbm, out_ref, ids_ref, p_ref, x_ref, g_ref, sems):
    copies = [
        pltpu.make_async_copy(source, target, sems.at[i])
        for i, (source, target) in enumerate(((ids_hbm, ids_ref), (p_hbm, p_ref), (x_hbm, x_ref), (g_hbm, g_ref)))
    ]
    for copy in copies:
        copy.start()
    k, at = iota((EXPERTS, WIDE, 7 * TOK), 1), iota((EXPERTS, WIDE, 7 * TOK), 2)
    q = (k * 43) >> 9
    k = k - 12 * q
    order = q * TOK + iota((EXPERTS, WIDE, 7 * TOK), 0) * 16 + k + jnp.where(k >= CAP, 2, 0)
    order = onehot(at == order).reshape(EXPERTS * WIDE, 7 * TOK)
    for copy in copies:
        copy.wait()
    ids = ids_ref[...]
    slot = jnp.where(ids < EXPERTS, ids * 16 + token_ranks(ids), -16)
    at = iota((TOK, TOK), 0)
    sel = jnp.concatenate([onehot(slot == at), onehot(slot + 8 == at)], axis=1)
    scaled = (to_column(p_ref[...]) * g_ref[...].astype(F32)).astype(BF)
    both = jnp.concatenate([x_ref[...], scaled], axis=0)
    rows = jnp.dot(sel, both, preferred_element_type=F32).astype(BF)
    for i in range(2):
        stack = []
        for q in range(7):
            left = 2 * i * PART + q * TOK
            stack.append(jnp.concatenate([rows[:, left:left + TOK], rows[:, left + PART:left + PART + TOK]], axis=1))
        moved = jnp.dot(order, jnp.concatenate(stack, axis=0), preferred_element_type=F32).astype(BF)
        for j in range(2):
            one = moved[:, j * TOK:(j + 1) * TOK].reshape(EXPERTS, WIDE, TOK)
            out_ref[2 * i + j] = one


def before_kernel(mine_ref, other_ref, weight_ref, part_ref, g_ref, x_scr):
    zl = lax.axis_index("zl")
    shape = (7, 2, SLAB, WIDER)
    j = iota(shape, 2)
    source = sixth(j)
    place = source * WIDE + iota(shape, 0) * 12 + iota(shape, 1) * CAP + (j - CAP * source)
    pick = onehot(iota(shape, 3) == place).reshape(14 * SLAB, WIDER)
    for ref, z in ((mine_ref, zl), (other_ref, 1 - zl)):
        for i in range(2):
            both = jnp.concatenate([ref[2 * i], ref[2 * i + 1]], axis=1)
            moved = jnp.dot(pick, both, preferred_element_type=F32).astype(BF)
            for k in range(2):
                rows = pl.ds(pl.multiple_of((2 * (2 * i + k) + z) * SLAB, 16), SLAB)
                for q in range(7):
                    columns, lanes = slice(q * TOK, (q + 1) * TOK), slice(k * TOK, (k + 1) * TOK)
                    x_scr[rows, columns] = moved[2 * q * SLAB:(2 * q + 1) * SLAB, lanes]
                    g_ref[rows, columns] = moved[(2 * q + 1) * SLAB:(2 * q + 2) * SLAB, lanes]
    pre = jnp.dot(x_scr[...], weight_ref[:, :2 * HALF], preferred_element_type=F32).astype(BF)
    part_ref[:, :, :2 * HALF] = pre.reshape(4, ROWS, 2 * HALF)
    hid = jnp.dot(g_ref[...], weight_ref[:, 2 * HALF:], preferred_element_type=F32).astype(BF)
    part_ref[:, :, 2 * HALF:] = hid.reshape(4, ROWS, HALF)


def middle_kernel(part_ref, out_ref, line_ref):
    total = part_ref[0].astype(F32) + part_ref[1].astype(F32) + part_ref[2].astype(F32) + part_ref[3].astype(F32)
    gate, up, grad = total[:, :HALF], total[:, HALF:2 * HALF], total[:, 2 * HALF:]
    sig = jax.nn.sigmoid(gate)
    act = gate * sig
    slope = sig * (1.0 + gate * (1.0 - sig))
    hidden = (act * up).astype(BF)
    route = jnp.sum(hidden.astype(F32) * grad, axis=1, keepdims=True)
    d_gate, d_up = (grad * up * slope).astype(BF), (grad * act).astype(BF)
    for i in range(4):
        out_ref[i, :, :HALF] = d_gate
        out_ref[i, :, HALF:2 * HALF] = d_up
        out_ref[i, :, 2 * HALF:] = hidden
    line_ref[...] = jnp.where(iota((ROWS, TOK), 1) == 0, route, 0.0).astype(BF)


def after_kernel(mid_ref, line_ref, g_ref, weight_ref, keep_ref, give_ref,
                 far_ref, plus_ref, minus_ref, own_ref, send_ref, down, grads):
    xi, zi, ci, zl = [lax.axis_index(a) for a in ("x", "zh", "c", "zl")]
    mid = mid_ref[...].reshape(4 * ROWS, 3 * HALF)
    grads[...] = lax.dot_general(
        mid[:, :2 * HALF], weight_ref[:, :2 * HALF], (((1,), (1,)), ((), ())), preferred_element_type=F32
    ).astype(BF)
    for ref, z in ((keep_ref, zl), (give_ref, 1 - zl)):
        own = line_ref[pl.ds(pl.multiple_of(z * SLAB, 16), SLAB)]
        for i in range(4):
            ref[i, :, :PART] = grads[pl.ds(pl.multiple_of((2 * i + z) * SLAB, 16), SLAB)]
            ref[i, :, PART:] = jnp.where(xi == i, own, jnp.zeros_like(own))
    down[...] = lax.dot_general(
        g_ref[...], mid[:, 2 * HALF:], (((0,), (0,)), ((), ())), preferred_element_type=F32
    ).astype(BF)

    def shard(shift, core):
        block = 2 * lax.rem(zi + shift, 4) + core
        return down[pl.ds(pl.multiple_of(block * SHARD, 16), SHARD)]

    for i, (ref, shift) in enumerate(((far_ref, 2), (plus_ref, 1), (minus_ref, 3), (own_ref, 0))):
        ref[...] = shard(shift, ci)
        send_ref[i] = shard(shift, 1 - ci)


def combine_kernel(keep_ref, got_ref, out_ref):
    order = regroup()
    for i in range(2):
        left, right = add(keep_ref[2 * i], got_ref[2 * i]), add(keep_ref[2 * i + 1], got_ref[2 * i + 1])
        stack = []
        for q in range(8):
            columns = slice(q * TOK, (q + 1) * TOK)
            stack.append(jnp.concatenate([left[:, columns], right[:, columns]], axis=1))
        moved = jnp.dot(order, jnp.concatenate(stack, axis=0), preferred_element_type=F32).astype(BF)
        for j in range(2):
            out_ref[2 * i + j] = moved[:, j * TOK:(j + 1) * TOK].reshape(EXPERTS, SLAB, TOK)


def finish_kernel(ids_ref, p_ref, rows_ref, tok_ref, route_ref):
    ids = ids_ref[...]
    base = jnp.where(ids < EXPERTS, ids * SLAB + token_ranks(ids), -GROUP)
    offset = iota((TOK, GROUP), 1) - to_column(base.astype(F32)).astype(I32)
    pairs = [jnp.concatenate([rows_ref[2 * i], rows_ref[2 * i + 1]], axis=1) for i in range(2)]
    route = jnp.zeros((TOK, 1), F32)
    for q in range(8):
        sel = onehot(offset == q * CAP)
        for i in range(2):
            got = jnp.dot(sel, pairs[i], preferred_element_type=F32)
            if q == 7:
                route = route + got[:, :1] + got[:, TOK:TOK + 1]
                continue
            for j in range(2):
                left = (2 * i + j) * PART + q * TOK
                tok_ref[:, left:left + TOK] = got[:, j * TOK:(j + 1) * TOK].astype(BF)
    diagonal = iota((TOK, TOK), 0) == iota((TOK, TOK), 1)
    route_ref[...] = jnp.sum(jnp.where(diagonal, route, 0.0), axis=0, keepdims=True) / p_ref[...]


def hop(a, axis, shift):
    n = lax.axis_size(axis)
    return lax.ppermute(a, axis, [(i, (i + shift) % n) for i in range(n)])


def add(*terms):
    return sum(a.astype(F32) for a in terms).astype(BF)


def exchange(a, axes):
    return lax.all_to_all(a, axes, split_axis=0, concat_axis=0, tiled=True)


def per_device(tokens, grad_out, routing, route_weight, gate_weight, up_weight, down_weight):
    ids, share = routing.reshape(1, TOK), route_weight.reshape(1, TOK)
    weights = jnp.concatenate([gate_weight, up_weight, down_weight], axis=1)
    weights = lax.all_gather(weights, ("zh", "c"), axis=0, tiled=True)

    sent, = call(
        dispatch_kernel, "dispatch", [((4, EXPERTS, WIDE, TOK), BF)], (ids, share, tokens, grad_out), 10**9,
        [pltpu.VMEM((1, TOK), I32), pltpu.VMEM((1, TOK), F32), pltpu.VMEM((TOK, D), BF), pltpu.VMEM((TOK, D), BF),
         pltpu.SemaphoreType.DMA((4,))], [ANYWHERE] * 4, MOST_VMEM,
    )
    rows = exchange(sent.reshape(32, WIDE, TOK), PEERS).reshape(4, WIDER, TOK)
    dense = pltpu.VMEM((4 * ROWS, PART), BF)
    part, g_rows = call(
        before_kernel, "before", [((4, ROWS, 3 * HALF), BF), ((4 * ROWS, PART), BF)],
        (rows, hop(rows, "zl", 1), weights), 2 * 10**9, [dense],
    )
    mid, line = call(middle_kernel, "middle", [((4, ROWS, 3 * HALF), BF), ((ROWS, TOK), BF)],
                     (exchange(part, "x"),), 10**7)
    shard, wide = ((SHARD, HALF), BF), ((4, SLAB, PART + TOK), BF)
    keep, give, far, plus, minus, mine, send = call(
        after_kernel, "after", [wide, wide, shard, shard, shard, shard, ((4, SHARD, HALF), BF)],
        (exchange(mid, "x"), line, g_rows, weights), 14 * 10**8, [pltpu.VMEM((PART, HALF), BF), dense],
    )
    back, = call(combine_kernel, "combine", [((4, EXPERTS, SLAB, TOK), BF)], (keep, hop(give, "zl", 1)), 2 * 10**8)
    back = exchange(back.reshape(32, SLAB, TOK), PEERS).reshape(4, GROUP, TOK)
    token_grad, route_grad = call(finish_kernel, "finish", [((TOK, D), BF), ((1, TOK), F32)],
                                  (ids, share, back), 4 * 10**8)

    got = hop(send, "c", 1)
    far, plus, minus, mine = [add(a, got[i]) for i, a in enumerate((far, plus, minus, mine))]
    down_grad = add(hop(plus, "zh", 1), hop(minus, "zh", -1), hop(far, "zh", 2), mine)
    return token_grad, route_grad.reshape(TOK, 1), down_grad


def solution(mesh):
    inner = Mesh(mesh.devices.reshape(4, 4, 2, 8, 2), AXES)
    rows = P(AXES, None)
    weights = P(("x", "zh", "c"), ("y", "zl"))
    return jax.shard_map(
        per_device,
        mesh=inner,
        in_specs=(rows, rows, rows, rows, weights, weights, weights),
        out_specs=(rows, rows, weights),
        check_vma=False,
    )
```

```python
import jax
import jax.numpy as jnp
from jax import lax
from jax.experimental import pallas as pl
from jax.experimental.pallas import tpu as pltpu
from jax.sharding import Mesh, PartitionSpec as P

BF = jnp.bfloat16
F32 = jnp.float32
I32 = jnp.int32
AXES = ("x", "zh", "c", "y", "zl")
PEERS = ("x", "y")
TOK = 128
D = 3584
EXPERTS = 8
CAP = 6
HALF = 512
SHARD = 112
PART = D // 4
ROWS = 2 * EXPERTS * CAP
SLAB = 48
GROUP = 8 * SLAB
WIDE = 88
WIDER = 8 * WIDE
VMEM_LIMIT = 24 * 1024 * 1024
MOST_VMEM = 56 * 1024 * 1024
ANYWHERE = pl.BlockSpec(memory_space=pl.ANY)
VMEM = pl.BlockSpec(memory_space=pltpu.VMEM)


def iota(shape, dim):
    return lax.broadcasted_iota(I32, shape, dim)


def onehot(hit):
    return jnp.where(hit, 1.0, 0.0).astype(BF)


def sixth(i):
    return (i * 43) >> 8


def regroup():
    a, i = iota((8, SLAB, GROUP), 0), iota((8, SLAB, GROUP), 1)
    b = sixth(i)
    return onehot(iota((8, SLAB, GROUP), 2) == b * SLAB + a * CAP + (i - CAP * b)).reshape(GROUP, GROUP)


def token_ranks(ids):
    member = jnp.where(ids == iota((EXPERTS, TOK), 0), 1.0, 0.0)
    earlier = onehot(iota((TOK, TOK), 0) < iota((TOK, TOK), 1))
    counts = jnp.dot(member.astype(BF), earlier, preferred_element_type=F32)
    return jnp.sum(member * counts, axis=0, keepdims=True).astype(I32)


def to_column(row):
    diagonal = iota((TOK, TOK), 0) == iota((TOK, TOK), 1)
    return jnp.sum(jnp.where(diagonal, row, 0.0), axis=1, keepdims=True)


def call(body, name, out_shape, operands, flops, scratch=(), specs=None, limit=VMEM_LIMIT):
    return pl.pallas_call(
        body,
        in_specs=specs or [VMEM] * len(operands),
        out_specs=[VMEM] * len(out_shape),
        out_shape=[jax.ShapeDtypeStruct(shape, kind) for shape, kind in out_shape],
        scratch_shapes=list(scratch),
        compiler_params=pltpu.CompilerParams(vmem_limit_bytes=limit),
        cost_estimate=pl.CostEstimate(flops=flops, bytes_accessed=4 * 10**6, transcendentals=0),
        name=name,
    )(*operands)


def dispatch_kernel(ids_hbm, p_hbm, x_hbm, g_hbm, out_ref, ids_ref, p_ref, x_ref, g_ref, sems):
    copies = [
        pltpu.make_async_copy(source, target, sems.at[i])
        for i, (source, target) in enumerate(((ids_hbm, ids_ref), (p_hbm, p_ref), (x_hbm, x_ref), (g_hbm, g_ref)))
    ]
    for copy in copies:
        copy.start()
    k, at = iota((EXPERTS, WIDE, 7 * TOK), 1), iota((EXPERTS, WIDE, 7 * TOK), 2)
    q = (k * 43) >> 9
    k = k - 12 * q
    order = q * TOK + iota((EXPERTS, WIDE, 7 * TOK), 0) * 16 + k + jnp.where(k >= CAP, 2, 0)
    order = onehot(at == order).reshape(EXPERTS * WIDE, 7 * TOK)
    for copy in copies:
        copy.wait()
    ids = ids_ref[...]
    slot = jnp.where(ids < EXPERTS, ids * 16 + token_ranks(ids), -16)
    at = iota((TOK, TOK), 0)
    sel = jnp.concatenate([onehot(slot == at), onehot(slot + 8 == at)], axis=1)
    scaled = (to_column(p_ref[...]) * g_ref[...].astype(F32)).astype(BF)
    both = jnp.concatenate([x_ref[...], scaled], axis=0)
    rows = jnp.dot(sel, both, preferred_element_type=F32).astype(BF)
    for i in range(2):
        stack = []
        for q in range(7):
            left = 2 * i * PART + q * TOK
            stack.append(jnp.concatenate([rows[:, left:left + TOK], rows[:, left + PART:left + PART + TOK]], axis=1))
        moved = jnp.dot(order, jnp.concatenate(stack, axis=0), preferred_element_type=F32).astype(BF)
        for j in range(2):
            one = moved[:, j * TOK:(j + 1) * TOK].reshape(EXPERTS, WIDE, TOK)
            out_ref[2 * i + j] = one


def assemble_kernel(near_ref, near_other_ref, far_ref, far_other_ref, out_ref):
    zi, ci = lax.axis_index("zh"), lax.axis_index("c")
    for core, near, far in ((ci, near_ref, far_ref), (1 - ci, near_other_ref, far_other_ref)):
        for i, shift in enumerate((0, 3, 1, 2)):
            at = pl.multiple_of((2 * lax.rem(zi + shift, 4) + core) * SHARD, 16)
            out_ref[pl.ds(at, SHARD)] = far[...] if shift == 2 else near[i * SHARD:(i + 1) * SHARD]


def before_kernel(mine_ref, other_ref, weight_ref, part_ref, g_ref, x_scr):
    zl = lax.axis_index("zl")
    shape = (7, 2, SLAB, WIDER)
    j = iota(shape, 2)
    source = sixth(j)
    place = source * WIDE + iota(shape, 0) * 12 + iota(shape, 1) * CAP + (j - CAP * source)
    pick = onehot(iota(shape, 3) == place).reshape(14 * SLAB, WIDER)
    for ref, z in ((mine_ref, zl), (other_ref, 1 - zl)):
        for i in range(2):
            both = jnp.concatenate([ref[2 * i], ref[2 * i + 1]], axis=1)
            moved = jnp.dot(pick, both, preferred_element_type=F32).astype(BF)
            for k in range(2):
                rows = pl.ds(pl.multiple_of((2 * (2 * i + k) + z) * SLAB, 16), SLAB)
                for q in range(7):
                    columns, lanes = slice(q * TOK, (q + 1) * TOK), slice(k * TOK, (k + 1) * TOK)
                    x_scr[rows, columns] = moved[2 * q * SLAB:(2 * q + 1) * SLAB, lanes]
                    g_ref[rows, columns] = moved[(2 * q + 1) * SLAB:(2 * q + 2) * SLAB, lanes]
    pre = jnp.dot(x_scr[...], weight_ref[:, :2 * HALF], preferred_element_type=F32).astype(BF)
    part_ref[:, :, :2 * HALF] = pre.reshape(4, ROWS, 2 * HALF)
    hid = jnp.dot(g_ref[...], weight_ref[:, 2 * HALF:], preferred_element_type=F32).astype(BF)
    part_ref[:, :, 2 * HALF:] = hid.reshape(4, ROWS, HALF)


def middle_kernel(part_ref, out_ref, line_ref):
    total = part_ref[0].astype(F32) + part_ref[1].astype(F32) + part_ref[2].astype(F32) + part_ref[3].astype(F32)
    gate, up, grad = total[:, :HALF], total[:, HALF:2 * HALF], total[:, 2 * HALF:]
    sig = jax.nn.sigmoid(gate)
    act = gate * sig
    slope = sig * (1.0 + gate * (1.0 - sig))
    hidden = (act * up).astype(BF)
    route = jnp.sum(hidden.astype(F32) * grad, axis=1, keepdims=True)
    d_gate, d_up = (grad * up * slope).astype(BF), (grad * act).astype(BF)
    for i in range(4):
        out_ref[i, :, :HALF] = d_gate
        out_ref[i, :, HALF:2 * HALF] = d_up
        out_ref[i, :, 2 * HALF:] = hidden
    line_ref[...] = jnp.where(iota((ROWS, TOK), 1) == 0, route, 0.0).astype(BF)


def after_kernel(mid_ref, line_ref, g_ref, weight_ref, keep_ref, give_ref,
                 far_ref, plus_ref, minus_ref, own_ref, send_ref, down, grads):
    xi, zi, ci, zl = [lax.axis_index(a) for a in ("x", "zh", "c", "zl")]
    mid = mid_ref[...].reshape(4 * ROWS, 3 * HALF)
    grads[...] = lax.dot_general(
        mid[:, :2 * HALF], weight_ref[:, :2 * HALF], (((1,), (1,)), ((), ())), preferred_element_type=F32
    ).astype(BF)
    for ref, z in ((keep_ref, zl), (give_ref, 1 - zl)):
        own = line_ref[pl.ds(pl.multiple_of(z * SLAB, 16), SLAB)]
        for i in range(4):
            ref[i, :, :PART] = grads[pl.ds(pl.multiple_of((2 * i + z) * SLAB, 16), SLAB)]
            ref[i, :, PART:] = jnp.where(xi == i, own, jnp.zeros_like(own))
    down[...] = lax.dot_general(
        g_ref[...], mid[:, 2 * HALF:], (((0,), (0,)), ((), ())), preferred_element_type=F32
    ).astype(BF)

    def shard(shift, core):
        block = 2 * lax.rem(zi + shift, 4) + core
        return down[pl.ds(pl.multiple_of(block * SHARD, 16), SHARD)]

    for i, (ref, shift) in enumerate(((far_ref, 2), (plus_ref, 1), (minus_ref, 3), (own_ref, 0))):
        ref[...] = shard(shift, ci)
        send_ref[i] = shard(shift, 1 - ci)


def combine_kernel(keep_ref, got_ref, out_ref):
    order = regroup()
    for i in range(2):
        left, right = add(keep_ref[2 * i], got_ref[2 * i]), add(keep_ref[2 * i + 1], got_ref[2 * i + 1])
        stack = []
        for q in range(8):
            columns = slice(q * TOK, (q + 1) * TOK)
            stack.append(jnp.concatenate([left[:, columns], right[:, columns]], axis=1))
        moved = jnp.dot(order, jnp.concatenate(stack, axis=0), preferred_element_type=F32).astype(BF)
        for j in range(2):
            out_ref[2 * i + j] = moved[:, j * TOK:(j + 1) * TOK].reshape(EXPERTS, SLAB, TOK)


def finish_kernel(ids_ref, p_ref, rows_ref, tok_ref, route_ref):
    ids = ids_ref[...]
    base = jnp.where(ids < EXPERTS, ids * SLAB + token_ranks(ids), -GROUP)
    offset = iota((TOK, GROUP), 1) - to_column(base.astype(F32)).astype(I32)
    pairs = [jnp.concatenate([rows_ref[2 * i], rows_ref[2 * i + 1]], axis=1) for i in range(2)]
    route = jnp.zeros((TOK, 1), F32)
    for q in range(8):
        sel = onehot(offset == q * CAP)
        for i in range(2):
            got = jnp.dot(sel, pairs[i], preferred_element_type=F32)
            if q == 7:
                route = route + got[:, :1] + got[:, TOK:TOK + 1]
                continue
            for j in range(2):
                left = (2 * i + j) * PART + q * TOK
                tok_ref[:, left:left + TOK] = got[:, j * TOK:(j + 1) * TOK].astype(BF)
    diagonal = iota((TOK, TOK), 0) == iota((TOK, TOK), 1)
    route_ref[...] = jnp.sum(jnp.where(diagonal, route, 0.0), axis=0, keepdims=True) / p_ref[...]


def hop(a, axis, shift):
    n = lax.axis_size(axis)
    return lax.ppermute(a, axis, [(i, (i + shift) % n) for i in range(n)])


def add(*terms):
    return sum(a.astype(F32) for a in terms).astype(BF)


def exchange(a, axes):
    return lax.all_to_all(a, axes, split_axis=0, concat_axis=0, tiled=True)


def per_device(tokens, grad_out, routing, route_weight, gate_weight, up_weight, down_weight):
    ids, share = routing.reshape(1, TOK), route_weight.reshape(1, TOK)
    sent, = call(
        dispatch_kernel, "dispatch", [((4, EXPERTS, WIDE, TOK), BF)], (ids, share, tokens, grad_out), 10**9,
        [pltpu.VMEM((1, TOK), I32), pltpu.VMEM((1, TOK), F32), pltpu.VMEM((TOK, D), BF), pltpu.VMEM((TOK, D), BF),
         pltpu.SemaphoreType.DMA((4,))], [ANYWHERE] * 4, MOST_VMEM,
    )
    gate_weight, sent = lax.optimization_barrier((gate_weight, sent))
    rows = exchange(sent.reshape(32, WIDE, TOK), PEERS).reshape(4, WIDER, TOK)

    cut = SHARD // 2
    weights = jnp.concatenate([gate_weight, up_weight, down_weight], axis=1)
    z_before, z_after = hop(weights, "zh", 1), hop(weights, "zh", -1)
    z_low, z_high = hop(z_before[:cut], "zh", 1), hop(z_after[cut:], "zh", -1)
    near = jnp.concatenate([weights, z_before, z_after], axis=0)
    far = jnp.concatenate([z_low, z_high], axis=0)
    weights, = call(assemble_kernel, "assemble", [((PART, 3 * HALF), BF)],
                    (near, hop(near, "c", 1), far, hop(far, "c", 1)), 10**6)

    dense = pltpu.VMEM((4 * ROWS, PART), BF)
    part, g_rows = call(
        before_kernel, "before", [((4, ROWS, 3 * HALF), BF), ((4 * ROWS, PART), BF)],
        (rows, hop(rows, "zl", 1), weights), 2 * 10**9, [dense],
    )
    mid, line = call(middle_kernel, "middle", [((4, ROWS, 3 * HALF), BF), ((ROWS, TOK), BF)],
                     (exchange(part, "x"),), 10**7)
    shard, wide = ((SHARD, HALF), BF), ((4, SLAB, PART + TOK), BF)
    keep, give, far, plus, minus, mine, send = call(
        after_kernel, "after", [wide, wide, shard, shard, shard, shard, ((4, SHARD, HALF), BF)],
        (exchange(mid, "x"), line, g_rows, weights), 14 * 10**8, [pltpu.VMEM((PART, HALF), BF), dense],
    )
    back, = call(combine_kernel, "combine", [((4, EXPERTS, SLAB, TOK), BF)], (keep, hop(give, "zl", 1)), 2 * 10**8)
    back = exchange(back.reshape(32, SLAB, TOK), PEERS).reshape(4, GROUP, TOK)
    token_grad, route_grad = call(finish_kernel, "finish", [((TOK, D), BF), ((1, TOK), F32)],
                                  (ids, share, back), 4 * 10**8)

    got = hop(send, "c", 1)
    far, plus, minus, mine = [add(a, got[i]) for i, a in enumerate((far, plus, minus, mine))]
    down_grad = add(hop(plus, "zh", 1), hop(minus, "zh", -1), hop(far, "zh", 2), mine)
    return token_grad, route_grad.reshape(TOK, 1), down_grad


def solution(mesh):
    inner = Mesh(mesh.devices.reshape(4, 4, 2, 8, 2), AXES)
    rows = P(AXES, None)
    weights = P(("x", "zh", "c"), ("y", "zl"))
    return jax.shard_map(
        per_device,
        mesh=inner,
        in_specs=(rows, rows, rows, rows, weights, weights, weights),
        out_specs=(rows, rows, weights),
        check_vma=False,
    )
```

```python
import jax
import jax.numpy as jnp
from jax import lax
from jax.experimental import pallas as pl
from jax.experimental.pallas import tpu as pltpu
from jax.sharding import Mesh, PartitionSpec as P

BF = jnp.bfloat16
F32 = jnp.float32
I32 = jnp.int32
AXES = ("x", "zh", "c", "y", "zl")
PEERS = ("x", "y")
TOK = 128
D = 3584
EXPERTS = 8
CAP = 6
HALF = 512
SHARD = 112
PART = D // 4
ROWS = 2 * EXPERTS * CAP
SLAB = 48
GROUP = 8 * SLAB
WIDE = 88
WIDER = 8 * WIDE
VMEM_LIMIT = 24 * 1024 * 1024
MOST_VMEM = 56 * 1024 * 1024
ANYWHERE = pl.BlockSpec(memory_space=pl.ANY)
VMEM = pl.BlockSpec(memory_space=pltpu.VMEM)


def iota(shape, dim):
    return lax.broadcasted_iota(I32, shape, dim)


def onehot(hit):
    return jnp.where(hit, 1.0, 0.0).astype(BF)


def sixth(i):
    return (i * 43) >> 8


def regroup():
    a, i = iota((8, SLAB, GROUP), 0), iota((8, SLAB, GROUP), 1)
    b = sixth(i)
    return onehot(iota((8, SLAB, GROUP), 2) == b * SLAB + a * CAP + (i - CAP * b)).reshape(GROUP, GROUP)


def token_ranks(ids):
    member = jnp.where(ids == iota((EXPERTS, TOK), 0), 1.0, 0.0)
    earlier = onehot(iota((TOK, TOK), 0) < iota((TOK, TOK), 1))
    counts = jnp.dot(member.astype(BF), earlier, preferred_element_type=F32)
    return jnp.sum(member * counts, axis=0, keepdims=True).astype(I32)


def to_column(row):
    diagonal = iota((TOK, TOK), 0) == iota((TOK, TOK), 1)
    return jnp.sum(jnp.where(diagonal, row, 0.0), axis=1, keepdims=True)


def call(body, name, out_shape, operands, flops, scratch=(), specs=None, limit=VMEM_LIMIT):
    return pl.pallas_call(
        body,
        in_specs=specs or [VMEM] * len(operands),
        out_specs=[VMEM] * len(out_shape),
        out_shape=[jax.ShapeDtypeStruct(shape, kind) for shape, kind in out_shape],
        scratch_shapes=list(scratch),
        compiler_params=pltpu.CompilerParams(vmem_limit_bytes=limit),
        cost_estimate=pl.CostEstimate(flops=flops, bytes_accessed=4 * 10**6, transcendentals=0),
        name=name,
    )(*operands)


def dispatch_kernel(ids_hbm, p_hbm, x_hbm, g_hbm, out_ref, ids_ref, p_ref, x_ref, g_ref, sems):
    copies = [
        pltpu.make_async_copy(source, target, sems.at[i])
        for i, (source, target) in enumerate(((ids_hbm, ids_ref), (p_hbm, p_ref), (x_hbm, x_ref), (g_hbm, g_ref)))
    ]
    for copy in copies:
        copy.start()
    k, at = iota((EXPERTS, WIDE, 7 * TOK), 1), iota((EXPERTS, WIDE, 7 * TOK), 2)
    q = (k * 43) >> 9
    k = k - 12 * q
    order = q * TOK + iota((EXPERTS, WIDE, 7 * TOK), 0) * 16 + k + jnp.where(k >= CAP, 2, 0)
    order = onehot(at == order).reshape(EXPERTS * WIDE, 7 * TOK)
    for copy in copies:
        copy.wait()
    ids = ids_ref[...]
    slot = jnp.where(ids < EXPERTS, ids * 16 + token_ranks(ids), -16)
    at = iota((TOK, TOK), 0)
    sel = jnp.concatenate([onehot(slot == at), onehot(slot + 8 == at)], axis=1)
    scaled = (to_column(p_ref[...]) * g_ref[...].astype(F32)).astype(BF)
    both = jnp.concatenate([x_ref[...], scaled], axis=0)
    rows = jnp.dot(sel, both, preferred_element_type=F32).astype(BF)
    for i in range(2):
        stack = []
        for q in range(7):
            left = 2 * i * PART + q * TOK
            stack.append(jnp.concatenate([rows[:, left:left + TOK], rows[:, left + PART:left + PART + TOK]], axis=1))
        moved = jnp.dot(order, jnp.concatenate(stack, axis=0), preferred_element_type=F32).astype(BF)
        for j in range(2):
            one = moved[:, j * TOK:(j + 1) * TOK].reshape(EXPERTS, WIDE, TOK)
            out_ref[2 * i + j] = one


def assemble_kernel(near_ref, near_other_ref, far_ref, far_other_ref, out_ref):
    zi, ci = lax.axis_index("zh"), lax.axis_index("c")
    for core, near, far in ((ci, near_ref, far_ref), (1 - ci, near_other_ref, far_other_ref)):
        for i, shift in enumerate((0, 3, 1, 2)):
            at = pl.multiple_of((2 * lax.rem(zi + shift, 4) + core) * SHARD, 16)
            out_ref[pl.ds(at, SHARD)] = far[...] if shift == 2 else near[i * SHARD:(i + 1) * SHARD]


def before_kernel(mine_ref, other_ref, weight_ref, part_ref, g_ref, x_scr):
    zl = lax.axis_index("zl")
    shape = (7, 2, SLAB, WIDER)
    j = iota(shape, 2)
    source = sixth(j)
    place = source * WIDE + iota(shape, 0) * 12 + iota(shape, 1) * CAP + (j - CAP * source)
    pick = onehot(iota(shape, 3) == place).reshape(14 * SLAB, WIDER)
    for ref, z in ((mine_ref, zl), (other_ref, 1 - zl)):
        for i in range(2):
            both = jnp.concatenate([ref[2 * i], ref[2 * i + 1]], axis=1)
            moved = jnp.dot(pick, both, preferred_element_type=F32).astype(BF)
            for k in range(2):
                rows = pl.ds(pl.multiple_of((2 * (2 * i + k) + z) * SLAB, 16), SLAB)
                for q in range(7):
                    columns, lanes = slice(q * TOK, (q + 1) * TOK), slice(k * TOK, (k + 1) * TOK)
                    x_scr[rows, columns] = moved[2 * q * SLAB:(2 * q + 1) * SLAB, lanes]
                    g_ref[rows, columns] = moved[(2 * q + 1) * SLAB:(2 * q + 2) * SLAB, lanes]
    pre = jnp.dot(x_scr[...], weight_ref[:, :2 * HALF], preferred_element_type=F32).astype(BF)
    part_ref[:, :, :2 * HALF] = pre.reshape(4, ROWS, 2 * HALF)
    hid = jnp.dot(g_ref[...], weight_ref[:, 2 * HALF:], preferred_element_type=F32).astype(BF)
    part_ref[:, :, 2 * HALF:] = hid.reshape(4, ROWS, HALF)


def middle_kernel(part_ref, out_ref, line_ref):
    total = part_ref[0].astype(F32) + part_ref[1].astype(F32) + part_ref[2].astype(F32) + part_ref[3].astype(F32)
    gate, up, grad = total[:, :HALF], total[:, HALF:2 * HALF], total[:, 2 * HALF:]
    sig = jax.nn.sigmoid(gate)
    act = gate * sig
    slope = sig * (1.0 + gate * (1.0 - sig))
    hidden = (act * up).astype(BF)
    route = jnp.sum(hidden.astype(F32) * grad, axis=1, keepdims=True)
    d_gate, d_up = (grad * up * slope).astype(BF), (grad * act).astype(BF)
    for i in range(4):
        out_ref[i, :, :HALF] = d_gate
        out_ref[i, :, HALF:2 * HALF] = d_up
        out_ref[i, :, 2 * HALF:] = hidden
    line_ref[...] = jnp.where(iota((ROWS, TOK), 1) == 0, route, 0.0).astype(BF)


def after_kernel(mid_ref, line_ref, g_ref, weight_ref, keep_ref, give_ref,
                 far_ref, plus_ref, minus_ref, own_ref, send_ref, down, grads):
    xi, zi, ci, zl = [lax.axis_index(a) for a in ("x", "zh", "c", "zl")]
    mid = mid_ref[...].reshape(4 * ROWS, 3 * HALF)
    grads[...] = lax.dot_general(
        mid[:, :2 * HALF], weight_ref[:, :2 * HALF], (((1,), (1,)), ((), ())), preferred_element_type=F32
    ).astype(BF)
    for ref, z in ((keep_ref, zl), (give_ref, 1 - zl)):
        own = line_ref[pl.ds(pl.multiple_of(z * SLAB, 16), SLAB)]
        for i in range(4):
            ref[i, :, :PART] = grads[pl.ds(pl.multiple_of((2 * i + z) * SLAB, 16), SLAB)]
            ref[i, :, PART:] = jnp.where(xi == i, own, jnp.zeros_like(own))
    down[...] = lax.dot_general(
        g_ref[...], mid[:, 2 * HALF:], (((0,), (0,)), ((), ())), preferred_element_type=F32
    ).astype(BF)

    def shard(shift, core):
        block = 2 * lax.rem(zi + shift, 4) + core
        return down[pl.ds(pl.multiple_of(block * SHARD, 16), SHARD)]

    for i, (ref, shift) in enumerate(((far_ref, 2), (plus_ref, 1), (minus_ref, 3), (own_ref, 0))):
        ref[...] = shard(shift, ci)
        send_ref[i] = shard(shift, 1 - ci)


def combine_kernel(keep_ref, got_ref, out_ref):
    order = regroup()
    for i in range(2):
        left, right = add(keep_ref[2 * i], got_ref[2 * i]), add(keep_ref[2 * i + 1], got_ref[2 * i + 1])
        stack = []
        for q in range(8):
            columns = slice(q * TOK, (q + 1) * TOK)
            stack.append(jnp.concatenate([left[:, columns], right[:, columns]], axis=1))
        moved = jnp.dot(order, jnp.concatenate(stack, axis=0), preferred_element_type=F32).astype(BF)
        for j in range(2):
            out_ref[2 * i + j] = moved[:, j * TOK:(j + 1) * TOK].reshape(EXPERTS, SLAB, TOK)


def finish_kernel(ids_ref, p_ref, rows_ref, tok_ref, route_ref):
    ids = ids_ref[...]
    base = jnp.where(ids < EXPERTS, ids * SLAB + token_ranks(ids), -GROUP)
    offset = iota((TOK, GROUP), 1) - to_column(base.astype(F32)).astype(I32)
    pairs = [jnp.concatenate([rows_ref[2 * i], rows_ref[2 * i + 1]], axis=1) for i in range(2)]
    route = jnp.zeros((TOK, 1), F32)
    for q in range(8):
        sel = onehot(offset == q * CAP)
        for i in range(2):
            got = jnp.dot(sel, pairs[i], preferred_element_type=F32)
            if q == 7:
                route = route + got[:, :1] + got[:, TOK:TOK + 1]
                continue
            for j in range(2):
                left = (2 * i + j) * PART + q * TOK
                tok_ref[:, left:left + TOK] = got[:, j * TOK:(j + 1) * TOK].astype(BF)
    diagonal = iota((TOK, TOK), 0) == iota((TOK, TOK), 1)
    route_ref[...] = jnp.sum(jnp.where(diagonal, route, 0.0), axis=0, keepdims=True) / p_ref[...]


def hop(a, axis, shift):
    n = lax.axis_size(axis)
    return lax.ppermute(a, axis, [(i, (i + shift) % n) for i in range(n)])


def add(*terms):
    return sum(a.astype(F32) for a in terms).astype(BF)


def exchange(a, axes):
    return lax.all_to_all(a, axes, split_axis=0, concat_axis=0, tiled=True)


def per_device(tokens, grad_out, routing, route_weight, gate_weight, up_weight, down_weight):
    ids, share = routing.reshape(1, TOK), route_weight.reshape(1, TOK)
    sent, = call(
        dispatch_kernel, "dispatch", [((4, EXPERTS, WIDE, TOK), BF)], (ids, share, tokens, grad_out), 10**9,
        [pltpu.VMEM((1, TOK), I32), pltpu.VMEM((1, TOK), F32), pltpu.VMEM((TOK, D), BF), pltpu.VMEM((TOK, D), BF),
         pltpu.SemaphoreType.DMA((4,))], [ANYWHERE] * 4, MOST_VMEM,
    )
    rows = exchange(sent.reshape(32, WIDE, TOK), PEERS).reshape(4, WIDER, TOK)

    cut = SHARD // 2
    weights = jnp.concatenate([gate_weight, up_weight, down_weight], axis=1)
    z_before, z_after = hop(weights, "zh", 1), hop(weights, "zh", -1)
    z_low, z_high = hop(z_before[:cut], "zh", 1), hop(z_after[cut:], "zh", -1)
    near = jnp.concatenate([weights, z_before, z_after], axis=0)
    far = jnp.concatenate([z_low, z_high], axis=0)
    weights, = call(assemble_kernel, "assemble", [((PART, 3 * HALF), BF)],
                    (near, hop(near, "c", 1), far, hop(far, "c", 1)), 2 * 10**10)

    dense = pltpu.VMEM((4 * ROWS, PART), BF)
    part, g_rows = call(
        before_kernel, "before", [((4, ROWS, 3 * HALF), BF), ((4 * ROWS, PART), BF)],
        (rows, hop(rows, "zl", 1), weights), 2 * 10**9, [dense],
    )
    mid, line = call(middle_kernel, "middle", [((4, ROWS, 3 * HALF), BF), ((ROWS, TOK), BF)],
                     (exchange(part, "x"),), 10**7)
    shard, wide = ((SHARD, HALF), BF), ((4, SLAB, PART + TOK), BF)
    keep, give, far, plus, minus, mine, send = call(
        after_kernel, "after", [wide, wide, shard, shard, shard, shard, ((4, SHARD, HALF), BF)],
        (exchange(mid, "x"), line, g_rows, weights), 14 * 10**8, [pltpu.VMEM((PART, HALF), BF), dense],
    )
    back, = call(combine_kernel, "combine", [((4, EXPERTS, SLAB, TOK), BF)], (keep, hop(give, "zl", 1)), 2 * 10**8)
    back = exchange(back.reshape(32, SLAB, TOK), PEERS).reshape(4, GROUP, TOK)
    token_grad, route_grad = call(finish_kernel, "finish", [((TOK, D), BF), ((1, TOK), F32)],
                                  (ids, share, back), 4 * 10**8)

    got = hop(send, "c", 1)
    far, plus, minus, mine = [add(a, got[i]) for i, a in enumerate((far, plus, minus, mine))]
    down_grad = add(hop(plus, "zh", 1), hop(minus, "zh", -1), hop(far, "zh", 2), mine)
    return token_grad, route_grad.reshape(TOK, 1), down_grad


def solution(mesh):
    inner = Mesh(mesh.devices.reshape(4, 4, 2, 8, 2), AXES)
    rows = P(AXES, None)
    weights = P(("x", "zh", "c"), ("y", "zl"))
    return jax.shard_map(
        per_device,
        mesh=inner,
        in_specs=(rows, rows, rows, rows, weights, weights, weights),
        out_specs=(rows, rows, weights),
        check_vma=False,
    )
```

```python
import jax
import jax.numpy as jnp
from jax import lax
from jax.experimental import pallas as pl
from jax.experimental.pallas import tpu as pltpu
from jax.sharding import Mesh, PartitionSpec as P

BF = jnp.bfloat16
F32 = jnp.float32
I32 = jnp.int32
AXES = ("x", "zh", "c", "y", "zl")
PEERS = ("x", "y")
TOK = 128
D = 3584
EXPERTS = 8
CAP = 6
HALF = 512
SHARD = 112
PART = D // 4
ROWS = 2 * EXPERTS * CAP
SLAB = 48
GROUP = 8 * SLAB
WIDE = 88
WIDER = 8 * WIDE
VMEM_LIMIT = 24 * 1024 * 1024
MOST_VMEM = 56 * 1024 * 1024
ANYWHERE = pl.BlockSpec(memory_space=pl.ANY)
VMEM = pl.BlockSpec(memory_space=pltpu.VMEM)


def iota(shape, dim):
    return lax.broadcasted_iota(I32, shape, dim)


def onehot(hit):
    return jnp.where(hit, 1.0, 0.0).astype(BF)


def sixth(i):
    return (i * 43) >> 8


def regroup():
    a, i = iota((8, SLAB, GROUP), 0), iota((8, SLAB, GROUP), 1)
    b = sixth(i)
    return onehot(iota((8, SLAB, GROUP), 2) == b * SLAB + a * CAP + (i - CAP * b)).reshape(GROUP, GROUP)


def token_ranks(ids):
    member = jnp.where(ids == iota((EXPERTS, TOK), 0), 1.0, 0.0)
    earlier = onehot(iota((TOK, TOK), 0) < iota((TOK, TOK), 1))
    counts = jnp.dot(member.astype(BF), earlier, preferred_element_type=F32)
    return jnp.sum(member * counts, axis=0, keepdims=True).astype(I32)


def to_column(row):
    diagonal = iota((TOK, TOK), 0) == iota((TOK, TOK), 1)
    return jnp.sum(jnp.where(diagonal, row, 0.0), axis=1, keepdims=True)


def call(body, name, out_shape, operands, flops, scratch=(), specs=None, limit=VMEM_LIMIT):
    return pl.pallas_call(
        body,
        in_specs=specs or [VMEM] * len(operands),
        out_specs=[VMEM] * len(out_shape),
        out_shape=[jax.ShapeDtypeStruct(shape, kind) for shape, kind in out_shape],
        scratch_shapes=list(scratch),
        compiler_params=pltpu.CompilerParams(vmem_limit_bytes=limit),
        cost_estimate=pl.CostEstimate(flops=flops, bytes_accessed=4 * 10**6, transcendentals=0),
        name=name,
    )(*operands)


def dispatch_kernel(ids_hbm, p_hbm, x_hbm, g_hbm, out_ref, ids_ref, p_ref, x_ref, g_ref, sems):
    copies = [
        pltpu.make_async_copy(source, target, sems.at[i])
        for i, (source, target) in enumerate(((ids_hbm, ids_ref), (p_hbm, p_ref), (x_hbm, x_ref), (g_hbm, g_ref)))
    ]
    for copy in copies:
        copy.start()
    k, at = iota((EXPERTS, WIDE, 7 * TOK), 1), iota((EXPERTS, WIDE, 7 * TOK), 2)
    q = (k * 43) >> 9
    k = k - 12 * q
    order = q * TOK + iota((EXPERTS, WIDE, 7 * TOK), 0) * 16 + k + jnp.where(k >= CAP, 2, 0)
    order = onehot(at == order).reshape(EXPERTS * WIDE, 7 * TOK)
    for copy in copies:
        copy.wait()
    ids = ids_ref[...]
    slot = jnp.where(ids < EXPERTS, ids * 16 + token_ranks(ids), -16)
    at = iota((TOK, TOK), 0)
    sel = jnp.concatenate([onehot(slot == at), onehot(slot + 8 == at)], axis=1)
    scaled = (to_column(p_ref[...]) * g_ref[...].astype(F32)).astype(BF)
    both = jnp.concatenate([x_ref[...], scaled], axis=0)
    rows = jnp.dot(sel, both, preferred_element_type=F32).astype(BF)
    for i in range(2):
        stack = []
        for q in range(7):
            left = 2 * i * PART + q * TOK
            stack.append(jnp.concatenate([rows[:, left:left + TOK], rows[:, left + PART:left + PART + TOK]], axis=1))
        moved = jnp.dot(order, jnp.concatenate(stack, axis=0), preferred_element_type=F32).astype(BF)
        for j in range(2):
            one = moved[:, j * TOK:(j + 1) * TOK].reshape(EXPERTS, WIDE, TOK)
            out_ref[2 * i + j] = one


def stack_kernel(a_ref, b_ref, c_ref, out_ref):
    for i, ref in enumerate((a_ref, b_ref, c_ref)):
        out_ref[:, i * HALF:(i + 1) * HALF] = ref[...]


def near_kernel(own_ref, before_ref, after_ref, out_ref, before_out):
    for i, ref in enumerate((own_ref, before_ref, after_ref)):
        out_ref[i * SHARD:(i + 1) * SHARD] = ref[...]
    before_out[...] = before_ref[...]


def assemble_kernel(near_ref, near_other_ref, far_ref, far_other_ref, out_ref, pick_ref):
    shape = (7, 2, SLAB, WIDER)
    j = iota(shape, 2)
    source = sixth(j)
    place = source * WIDE + iota(shape, 0) * 12 + iota(shape, 1) * CAP + (j - CAP * source)
    pick_ref[...] = onehot(iota(shape, 3) == place).reshape(14 * SLAB, WIDER)
    zi, ci = lax.axis_index("zh"), lax.axis_index("c")
    for core, near, far in ((ci, near_ref, far_ref), (1 - ci, near_other_ref, far_other_ref)):
        for i, shift in enumerate((0, 3, 1, 2)):
            block = lax.rem(zi + jnp.where(core == 0, shift, 4 - shift), 4)
            at = pl.multiple_of((2 * block + core) * SHARD, 16)
            out_ref[pl.ds(at, SHARD)] = far[...] if shift == 2 else near[i * SHARD:(i + 1) * SHARD]


def before_kernel(mine_ref, other_ref, weight_ref, pick_ref, part_ref, g_ref, x_scr):
    zl = lax.axis_index("zl")
    for ref, z in ((mine_ref, zl), (other_ref, 1 - zl)):
        for i in range(2):
            both = jnp.concatenate([ref[2 * i], ref[2 * i + 1]], axis=1)
            moved = jnp.dot(pick_ref[...], both, preferred_element_type=F32).astype(BF)
            for k in range(2):
                rows = pl.ds(pl.multiple_of((2 * (2 * i + k) + z) * SLAB, 16), SLAB)
                for q in range(7):
                    columns, lanes = slice(q * TOK, (q + 1) * TOK), slice(k * TOK, (k + 1) * TOK)
                    x_scr[rows, columns] = moved[2 * q * SLAB:(2 * q + 1) * SLAB, lanes]
                    g_ref[rows, columns] = moved[(2 * q + 1) * SLAB:(2 * q + 2) * SLAB, lanes]
    pre = jnp.dot(x_scr[...], weight_ref[:, :2 * HALF], preferred_element_type=F32).astype(BF)
    part_ref[:, :, :2 * HALF] = pre.reshape(4, ROWS, 2 * HALF)
    hid = jnp.dot(g_ref[...], weight_ref[:, 2 * HALF:], preferred_element_type=F32).astype(BF)
    part_ref[:, :, 2 * HALF:] = hid.reshape(4, ROWS, HALF)


def middle_kernel(part_ref, out_ref, line_ref):
    total = part_ref[0].astype(F32) + part_ref[1].astype(F32) + part_ref[2].astype(F32) + part_ref[3].astype(F32)
    gate, up, grad = total[:, :HALF], total[:, HALF:2 * HALF], total[:, 2 * HALF:]
    sig = jax.nn.sigmoid(gate)
    act = gate * sig
    slope = sig * (1.0 + gate * (1.0 - sig))
    hidden = (act * up).astype(BF)
    route = jnp.sum(hidden.astype(F32) * grad, axis=1, keepdims=True)
    d_gate, d_up = (grad * up * slope).astype(BF), (grad * act).astype(BF)
    for i in range(4):
        out_ref[i, :, :HALF] = d_gate
        out_ref[i, :, HALF:2 * HALF] = d_up
        out_ref[i, :, 2 * HALF:] = hidden
    line_ref[...] = jnp.where(iota((ROWS, TOK), 1) == 0, route, 0.0).astype(BF)


def after_kernel(mid_ref, line_ref, g_ref, weight_ref, keep_ref, give_ref,
                 far_ref, plus_ref, minus_ref, own_ref, send_ref, down, grads):
    xi, zi, ci, zl = [lax.axis_index(a) for a in ("x", "zh", "c", "zl")]
    mid = mid_ref[...].reshape(4 * ROWS, 3 * HALF)
    grads[...] = lax.dot_general(
        mid[:, :2 * HALF], weight_ref[:, :2 * HALF], (((1,), (1,)), ((), ())), preferred_element_type=F32
    ).astype(BF)
    for ref, z in ((keep_ref, zl), (give_ref, 1 - zl)):
        own = line_ref[pl.ds(pl.multiple_of(z * SLAB, 16), SLAB)]
        for i in range(4):
            ref[i, :, :PART] = grads[pl.ds(pl.multiple_of((2 * i + z) * SLAB, 16), SLAB)]
            ref[i, :, PART:] = jnp.where(xi == i, own, jnp.zeros_like(own))
    down[...] = lax.dot_general(
        g_ref[...], mid[:, 2 * HALF:], (((0,), (0,)), ((), ())), preferred_element_type=F32
    ).astype(BF)

    def shard(shift, core):
        block = 2 * lax.rem(zi + shift, 4) + core
        return down[pl.ds(pl.multiple_of(block * SHARD, 16), SHARD)]

    for i, (ref, shift) in enumerate(((far_ref, 2), (plus_ref, 1), (minus_ref, 3), (own_ref, 0))):
        ref[...] = shard(shift, ci)
        send_ref[i] = shard(shift, 1 - ci)


def combine_kernel(keep_ref, got_ref, out_ref):
    order = regroup()
    for i in range(2):
        left, right = add(keep_ref[2 * i], got_ref[2 * i]), add(keep_ref[2 * i + 1], got_ref[2 * i + 1])
        stack = []
        for q in range(8):
            columns = slice(q * TOK, (q + 1) * TOK)
            stack.append(jnp.concatenate([left[:, columns], right[:, columns]], axis=1))
        moved = jnp.dot(order, jnp.concatenate(stack, axis=0), preferred_element_type=F32).astype(BF)
        for j in range(2):
            out_ref[2 * i + j] = moved[:, j * TOK:(j + 1) * TOK].reshape(EXPERTS, SLAB, TOK)


def finish_kernel(ids_ref, p_ref, rows_ref, tok_ref, route_ref):
    ids = ids_ref[...]
    base = jnp.where(ids < EXPERTS, ids * SLAB + token_ranks(ids), -GROUP)
    offset = iota((TOK, GROUP), 1) - to_column(base.astype(F32)).astype(I32)
    pairs = [jnp.concatenate([rows_ref[2 * i], rows_ref[2 * i + 1]], axis=1) for i in range(2)]
    route = jnp.zeros((TOK, 1), F32)
    for q in range(8):
        sel = onehot(offset == q * CAP)
        for i in range(2):
            got = jnp.dot(sel, pairs[i], preferred_element_type=F32)
            if q == 7:
                route = route + got[:, :1] + got[:, TOK:TOK + 1]
                continue
            for j in range(2):
                left = (2 * i + j) * PART + q * TOK
                tok_ref[:, left:left + TOK] = got[:, j * TOK:(j + 1) * TOK].astype(BF)
    diagonal = iota((TOK, TOK), 0) == iota((TOK, TOK), 1)
    route_ref[...] = jnp.sum(jnp.where(diagonal, route, 0.0), axis=0, keepdims=True) / p_ref[...]


def hop(a, axis, shift):
    n = lax.axis_size(axis)
    return lax.ppermute(a, axis, [(i, (i + shift) % n) for i in range(n)])


def turn(a, axis, shift):
    n = lax.axis_size(axis)
    pairs = []
    for i in range(n):
        pairs += [(2 * i, 2 * ((i + shift) % n)), (2 * i + 1, 2 * ((i - shift) % n) + 1)]
    return lax.ppermute(a, (axis, "c"), pairs)


def add(*terms):
    return sum(a.astype(F32) for a in terms).astype(BF)


def exchange(a, axes):
    return lax.all_to_all(a, axes, split_axis=0, concat_axis=0, tiled=True)


def per_device(tokens, grad_out, routing, route_weight, gate_weight, up_weight, down_weight):
    ids, share = routing.reshape(1, TOK), route_weight.reshape(1, TOK)
    weights, = call(stack_kernel, "stack", [((SHARD, 3 * HALF), BF)], (gate_weight, up_weight, down_weight), 10**6)
    sent, = call(
        dispatch_kernel, "dispatch", [((4, EXPERTS, WIDE, TOK), BF)], (ids, share, tokens, grad_out), 10**9,
        [pltpu.VMEM((1, TOK), I32), pltpu.VMEM((1, TOK), F32), pltpu.VMEM((TOK, D), BF), pltpu.VMEM((TOK, D), BF),
         pltpu.SemaphoreType.DMA((4,))], [ANYWHERE] * 4, MOST_VMEM,
    )
    rows = exchange(sent.reshape(32, WIDE, TOK), PEERS).reshape(4, WIDER, TOK)

    z_before, z_after = turn(weights, "zh", 1), turn(weights, "zh", -1)
    near, passed = call(near_kernel, "near", [((3 * SHARD, 3 * HALF), BF), ((SHARD, 3 * HALF), BF)],
                        (weights, z_before, z_after), 4 * 10**9)
    far = turn(passed, "zh", 1)
    rows_other = hop(rows, "zl", 1)
    weights, pick = call(assemble_kernel, "assemble", [((PART, 3 * HALF), BF), ((14 * SLAB, WIDER), BF)],
                    (near, hop(near, "c", 1), far, hop(far, "c", 1)), 4 * 10**9)

    dense = pltpu.VMEM((4 * ROWS, PART), BF)
    part, g_rows = call(
        before_kernel, "before", [((4, ROWS, 3 * HALF), BF), ((4 * ROWS, PART), BF)],
        (rows, rows_other, weights, pick), 2 * 10**9, [dense],
    )
    mid, line = call(middle_kernel, "middle", [((4, ROWS, 3 * HALF), BF), ((ROWS, TOK), BF)],
                     (exchange(part, "x"),), 10**7)
    shard, wide = ((SHARD, HALF), BF), ((4, SLAB, PART + TOK), BF)
    keep, give, far, plus, minus, mine, send = call(
        after_kernel, "after", [wide, wide, shard, shard, shard, shard, ((4, SHARD, HALF), BF)],
        (exchange(mid, "x"), line, g_rows, weights), 14 * 10**8, [pltpu.VMEM((PART, HALF), BF), dense],
    )
    back, = call(combine_kernel, "combine", [((4, EXPERTS, SLAB, TOK), BF)], (keep, hop(give, "zl", 1)), 2 * 10**8)
    back = exchange(back.reshape(32, SLAB, TOK), PEERS).reshape(4, GROUP, TOK)
    token_grad, route_grad = call(finish_kernel, "finish", [((TOK, D), BF), ((1, TOK), F32)],
                                  (ids, share, back), 4 * 10**8)

    got = hop(send, "c", 1)
    far, plus, minus, mine = [add(a, got[i]) for i, a in enumerate((far, plus, minus, mine))]
    down_grad = add(hop(plus, "zh", 1), hop(minus, "zh", -1), hop(far, "zh", 2), mine)
    return token_grad, route_grad.reshape(TOK, 1), down_grad


def solution(mesh):
    inner = Mesh(mesh.devices.reshape(4, 4, 2, 8, 2), AXES)
    rows = P(AXES, None)
    weights = P(("x", "zh", "c"), ("y", "zl"))
    return jax.shard_map(
        per_device,
        mesh=inner,
        in_specs=(rows, rows, rows, rows, weights, weights, weights),
        out_specs=(rows, rows, weights),
        check_vma=False,
    )
```

```python
import jax
import jax.numpy as jnp
from jax import lax
from jax.experimental import pallas as pl
from jax.experimental.pallas import tpu as pltpu
from jax.sharding import Mesh, PartitionSpec as P

BF = jnp.bfloat16
F32 = jnp.float32
I32 = jnp.int32
AXES = ("x", "zh", "c", "y", "zl")
PEERS = ("x", "y")
TOK = 128
D = 3584
EXPERTS = 8
CAP = 6
HALF = 512
SHARD = 112
PART = D // 4
ROWS = 2 * EXPERTS * CAP
SLAB = 48
GROUP = 8 * SLAB
WIDE = 88
WIDER = 8 * WIDE
VMEM_LIMIT = 24 * 1024 * 1024
MOST_VMEM = 56 * 1024 * 1024
ANYWHERE = pl.BlockSpec(memory_space=pl.ANY)
VMEM = pl.BlockSpec(memory_space=pltpu.VMEM)


def iota(shape, dim):
    return lax.broadcasted_iota(I32, shape, dim)


def onehot(hit):
    return jnp.where(hit, 1.0, 0.0).astype(BF)


def sixth(i):
    return (i * 43) >> 8


def regroup():
    a, i = iota((8, SLAB, GROUP), 0), iota((8, SLAB, GROUP), 1)
    b = sixth(i)
    return onehot(iota((8, SLAB, GROUP), 2) == b * SLAB + a * CAP + (i - CAP * b)).reshape(GROUP, GROUP)


def token_ranks(ids):
    member = jnp.where(ids == iota((EXPERTS, TOK), 0), 1.0, 0.0)
    earlier = onehot(iota((TOK, TOK), 0) < iota((TOK, TOK), 1))
    counts = jnp.dot(member.astype(BF), earlier, preferred_element_type=F32)
    return jnp.sum(member * counts, axis=0, keepdims=True).astype(I32)


def to_column(row):
    diagonal = iota((TOK, TOK), 0) == iota((TOK, TOK), 1)
    return jnp.sum(jnp.where(diagonal, row, 0.0), axis=1, keepdims=True)


def call(body, name, out_shape, operands, flops, scratch=(), specs=None, limit=VMEM_LIMIT):
    return pl.pallas_call(
        body,
        in_specs=specs or [VMEM] * len(operands),
        out_specs=[VMEM] * len(out_shape),
        out_shape=[jax.ShapeDtypeStruct(shape, kind) for shape, kind in out_shape],
        scratch_shapes=list(scratch),
        compiler_params=pltpu.CompilerParams(vmem_limit_bytes=limit),
        cost_estimate=pl.CostEstimate(flops=flops, bytes_accessed=4 * 10**6, transcendentals=0),
        name=name,
    )(*operands)


def dispatch_kernel(ids_hbm, p_hbm, x_hbm, g_hbm, out_ref, ids_ref, p_ref, x_ref, g_ref, sems):
    copies = [
        pltpu.make_async_copy(source, target, sems.at[i])
        for i, (source, target) in enumerate(((ids_hbm, ids_ref), (p_hbm, p_ref), (x_hbm, x_ref), (g_hbm, g_ref)))
    ]
    for copy in copies:
        copy.start()
    k, at = iota((EXPERTS, WIDE, 7 * TOK), 1), iota((EXPERTS, WIDE, 7 * TOK), 2)
    q = (k * 43) >> 9
    k = k - 12 * q
    order = q * TOK + iota((EXPERTS, WIDE, 7 * TOK), 0) * 16 + k + jnp.where(k >= CAP, 2, 0)
    order = onehot(at == order).reshape(EXPERTS * WIDE, 7 * TOK)
    for copy in copies:
        copy.wait()
    ids = ids_ref[...]
    slot = jnp.where(ids < EXPERTS, ids * 16 + token_ranks(ids), -16)
    at = iota((TOK, TOK), 0)
    sel = jnp.concatenate([onehot(slot == at), onehot(slot + 8 == at)], axis=1)
    scaled = (to_column(p_ref[...]) * g_ref[...].astype(F32)).astype(BF)
    both = jnp.concatenate([x_ref[...], scaled], axis=0)
    rows = jnp.dot(sel, both, preferred_element_type=F32).astype(BF)
    for i in range(2):
        stack = []
        for q in range(7):
            left = 2 * i * PART + q * TOK
            stack.append(jnp.concatenate([rows[:, left:left + TOK], rows[:, left + PART:left + PART + TOK]], axis=1))
        moved = jnp.dot(order, jnp.concatenate(stack, axis=0), preferred_element_type=F32).astype(BF)
        for j in range(2):
            one = moved[:, j * TOK:(j + 1) * TOK].reshape(EXPERTS, WIDE, TOK)
            out_ref[2 * i + j] = one


def stack_kernel(a_hbm, b_hbm, c_hbm, out_ref, sems):
    copies = [
        pltpu.make_async_copy(source, out_ref.at[:, pl.ds(i * HALF, HALF)], sems.at[i])
        for i, source in enumerate((a_hbm, b_hbm, c_hbm))
    ]
    for copy in copies:
        copy.start()
    for copy in copies:
        copy.wait()


def near_kernel(own_ref, before_ref, after_ref, out_ref, before_out):
    for i, ref in enumerate((own_ref, before_ref, after_ref)):
        out_ref[i * SHARD:(i + 1) * SHARD] = ref[...]
    before_out[...] = before_ref[...]


def assemble_kernel(near_ref, near_other_ref, far_ref, far_other_ref, out_ref, pick_ref):
    shape = (7, 2, SLAB, WIDER)
    j = iota(shape, 2)
    source = sixth(j)
    place = source * WIDE + iota(shape, 0) * 12 + iota(shape, 1) * CAP + (j - CAP * source)
    pick_ref[...] = onehot(iota(shape, 3) == place).reshape(14 * SLAB, WIDER)
    zi, ci = lax.axis_index("zh"), lax.axis_index("c")
    for core, near, far in ((ci, near_ref, far_ref), (1 - ci, near_other_ref, far_other_ref)):
        for i, shift in enumerate((0, 3, 1, 2)):
            block = lax.rem(zi + jnp.where(core == 0, shift, 4 - shift), 4)
            at = pl.multiple_of((2 * block + core) * SHARD, 16)
            out_ref[pl.ds(at, SHARD)] = far[...] if shift == 2 else near[i * SHARD:(i + 1) * SHARD]


def before_kernel(mine_ref, other_ref, weight_ref, pick_ref, part_ref, g_ref, x_scr):
    zl = lax.axis_index("zl")
    for ref, z in ((mine_ref, zl), (other_ref, 1 - zl)):
        for i in range(2):
            both = jnp.concatenate([ref[2 * i], ref[2 * i + 1]], axis=1)
            moved = jnp.dot(pick_ref[...], both, preferred_element_type=F32).astype(BF)
            for k in range(2):
                rows = pl.ds(pl.multiple_of((2 * (2 * i + k) + z) * SLAB, 16), SLAB)
                for q in range(7):
                    columns, lanes = slice(q * TOK, (q + 1) * TOK), slice(k * TOK, (k + 1) * TOK)
                    x_scr[rows, columns] = moved[2 * q * SLAB:(2 * q + 1) * SLAB, lanes]
                    g_ref[rows, columns] = moved[(2 * q + 1) * SLAB:(2 * q + 2) * SLAB, lanes]
    pre = jnp.dot(x_scr[...], weight_ref[:, :2 * HALF], preferred_element_type=F32).astype(BF)
    part_ref[:, :, :2 * HALF] = pre.reshape(4, ROWS, 2 * HALF)
    hid = jnp.dot(g_ref[...], weight_ref[:, 2 * HALF:], preferred_element_type=F32).astype(BF)
    part_ref[:, :, 2 * HALF:] = hid.reshape(4, ROWS, HALF)


def middle_kernel(part_ref, out_ref, line_ref):
    total = part_ref[0].astype(F32) + part_ref[1].astype(F32) + part_ref[2].astype(F32) + part_ref[3].astype(F32)
    gate, up, grad = total[:, :HALF], total[:, HALF:2 * HALF], total[:, 2 * HALF:]
    sig = jax.nn.sigmoid(gate)
    act = gate * sig
    slope = sig * (1.0 + gate * (1.0 - sig))
    hidden = (act * up).astype(BF)
    route = jnp.sum(hidden.astype(F32) * grad, axis=1, keepdims=True)
    d_gate, d_up = (grad * up * slope).astype(BF), (grad * act).astype(BF)
    for i in range(4):
        out_ref[i, :, :HALF] = d_gate
        out_ref[i, :, HALF:2 * HALF] = d_up
        out_ref[i, :, 2 * HALF:] = hidden
    line_ref[...] = jnp.where(iota((ROWS, TOK), 1) == 0, route, 0.0).astype(BF)


def after_kernel(mid_ref, line_ref, g_ref, weight_ref, keep_ref, give_ref,
                 far_ref, plus_ref, minus_ref, own_ref, send_ref, down, grads):
    xi, zi, ci, zl = [lax.axis_index(a) for a in ("x", "zh", "c", "zl")]
    mid = mid_ref[...].reshape(4 * ROWS, 3 * HALF)
    grads[...] = lax.dot_general(
        mid[:, :2 * HALF], weight_ref[:, :2 * HALF], (((1,), (1,)), ((), ())), preferred_element_type=F32
    ).astype(BF)
    for ref, z in ((keep_ref, zl), (give_ref, 1 - zl)):
        own = line_ref[pl.ds(pl.multiple_of(z * SLAB, 16), SLAB)]
        for i in range(4):
            ref[i, :, :PART] = grads[pl.ds(pl.multiple_of((2 * i + z) * SLAB, 16), SLAB)]
            ref[i, :, PART:] = jnp.where(xi == i, own, jnp.zeros_like(own))
    down[...] = lax.dot_general(
        g_ref[...], mid[:, 2 * HALF:], (((0,), (0,)), ((), ())), preferred_element_type=F32
    ).astype(BF)

    def shard(shift, core):
        block = 2 * lax.rem(zi + shift, 4) + core
        return down[pl.ds(pl.multiple_of(block * SHARD, 16), SHARD)]

    for i, (ref, shift) in enumerate(((far_ref, 2), (plus_ref, 1), (minus_ref, 3), (own_ref, 0))):
        ref[...] = shard(shift, ci)
        send_ref[i] = shard(shift, 1 - ci)


def combine_kernel(keep_ref, got_ref, out_ref):
    order = regroup()
    for i in range(2):
        left, right = add(keep_ref[2 * i], got_ref[2 * i]), add(keep_ref[2 * i + 1], got_ref[2 * i + 1])
        stack = []
        for q in range(8):
            columns = slice(q * TOK, (q + 1) * TOK)
            stack.append(jnp.concatenate([left[:, columns], right[:, columns]], axis=1))
        moved = jnp.dot(order, jnp.concatenate(stack, axis=0), preferred_element_type=F32).astype(BF)
        for j in range(2):
            out_ref[2 * i + j] = moved[:, j * TOK:(j + 1) * TOK].reshape(EXPERTS, SLAB, TOK)


def finish_kernel(ids_ref, p_ref, rows_ref, tok_ref, route_ref):
    ids = ids_ref[...]
    base = jnp.where(ids < EXPERTS, ids * SLAB + token_ranks(ids), -GROUP)
    offset = iota((TOK, GROUP), 1) - to_column(base.astype(F32)).astype(I32)
    pairs = [jnp.concatenate([rows_ref[2 * i], rows_ref[2 * i + 1]], axis=1) for i in range(2)]
    route = jnp.zeros((TOK, 1), F32)
    for q in range(8):
        sel = onehot(offset == q * CAP)
        for i in range(2):
            got = jnp.dot(sel, pairs[i], preferred_element_type=F32)
            if q == 7:
                route = route + got[:, :1] + got[:, TOK:TOK + 1]
                continue
            for j in range(2):
                left = (2 * i + j) * PART + q * TOK
                tok_ref[:, left:left + TOK] = got[:, j * TOK:(j + 1) * TOK].astype(BF)
    diagonal = iota((TOK, TOK), 0) == iota((TOK, TOK), 1)
    route_ref[...] = jnp.sum(jnp.where(diagonal, route, 0.0), axis=0, keepdims=True) / p_ref[...]


def hop(a, axis, shift):
    n = lax.axis_size(axis)
    return lax.ppermute(a, axis, [(i, (i + shift) % n) for i in range(n)])


def turn(a, axis, shift):
    n = lax.axis_size(axis)
    pairs = []
    for i in range(n):
        pairs += [(2 * i, 2 * ((i + shift) % n)), (2 * i + 1, 2 * ((i - shift) % n) + 1)]
    return lax.ppermute(a, (axis, "c"), pairs)


def add(*terms):
    return sum(a.astype(F32) for a in terms).astype(BF)


def exchange(a, axes):
    return lax.all_to_all(a, axes, split_axis=0, concat_axis=0, tiled=True)


def per_device(tokens, grad_out, routing, route_weight, gate_weight, up_weight, down_weight):
    ids, share = routing.reshape(1, TOK), route_weight.reshape(1, TOK)
    weights, = call(stack_kernel, "stack", [((SHARD, 3 * HALF), BF)], (gate_weight, up_weight, down_weight), 10**6,
                    [pltpu.SemaphoreType.DMA((3,))], [ANYWHERE] * 3, MOST_VMEM)
    sent, = call(
        dispatch_kernel, "dispatch", [((4, EXPERTS, WIDE, TOK), BF)], (ids, share, tokens, grad_out), 10**9,
        [pltpu.VMEM((1, TOK), I32), pltpu.VMEM((1, TOK), F32), pltpu.VMEM((TOK, D), BF), pltpu.VMEM((TOK, D), BF),
         pltpu.SemaphoreType.DMA((4,))], [ANYWHERE] * 4, MOST_VMEM,
    )
    rows = exchange(sent.reshape(32, WIDE, TOK), PEERS).reshape(4, WIDER, TOK)

    z_before, z_after = turn(weights, "zh", 1), turn(weights, "zh", -1)
    near, passed = call(near_kernel, "near", [((3 * SHARD, 3 * HALF), BF), ((SHARD, 3 * HALF), BF)],
                        (weights, z_before, z_after), 4 * 10**9)
    far = turn(passed, "zh", 1)
    rows_other = hop(rows, "zl", 1)
    weights, pick = call(assemble_kernel, "assemble", [((PART, 3 * HALF), BF), ((14 * SLAB, WIDER), BF)],
                    (near, hop(near, "c", 1), far, hop(far, "c", 1)), 4 * 10**9)

    dense = pltpu.VMEM((4 * ROWS, PART), BF)
    part, g_rows = call(
        before_kernel, "before", [((4, ROWS, 3 * HALF), BF), ((4 * ROWS, PART), BF)],
        (rows, rows_other, weights, pick), 2 * 10**9, [dense],
    )
    mid, line = call(middle_kernel, "middle", [((4, ROWS, 3 * HALF), BF), ((ROWS, TOK), BF)],
                     (exchange(part, "x"),), 10**7)
    shard, wide = ((SHARD, HALF), BF), ((4, SLAB, PART + TOK), BF)
    keep, give, far, plus, minus, mine, send = call(
        after_kernel, "after", [wide, wide, shard, shard, shard, shard, ((4, SHARD, HALF), BF)],
        (exchange(mid, "x"), line, g_rows, weights), 14 * 10**8, [pltpu.VMEM((PART, HALF), BF), dense],
    )
    back, = call(combine_kernel, "combine", [((4, EXPERTS, SLAB, TOK), BF)], (keep, hop(give, "zl", 1)), 2 * 10**8)
    back = exchange(back.reshape(32, SLAB, TOK), PEERS).reshape(4, GROUP, TOK)
    token_grad, route_grad = call(finish_kernel, "finish", [((TOK, D), BF), ((1, TOK), F32)],
                                  (ids, share, back), 4 * 10**8)

    got = hop(send, "c", 1)
    far, plus, minus, mine = [add(a, got[i]) for i, a in enumerate((far, plus, minus, mine))]
    down_grad = add(hop(plus, "zh", 1), hop(minus, "zh", -1), hop(far, "zh", 2), mine)
    return token_grad, route_grad.reshape(TOK, 1), down_grad


def solution(mesh):
    inner = Mesh(mesh.devices.reshape(4, 4, 2, 8, 2), AXES)
    rows = P(AXES, None)
    weights = P(("x", "zh", "c"), ("y", "zl"))
    return jax.shard_map(
        per_device,
        mesh=inner,
        in_specs=(rows, rows, rows, rows, weights, weights, weights),
        out_specs=(rows, rows, weights),
        check_vma=False,
    )
```

```python
import jax
import jax.numpy as jnp
from jax import lax
from jax.experimental import pallas as pl
from jax.experimental.pallas import tpu as pltpu
from jax.sharding import Mesh, PartitionSpec as P

BF = jnp.bfloat16
F32 = jnp.float32
I32 = jnp.int32
AXES = ("x", "zh", "c", "y", "zl")
PEERS = ("x", "y")
TOK = 128
D = 3584
EXPERTS = 8
CAP = 6
HALF = 512
SHARD = 112
PART = D // 4
ROWS = 2 * EXPERTS * CAP
SLAB = 48
GROUP = 8 * SLAB
WIDE = 88
WIDER = 8 * WIDE
VMEM_LIMIT = 24 * 1024 * 1024
MOST_VMEM = 56 * 1024 * 1024
ANYWHERE = pl.BlockSpec(memory_space=pl.ANY)
VMEM = pl.BlockSpec(memory_space=pltpu.VMEM)


def iota(shape, dim):
    return lax.broadcasted_iota(I32, shape, dim)


def onehot(hit):
    return jnp.where(hit, 1.0, 0.0).astype(BF)


def sixth(i):
    return (i * 43) >> 8


def regroup():
    a, i = iota((8, SLAB, GROUP), 0), iota((8, SLAB, GROUP), 1)
    b = sixth(i)
    return onehot(iota((8, SLAB, GROUP), 2) == b * SLAB + a * CAP + (i - CAP * b)).reshape(GROUP, GROUP)


def token_ranks(ids):
    member = jnp.where(ids == iota((EXPERTS, TOK), 0), 1.0, 0.0)
    earlier = onehot(iota((TOK, TOK), 0) < iota((TOK, TOK), 1))
    counts = jnp.dot(member.astype(BF), earlier, preferred_element_type=F32)
    return jnp.sum(member * counts, axis=0, keepdims=True).astype(I32)


def to_column(row):
    diagonal = iota((TOK, TOK), 0) == iota((TOK, TOK), 1)
    return jnp.sum(jnp.where(diagonal, row, 0.0), axis=1, keepdims=True)


def call(body, name, out_shape, operands, flops, scratch=(), specs=None, limit=VMEM_LIMIT):
    return pl.pallas_call(
        body,
        in_specs=specs or [VMEM] * len(operands),
        out_specs=[VMEM] * len(out_shape),
        out_shape=[jax.ShapeDtypeStruct(shape, kind) for shape, kind in out_shape],
        scratch_shapes=list(scratch),
        compiler_params=pltpu.CompilerParams(vmem_limit_bytes=limit),
        cost_estimate=pl.CostEstimate(flops=flops, bytes_accessed=4 * 10**6, transcendentals=0),
        name=name,
    )(*operands)


def dispatch_kernel(ids_hbm, p_hbm, x_hbm, g_hbm, out_ref, ids_ref, p_ref, x_ref, g_ref, sems):
    copies = [
        pltpu.make_async_copy(source, target, sems.at[i])
        for i, (source, target) in enumerate(((ids_hbm, ids_ref), (p_hbm, p_ref), (x_hbm, x_ref), (g_hbm, g_ref)))
    ]
    for copy in copies:
        copy.start()
    shape = (EXPERTS, WIDE, 14 * SLAB)
    k = iota(shape, 1)
    q = (k * 43) >> 9
    k = k - 12 * q
    order = q * (2 * SLAB) + iota(shape, 0) * CAP + k + jnp.where(k >= CAP, SLAB - CAP, 0)
    order = onehot(iota(shape, 2) == order).reshape(EXPERTS * WIDE, 14 * SLAB)
    for copy in copies:
        copy.wait()
    ids = ids_ref[...]
    slot = jnp.where(ids < EXPERTS, ids * CAP + token_ranks(ids), -1)
    sel = onehot(slot == iota((SLAB, TOK), 0))
    scaled = (to_column(p_ref[...]) * g_ref[...].astype(F32)).astype(BF)
    rows = jnp.concatenate([
        jnp.dot(sel, x_ref[...], preferred_element_type=F32).astype(BF),
        jnp.dot(sel, scaled, preferred_element_type=F32).astype(BF),
    ], axis=0)
    for i in range(2):
        stack = []
        for q in range(7):
            left = 2 * i * PART + q * TOK
            stack.append(jnp.concatenate([rows[:, left:left + TOK], rows[:, left + PART:left + PART + TOK]], axis=1))
        moved = jnp.dot(order, jnp.concatenate(stack, axis=0), preferred_element_type=F32).astype(BF)
        for j in range(2):
            one = moved[:, j * TOK:(j + 1) * TOK].reshape(EXPERTS, WIDE, TOK)
            out_ref[2 * i + j] = one


def stack_kernel(a_hbm, b_hbm, c_hbm, out_ref, sems):
    copies = [
        pltpu.make_async_copy(source, out_ref.at[:, pl.ds(i * HALF, HALF)], sems.at[i])
        for i, source in enumerate((a_hbm, b_hbm, c_hbm))
    ]
    for copy in copies:
        copy.start()
    for copy in copies:
        copy.wait()


def near_kernel(own_ref, before_ref, after_ref, out_ref, before_out):
    for i, ref in enumerate((own_ref, before_ref, after_ref)):
        out_ref[i * SHARD:(i + 1) * SHARD] = ref[...]
    before_out[...] = before_ref[...]


def assemble_kernel(near_ref, near_other_ref, far_ref, far_other_ref, out_ref, pick_ref):
    shape = (7, 2, SLAB, WIDER)
    j = iota(shape, 2)
    source = sixth(j)
    place = source * WIDE + iota(shape, 0) * 12 + iota(shape, 1) * CAP + (j - CAP * source)
    pick_ref[...] = onehot(iota(shape, 3) == place).reshape(14 * SLAB, WIDER)
    zi, ci = lax.axis_index("zh"), lax.axis_index("c")
    for core, near, far in ((ci, near_ref, far_ref), (1 - ci, near_other_ref, far_other_ref)):
        for i, shift in enumerate((0, 3, 1, 2)):
            block = lax.rem(zi + jnp.where(core == 0, shift, 4 - shift), 4)
            at = pl.multiple_of((2 * block + core) * SHARD, 16)
            out_ref[pl.ds(at, SHARD)] = far[...] if shift == 2 else near[i * SHARD:(i + 1) * SHARD]


def before_kernel(mine_ref, other_ref, weight_ref, pick_ref, part_ref, g_ref, x_scr):
    zl = lax.axis_index("zl")
    for ref, z in ((mine_ref, zl), (other_ref, 1 - zl)):
        for i in range(2):
            both = jnp.concatenate([ref[2 * i], ref[2 * i + 1]], axis=1)
            moved = jnp.dot(pick_ref[...], both, preferred_element_type=F32).astype(BF)
            for k in range(2):
                rows = pl.ds(pl.multiple_of((2 * (2 * i + k) + z) * SLAB, 16), SLAB)
                for q in range(7):
                    columns, lanes = slice(q * TOK, (q + 1) * TOK), slice(k * TOK, (k + 1) * TOK)
                    x_scr[rows, columns] = moved[2 * q * SLAB:(2 * q + 1) * SLAB, lanes]
                    g_ref[rows, columns] = moved[(2 * q + 1) * SLAB:(2 * q + 2) * SLAB, lanes]
    pre = jnp.dot(x_scr[...], weight_ref[:, :2 * HALF], preferred_element_type=F32).astype(BF)
    part_ref[:, :, :2 * HALF] = pre.reshape(4, ROWS, 2 * HALF)
    hid = jnp.dot(g_ref[...], weight_ref[:, 2 * HALF:], preferred_element_type=F32).astype(BF)
    part_ref[:, :, 2 * HALF:] = hid.reshape(4, ROWS, HALF)


def middle_kernel(part_ref, out_ref, line_ref):
    total = part_ref[0].astype(F32) + part_ref[1].astype(F32) + part_ref[2].astype(F32) + part_ref[3].astype(F32)
    gate, up, grad = total[:, :HALF], total[:, HALF:2 * HALF], total[:, 2 * HALF:]
    sig = jax.nn.sigmoid(gate)
    act = gate * sig
    slope = sig * (1.0 + gate * (1.0 - sig))
    hidden = (act * up).astype(BF)
    route = jnp.sum(hidden.astype(F32) * grad, axis=1, keepdims=True)
    d_gate, d_up = (grad * up * slope).astype(BF), (grad * act).astype(BF)
    for i in range(4):
        out_ref[i, :, :HALF] = d_gate
        out_ref[i, :, HALF:2 * HALF] = d_up
        out_ref[i, :, 2 * HALF:] = hidden
    line_ref[...] = jnp.where(iota((ROWS, TOK), 1) == 0, route, 0.0).astype(BF)


def after_kernel(mid_ref, line_ref, g_ref, weight_ref, keep_ref, give_ref,
                 far_ref, plus_ref, minus_ref, own_ref, send_ref, down, grads):
    xi, zi, ci, zl = [lax.axis_index(a) for a in ("x", "zh", "c", "zl")]
    mid = mid_ref[...].reshape(4 * ROWS, 3 * HALF)
    grads[...] = lax.dot_general(
        mid[:, :2 * HALF], weight_ref[:, :2 * HALF], (((1,), (1,)), ((), ())), preferred_element_type=F32
    ).astype(BF)
    for ref, z in ((keep_ref, zl), (give_ref, 1 - zl)):
        own = line_ref[pl.ds(pl.multiple_of(z * SLAB, 16), SLAB)]
        for i in range(4):
            ref[i, :, :PART] = grads[pl.ds(pl.multiple_of((2 * i + z) * SLAB, 16), SLAB)]
            ref[i, :, PART:] = jnp.where(xi == i, own, jnp.zeros_like(own))
    down[...] = lax.dot_general(
        g_ref[...], mid[:, 2 * HALF:], (((0,), (0,)), ((), ())), preferred_element_type=F32
    ).astype(BF)

    def shard(shift, core):
        block = 2 * lax.rem(zi + shift, 4) + core
        return down[pl.ds(pl.multiple_of(block * SHARD, 16), SHARD)]

    for i, (ref, shift) in enumerate(((far_ref, 2), (plus_ref, 1), (minus_ref, 3), (own_ref, 0))):
        ref[...] = shard(shift, ci)
        send_ref[i] = shard(shift, 1 - ci)


def combine_kernel(keep_ref, got_ref, out_ref):
    order = regroup()
    for i in range(2):
        left, right = add(keep_ref[2 * i], got_ref[2 * i]), add(keep_ref[2 * i + 1], got_ref[2 * i + 1])
        stack = []
        for q in range(8):
            columns = slice(q * TOK, (q + 1) * TOK)
            stack.append(jnp.concatenate([left[:, columns], right[:, columns]], axis=1))
        moved = jnp.dot(order, jnp.concatenate(stack, axis=0), preferred_element_type=F32).astype(BF)
        for j in range(2):
            out_ref[2 * i + j] = moved[:, j * TOK:(j + 1) * TOK].reshape(EXPERTS, SLAB, TOK)


def finish_kernel(ids_ref, p_ref, rows_ref, tok_ref, route_ref):
    ids = ids_ref[...]
    base = jnp.where(ids < EXPERTS, ids * SLAB + token_ranks(ids), -GROUP)
    offset = iota((TOK, GROUP), 1) - to_column(base.astype(F32)).astype(I32)
    pairs = [jnp.concatenate([rows_ref[2 * i], rows_ref[2 * i + 1]], axis=1) for i in range(2)]
    route = jnp.zeros((TOK, 1), F32)
    for q in range(8):
        sel = onehot(offset == q * CAP)
        for i in range(2):
            got = jnp.dot(sel, pairs[i], preferred_element_type=F32)
            if q == 7:
                route = route + got[:, :1] + got[:, TOK:TOK + 1]
                continue
            for j in range(2):
                left = (2 * i + j) * PART + q * TOK
                tok_ref[:, left:left + TOK] = got[:, j * TOK:(j + 1) * TOK].astype(BF)
    diagonal = iota((TOK, TOK), 0) == iota((TOK, TOK), 1)
    route_ref[...] = jnp.sum(jnp.where(diagonal, route, 0.0), axis=0, keepdims=True) / p_ref[...]


def hop(a, axis, shift):
    n = lax.axis_size(axis)
    return lax.ppermute(a, axis, [(i, (i + shift) % n) for i in range(n)])


def turn(a, axis, shift):
    n = lax.axis_size(axis)
    pairs = []
    for i in range(n):
        pairs += [(2 * i, 2 * ((i + shift) % n)), (2 * i + 1, 2 * ((i - shift) % n) + 1)]
    return lax.ppermute(a, (axis, "c"), pairs)


def add(*terms):
    return sum(a.astype(F32) for a in terms).astype(BF)


def exchange(a, axes):
    return lax.all_to_all(a, axes, split_axis=0, concat_axis=0, tiled=True)


def per_device(tokens, grad_out, routing, route_weight, gate_weight, up_weight, down_weight):
    ids, share = routing.reshape(1, TOK), route_weight.reshape(1, TOK)
    weights, = call(stack_kernel, "stack", [((SHARD, 3 * HALF), BF)], (gate_weight, up_weight, down_weight), 10**6,
                    [pltpu.SemaphoreType.DMA((3,))], [ANYWHERE] * 3, MOST_VMEM)
    sent, = call(
        dispatch_kernel, "dispatch", [((4, EXPERTS, WIDE, TOK), BF)], (ids, share, tokens, grad_out), 10**9,
        [pltpu.VMEM((1, TOK), I32), pltpu.VMEM((1, TOK), F32), pltpu.VMEM((TOK, D), BF), pltpu.VMEM((TOK, D), BF),
         pltpu.SemaphoreType.DMA((4,))], [ANYWHERE] * 4, MOST_VMEM,
    )
    rows = exchange(sent.reshape(32, WIDE, TOK), PEERS).reshape(4, WIDER, TOK)

    z_before, z_after = turn(weights, "zh", 1), turn(weights, "zh", -1)
    near, passed = call(near_kernel, "near", [((3 * SHARD, 3 * HALF), BF), ((SHARD, 3 * HALF), BF)],
                        (weights, z_before, z_after), 4 * 10**9)
    far = turn(passed, "zh", 1)
    rows_other = hop(rows, "zl", 1)
    weights, pick = call(assemble_kernel, "assemble", [((PART, 3 * HALF), BF), ((14 * SLAB, WIDER), BF)],
                    (near, hop(near, "c", 1), far, hop(far, "c", 1)), 4 * 10**9)

    dense = pltpu.VMEM((4 * ROWS, PART), BF)
    part, g_rows = call(
        before_kernel, "before", [((4, ROWS, 3 * HALF), BF), ((4 * ROWS, PART), BF)],
        (rows, rows_other, weights, pick), 2 * 10**9, [dense],
    )
    mid, line = call(middle_kernel, "middle", [((4, ROWS, 3 * HALF), BF), ((ROWS, TOK), BF)],
                     (exchange(part, "x"),), 10**7)
    shard, wide = ((SHARD, HALF), BF), ((4, SLAB, PART + TOK), BF)
    keep, give, far, plus, minus, mine, send = call(
        after_kernel, "after", [wide, wide, shard, shard, shard, shard, ((4, SHARD, HALF), BF)],
        (exchange(mid, "x"), line, g_rows, weights), 14 * 10**8, [pltpu.VMEM((PART, HALF), BF), dense],
    )
    back, = call(combine_kernel, "combine", [((4, EXPERTS, SLAB, TOK), BF)], (keep, hop(give, "zl", 1)), 2 * 10**8)
    back = exchange(back.reshape(32, SLAB, TOK), PEERS).reshape(4, GROUP, TOK)
    token_grad, route_grad = call(finish_kernel, "finish", [((TOK, D), BF), ((1, TOK), F32)],
                                  (ids, share, back), 4 * 10**8)

    got = hop(send, "c", 1)
    far, plus, minus, mine = [add(a, got[i]) for i, a in enumerate((far, plus, minus, mine))]
    down_grad = add(hop(plus, "zh", 1), hop(minus, "zh", -1), hop(far, "zh", 2), mine)
    return token_grad, route_grad.reshape(TOK, 1), down_grad


def solution(mesh):
    inner = Mesh(mesh.devices.reshape(4, 4, 2, 8, 2), AXES)
    rows = P(AXES, None)
    weights = P(("x", "zh", "c"), ("y", "zl"))
    return jax.shard_map(
        per_device,
        mesh=inner,
        in_specs=(rows, rows, rows, rows, weights, weights, weights),
        out_specs=(rows, rows, weights),
        check_vma=False,
    )
```

```python
import jax
import jax.numpy as jnp
from jax import lax
from jax.experimental import pallas as pl
from jax.experimental.pallas import tpu as pltpu
from jax.sharding import Mesh, PartitionSpec as P

BF = jnp.bfloat16
F32 = jnp.float32
I32 = jnp.int32
AXES = ("x", "zh", "c", "y", "zl")
PEERS = ("x", "y")
TOK = 128
D = 3584
EXPERTS = 8
CAP = 6
HALF = 512
SHARD = 112
PART = D // 4
ROWS = 2 * EXPERTS * CAP
SLAB = 48
GROUP = 8 * SLAB
WIDE = 88
WIDER = 8 * WIDE
VMEM_LIMIT = 24 * 1024 * 1024
MOST_VMEM = 56 * 1024 * 1024
ANYWHERE = pl.BlockSpec(memory_space=pl.ANY)
VMEM = pl.BlockSpec(memory_space=pltpu.VMEM)


def iota(shape, dim):
    return lax.broadcasted_iota(I32, shape, dim)


def onehot(hit):
    return jnp.where(hit, 1.0, 0.0).astype(BF)


def sixth(i):
    return (i * 43) >> 8


def regroup():
    a, i = iota((8, SLAB, GROUP), 0), iota((8, SLAB, GROUP), 1)
    b = sixth(i)
    return onehot(iota((8, SLAB, GROUP), 2) == b * SLAB + a * CAP + (i - CAP * b)).reshape(GROUP, GROUP)


def token_ranks(ids):
    member = jnp.where(ids == iota((EXPERTS, TOK), 0), 1.0, 0.0)
    earlier = onehot(iota((TOK, TOK), 0) < iota((TOK, TOK), 1))
    counts = jnp.dot(member.astype(BF), earlier, preferred_element_type=F32)
    return jnp.sum(member * counts, axis=0, keepdims=True).astype(I32)


def to_column(row):
    diagonal = iota((TOK, TOK), 0) == iota((TOK, TOK), 1)
    return jnp.sum(jnp.where(diagonal, row, 0.0), axis=1, keepdims=True)


def call(body, name, out_shape, operands, flops, scratch=(), specs=None, limit=VMEM_LIMIT):
    return pl.pallas_call(
        body,
        in_specs=specs or [VMEM] * len(operands),
        out_specs=[VMEM] * len(out_shape),
        out_shape=[jax.ShapeDtypeStruct(shape, kind) for shape, kind in out_shape],
        scratch_shapes=list(scratch),
        compiler_params=pltpu.CompilerParams(vmem_limit_bytes=limit),
        cost_estimate=pl.CostEstimate(flops=flops, bytes_accessed=4 * 10**6, transcendentals=0),
        name=name,
    )(*operands)


def dispatch_kernel(ids_hbm, p_hbm, x_hbm, g_hbm, out_ref, ids_ref, p_ref, x_ref, g_ref, sems):
    copies = [
        pltpu.make_async_copy(source, target, sems.at[i])
        for i, (source, target) in enumerate(((ids_hbm, ids_ref), (p_hbm, p_ref), (x_hbm, x_ref), (g_hbm, g_ref)))
    ]
    for copy in copies:
        copy.start()
    shape = (EXPERTS, WIDE, 14 * SLAB)
    k = iota(shape, 1)
    q = (k * 43) >> 9
    k = k - 12 * q
    order = q * (2 * SLAB) + iota(shape, 0) * CAP + k + jnp.where(k >= CAP, SLAB - CAP, 0)
    order = onehot(iota(shape, 2) == order).reshape(EXPERTS * WIDE, 14 * SLAB)
    for copy in copies:
        copy.wait()
    ids = ids_ref[...]
    slot = jnp.where(ids < EXPERTS, ids * CAP + token_ranks(ids), -1)
    sel = onehot(slot == iota((SLAB, TOK), 0))
    scaled = (to_column(p_ref[...]) * g_ref[...].astype(F32)).astype(BF)
    rows = jnp.concatenate([
        jnp.dot(sel, x_ref[...], preferred_element_type=F32).astype(BF),
        jnp.dot(sel, scaled, preferred_element_type=F32).astype(BF),
    ], axis=0)
    for i in range(2):
        stack = []
        for q in range(7):
            left = 2 * i * PART + q * TOK
            stack.append(jnp.concatenate([rows[:, left:left + TOK], rows[:, left + PART:left + PART + TOK]], axis=1))
        moved = jnp.dot(order, jnp.concatenate(stack, axis=0), preferred_element_type=F32).astype(BF)
        for j in range(2):
            one = moved[:, j * TOK:(j + 1) * TOK].reshape(EXPERTS, WIDE, TOK)
            out_ref[2 * i + j] = one


def stack_kernel(a_hbm, b_hbm, c_hbm, out_ref, sems):
    copies = [
        pltpu.make_async_copy(source, out_ref.at[:, pl.ds(i * HALF, HALF)], sems.at[i])
        for i, source in enumerate((a_hbm, b_hbm, c_hbm))
    ]
    for copy in copies:
        copy.start()
    for copy in copies:
        copy.wait()


def near_kernel(own_ref, before_ref, after_ref, out_ref, after_out):
    for i, ref in enumerate((own_ref, before_ref, after_ref)):
        out_ref[i * SHARD:(i + 1) * SHARD] = ref[...]
    after_out[...] = after_ref[...]


def assemble_kernel(near_ref, near_other_ref, far_ref, far_other_ref, out_ref, pick_ref):
    shape = (7, 2, SLAB, WIDER)
    j = iota(shape, 2)
    source = sixth(j)
    place = source * WIDE + iota(shape, 0) * 12 + iota(shape, 1) * CAP + (j - CAP * source)
    pick_ref[...] = onehot(iota(shape, 3) == place).reshape(14 * SLAB, WIDER)
    zi, ci = lax.axis_index("zh"), lax.axis_index("c")
    for core, near, far in ((ci, near_ref, far_ref), (1 - ci, near_other_ref, far_other_ref)):
        for i, shift in enumerate((0, 3, 2, 1)):
            block = lax.rem(zi + jnp.where(core == 0, shift, 4 - shift), 4)
            at = pl.multiple_of((2 * block + core) * SHARD, 16)
            out_ref[pl.ds(at, SHARD)] = far[...] if i == 3 else near[i * SHARD:(i + 1) * SHARD]


def before_kernel(mine_ref, other_ref, weight_ref, pick_ref, part_ref, g_ref, x_scr):
    zl = lax.axis_index("zl")
    for ref, z in ((mine_ref, zl), (other_ref, 1 - zl)):
        for i in range(2):
            both = jnp.concatenate([ref[2 * i], ref[2 * i + 1]], axis=1)
            moved = jnp.dot(pick_ref[...], both, preferred_element_type=F32).astype(BF)
            for k in range(2):
                rows = pl.ds(pl.multiple_of((2 * (2 * i + k) + z) * SLAB, 16), SLAB)
                for q in range(7):
                    columns, lanes = slice(q * TOK, (q + 1) * TOK), slice(k * TOK, (k + 1) * TOK)
                    x_scr[rows, columns] = moved[2 * q * SLAB:(2 * q + 1) * SLAB, lanes]
                    g_ref[rows, columns] = moved[(2 * q + 1) * SLAB:(2 * q + 2) * SLAB, lanes]
    pre = jnp.dot(x_scr[...], weight_ref[:, :2 * HALF], preferred_element_type=F32).astype(BF)
    part_ref[:, :, :2 * HALF] = pre.reshape(4, ROWS, 2 * HALF)
    hid = jnp.dot(g_ref[...], weight_ref[:, 2 * HALF:], preferred_element_type=F32).astype(BF)
    part_ref[:, :, 2 * HALF:] = hid.reshape(4, ROWS, HALF)


def middle_kernel(part_ref, out_ref, line_ref):
    total = part_ref[0].astype(F32) + part_ref[1].astype(F32) + part_ref[2].astype(F32) + part_ref[3].astype(F32)
    gate, up, grad = total[:, :HALF], total[:, HALF:2 * HALF], total[:, 2 * HALF:]
    sig = jax.nn.sigmoid(gate)
    act = gate * sig
    slope = sig * (1.0 + gate * (1.0 - sig))
    hidden = (act * up).astype(BF)
    route = jnp.sum(hidden.astype(F32) * grad, axis=1, keepdims=True)
    d_gate, d_up = (grad * up * slope).astype(BF), (grad * act).astype(BF)
    for i in range(4):
        out_ref[i, :, :HALF] = d_gate
        out_ref[i, :, HALF:2 * HALF] = d_up
        out_ref[i, :, 2 * HALF:] = hidden
    line_ref[...] = jnp.where(iota((ROWS, TOK), 1) == 0, route, 0.0).astype(BF)


def after_kernel(mid_ref, line_ref, g_ref, weight_ref, keep_ref, give_ref,
                 far_ref, plus_ref, minus_ref, own_ref, send_ref, down, grads):
    xi, zi, ci, zl = [lax.axis_index(a) for a in ("x", "zh", "c", "zl")]
    mid = mid_ref[...].reshape(4 * ROWS, 3 * HALF)
    grads[...] = lax.dot_general(
        mid[:, :2 * HALF], weight_ref[:, :2 * HALF], (((1,), (1,)), ((), ())), preferred_element_type=F32
    ).astype(BF)
    for ref, z in ((keep_ref, zl), (give_ref, 1 - zl)):
        own = line_ref[pl.ds(pl.multiple_of(z * SLAB, 16), SLAB)]
        for i in range(4):
            ref[i, :, :PART] = grads[pl.ds(pl.multiple_of((2 * i + z) * SLAB, 16), SLAB)]
            ref[i, :, PART:] = jnp.where(xi == i, own, jnp.zeros_like(own))
    down[...] = lax.dot_general(
        g_ref[...], mid[:, 2 * HALF:], (((0,), (0,)), ((), ())), preferred_element_type=F32
    ).astype(BF)

    def shard(shift, core):
        block = 2 * lax.rem(zi + shift, 4) + core
        return down[pl.ds(pl.multiple_of(block * SHARD, 16), SHARD)]

    for i, (ref, shift) in enumerate(((far_ref, 2), (plus_ref, 1), (minus_ref, 3), (own_ref, 0))):
        ref[...] = shard(shift, ci)
        send_ref[i] = shard(shift, 1 - ci)


def combine_kernel(keep_ref, got_ref, out_ref):
    order = regroup()
    for i in range(2):
        left, right = add(keep_ref[2 * i], got_ref[2 * i]), add(keep_ref[2 * i + 1], got_ref[2 * i + 1])
        stack = []
        for q in range(8):
            columns = slice(q * TOK, (q + 1) * TOK)
            stack.append(jnp.concatenate([left[:, columns], right[:, columns]], axis=1))
        moved = jnp.dot(order, jnp.concatenate(stack, axis=0), preferred_element_type=F32).astype(BF)
        for j in range(2):
            out_ref[2 * i + j] = moved[:, j * TOK:(j + 1) * TOK].reshape(EXPERTS, SLAB, TOK)


def finish_kernel(ids_ref, p_ref, rows_ref, tok_ref, route_ref):
    ids = ids_ref[...]
    base = jnp.where(ids < EXPERTS, ids * SLAB + token_ranks(ids), -GROUP)
    offset = iota((TOK, GROUP), 1) - to_column(base.astype(F32)).astype(I32)
    pairs = [jnp.concatenate([rows_ref[2 * i], rows_ref[2 * i + 1]], axis=1) for i in range(2)]
    route = jnp.zeros((TOK, 1), F32)
    for q in range(8):
        sel = onehot(offset == q * CAP)
        for i in range(2):
            got = jnp.dot(sel, pairs[i], preferred_element_type=F32)
            if q == 7:
                route = route + got[:, :1] + got[:, TOK:TOK + 1]
                continue
            for j in range(2):
                left = (2 * i + j) * PART + q * TOK
                tok_ref[:, left:left + TOK] = got[:, j * TOK:(j + 1) * TOK].astype(BF)
    diagonal = iota((TOK, TOK), 0) == iota((TOK, TOK), 1)
    route_ref[...] = jnp.sum(jnp.where(diagonal, route, 0.0), axis=0, keepdims=True) / p_ref[...]


def hop(a, axis, shift):
    n = lax.axis_size(axis)
    return lax.ppermute(a, axis, [(i, (i + shift) % n) for i in range(n)])


def turn(a, axis, shift):
    n = lax.axis_size(axis)
    pairs = []
    for i in range(n):
        pairs += [(2 * i, 2 * ((i + shift) % n)), (2 * i + 1, 2 * ((i - shift) % n) + 1)]
    return lax.ppermute(a, (axis, "c"), pairs)


def add(*terms):
    return sum(a.astype(F32) for a in terms).astype(BF)


def exchange(a, axes):
    return lax.all_to_all(a, axes, split_axis=0, concat_axis=0, tiled=True)


def per_device(tokens, grad_out, routing, route_weight, gate_weight, up_weight, down_weight):
    ids, share = routing.reshape(1, TOK), route_weight.reshape(1, TOK)
    weights, = call(stack_kernel, "stack", [((SHARD, 3 * HALF), BF)], (gate_weight, up_weight, down_weight), 10**6,
                    [pltpu.SemaphoreType.DMA((3,))], [ANYWHERE] * 3, MOST_VMEM)
    sent, = call(
        dispatch_kernel, "dispatch", [((4, EXPERTS, WIDE, TOK), BF)], (ids, share, tokens, grad_out), 10**9,
        [pltpu.VMEM((1, TOK), I32), pltpu.VMEM((1, TOK), F32), pltpu.VMEM((TOK, D), BF), pltpu.VMEM((TOK, D), BF),
         pltpu.SemaphoreType.DMA((4,))], [ANYWHERE] * 4, MOST_VMEM,
    )
    rows = exchange(sent.reshape(32, WIDE, TOK), PEERS).reshape(4, WIDER, TOK)

    first = turn(weights, "zh", 1)
    second = turn(first, "zh", 1)
    near, passed = call(near_kernel, "near", [((3 * SHARD, 3 * HALF), BF), ((SHARD, 3 * HALF), BF)],
                        (weights, first, second), 4 * 10**9)
    far = turn(passed, "zh", 1)
    rows_other = hop(rows, "zl", 1)
    weights, pick = call(assemble_kernel, "assemble", [((PART, 3 * HALF), BF), ((14 * SLAB, WIDER), BF)],
                    (near, hop(near, "c", 1), far, hop(far, "c", 1)), 2 * 10**9)

    dense = pltpu.VMEM((4 * ROWS, PART), BF)
    part, g_rows = call(
        before_kernel, "before", [((4, ROWS, 3 * HALF), BF), ((4 * ROWS, PART), BF)],
        (rows, rows_other, weights, pick), 2 * 10**9, [dense],
    )
    mid, line = call(middle_kernel, "middle", [((4, ROWS, 3 * HALF), BF), ((ROWS, TOK), BF)],
                     (exchange(part, "x"),), 10**7)
    shard, wide = ((SHARD, HALF), BF), ((4, SLAB, PART + TOK), BF)
    keep, give, far, plus, minus, mine, send = call(
        after_kernel, "after", [wide, wide, shard, shard, shard, shard, ((4, SHARD, HALF), BF)],
        (exchange(mid, "x"), line, g_rows, weights), 14 * 10**8, [pltpu.VMEM((PART, HALF), BF), dense],
    )
    back, = call(combine_kernel, "combine", [((4, EXPERTS, SLAB, TOK), BF)], (keep, hop(give, "zl", 1)), 2 * 10**8)
    back = exchange(back.reshape(32, SLAB, TOK), PEERS).reshape(4, GROUP, TOK)
    token_grad, route_grad = call(finish_kernel, "finish", [((TOK, D), BF), ((1, TOK), F32)],
                                  (ids, share, back), 4 * 10**8)

    got = hop(send, "c", 1)
    far, plus, minus, mine = [add(a, got[i]) for i, a in enumerate((far, plus, minus, mine))]
    down_grad = add(hop(plus, "zh", 1), hop(minus, "zh", -1), hop(far, "zh", 2), mine)
    return token_grad, route_grad.reshape(TOK, 1), down_grad


def solution(mesh):
    inner = Mesh(mesh.devices.reshape(4, 4, 2, 8, 2), AXES)
    rows = P(AXES, None)
    weights = P(("x", "zh", "c"), ("y", "zl"))
    return jax.shard_map(
        per_device,
        mesh=inner,
        in_specs=(rows, rows, rows, rows, weights, weights, weights),
        out_specs=(rows, rows, weights),
        check_vma=False,
    )
```
